128 devices in a mesh: store: 4 (over z), trainer: 32 (over x, y, core).
Axes of the slice: x: 4, y: 4, z: 4, core: 2. Of those that a mesh axis runs over, the one named last changes fastest.
Arguments:
- features: bfloat16 [262144, 1024], P(('store', 'trainer')), may hold values from -6 to 6
- sent_ids: int32 [128, 32, 12], P(('store', 'trainer')), may hold values from 0 to 2047
- block_sizes: int32 [128, 32], P(('store', 'trainer')), may hold values from 1 to 12, as said below
- self_ids: int32 [24576], P('trainer'), may hold values from 0 to 1535, as said below
- near_one: int32 [24576, 10], P('trainer'), may hold values from 0 to 1535
- degree_one: int32 [24576], P('trainer'), may hold values from 1 to 10
- near_two: int32 [12288, 10], P('trainer'), may hold values from 0 to 767
- degree_two: int32 [12288], P('trainer'), may hold values from 1 to 10
- near_three: int32 [6144, 10], P('trainer'), may hold values from 0 to 383
- degree_three: int32 [6144], P('trainer'), may hold values from 1 to 10
- weight_one: bfloat16 [2048, 1024], P(None, 'store'), may hold values from -0.125 to 0.125
- weight_two: bfloat16 [2048, 1024], P(None, 'store'), may hold values from -0.125 to 0.125
- weight_three: bfloat16 [2048, 1024], P(None, 'store'), may hold values from -0.125 to 0.125
- cotangent: bfloat16 [6144, 1024], P('trainer', 'store'), may hold values from -6 to 6
Outputs:
- embedding: bfloat16 [6144, 1024], P('trainer', 'store')
- grad_one: float32 [2048, 1024], P('trainer', 'store')
- grad_two: float32 [2048, 1024], P('trainer', 'store')
- grad_three: float32 [2048, 1024], P('trainer', 'store')
The draws below stay inside these ranges and needn't reach their ends.
Inputs may be any that keep to these rules, and one draw needn't show every extreme that they name: `block_sizes`: every owner sends 1 to 12 filled slots to every trainer group, and in every draw some trainer group receives exactly 12 filled slots from every owner. `self_ids`: each first-layer node names a filled slot: owner o = id // 12 and slot id % 12 < block_sizes[o, g] for its group g.
All inputs are finite; a program needn't handle non-finite values.
Results may differ from the reference program's by a relative error of at most 0.02.
Values may be sent and summed in bfloat16 or wider, within the bound.
A program may use at most 64 MiB of HBM per device.

```python
import jax
import jax.numpy as jnp
from jax import lax

F = 1024
H = 1024
FAN = 10
SEEDS = 192
ROWS_DEV = 2048
IN_ROWS = 1536
OUTER_ROWS = 768
MID_ROWS = 384
OWNERS = 128
GROUPS = 32
CAP = 12
TABLE_ROWS = 262144


def shared_counts(key):
    inner = jax.random.fold_in(key, 11)
    first, second = jax.random.split(inner)
    counts = jax.random.randint(first, (OWNERS, GROUPS), 1, CAP + 1)
    busiest = jax.random.randint(second, (), 0, GROUPS)
    counts = jnp.where(jnp.arange(GROUPS)[None, :] == busiest, CAP, counts)
    return counts.astype(jnp.int32)


def draw_block_sizes(key, part):
    counts = shared_counts(key)
    return counts


def draw_self_ids(key, part):
    counts = shared_counts(key)
    key = jax.random.fold_in(key, 5)
    first, second = jax.random.split(key)
    owner = jax.random.randint(first, (GROUPS, OUTER_ROWS), 0, OWNERS)
    spot = jax.random.randint(second, (GROUPS, OUTER_ROWS), 0, 1 << 20)
    group = jnp.arange(GROUPS, dtype=jnp.int32)[:, None]
    limit = counts[owner, group]
    slot = jnp.remainder(spot, limit)
    return (owner * CAP + slot).reshape(-1).astype(jnp.int32)


def set_ends(values, own_key, smallest, largest):
    spot = [jax.random.randint(jax.random.fold_in(own_key, axis), (), 0, length) for axis, length in enumerate(values.shape)]
    main_axis = values.shape.index(max(values.shape))
    beside = spot[:main_axis] + [(spot[main_axis] + 1) % values.shape[main_axis]] + spot[main_axis + 1:]
    return values.at[tuple(spot)].set(smallest).at[tuple(beside)].set(largest)


def block_levels(key, dims, cuts, smallest, top_value):
    level, own = 1.0, jax.random.fold_in(key, 6)
    for position, blocks in cuts:
        heights = jnp.exp(jax.random.uniform(jax.random.fold_in(own, position), (blocks,), jnp.float32, smallest / len(cuts), top_value / len(cuts)))
        level = level * jnp.repeat(heights, dims[position] // blocks).reshape([-1 if axis == position else 1 for axis in range(len(dims))])
    return level


def bell_draw(rng, dims, scale, most, shards=(), held_as=jnp.bfloat16):
    gain = block_levels(rng, dims, shards, -0.22, 0.18) if shards else 1.0
    values = jax.random.normal(rng, dims, jnp.float32) * scale * gain
    return jnp.minimum(jnp.maximum(values, -most), most).astype(held_as)


def setup_inputs(seed: int = 0) -> dict:
    keys = jax.random.split(jax.random.key(seed), 15)
    return {
        "features": bell_draw(keys[0], (TABLE_ROWS, F), 1.0, 6.0, ((0, 128),)),
        "sent_ids": set_ends(jax.random.randint(keys[1], (OWNERS, GROUPS, CAP), 0, ROWS_DEV), jax.random.fold_in(keys[1], 1), 0, ROWS_DEV - 1).astype(jnp.int32),
        "block_sizes": draw_block_sizes(jax.random.fold_in(keys[14], 71), 0),
        "self_ids": draw_self_ids(jax.random.fold_in(keys[14], 71), 0),
        "near_one": set_ends(jax.random.randint(keys[4], (GROUPS * OUTER_ROWS, FAN), 0, IN_ROWS), jax.random.fold_in(keys[4], 1), 0, IN_ROWS - 1).astype(jnp.int32),
        "degree_one": set_ends(jax.random.randint(keys[5], (GROUPS * OUTER_ROWS,), 1, FAN + 1), jax.random.fold_in(keys[5], 1), 1, FAN).astype(jnp.int32),
        "near_two": set_ends(jax.random.randint(keys[6], (GROUPS * MID_ROWS, FAN), 0, OUTER_ROWS), jax.random.fold_in(keys[6], 1), 0, OUTER_ROWS - 1).astype(jnp.int32),
        "degree_two": set_ends(jax.random.randint(keys[7], (GROUPS * MID_ROWS,), 1, FAN + 1), jax.random.fold_in(keys[7], 1), 1, FAN).astype(jnp.int32),
        "near_three": set_ends(jax.random.randint(keys[8], (GROUPS * SEEDS, FAN), 0, MID_ROWS), jax.random.fold_in(keys[8], 1), 0, MID_ROWS - 1).astype(jnp.int32),
        "degree_three": set_ends(jax.random.randint(keys[9], (GROUPS * SEEDS,), 1, FAN + 1), jax.random.fold_in(keys[9], 1), 1, FAN).astype(jnp.int32),
        "weight_one": bell_draw(keys[10], (2 * F, H), (2 * F) ** -0.5, 0.125, ((1, 4),)),
        "weight_two": bell_draw(keys[11], (2 * H, H), (2 * H) ** -0.5, 0.125, ((1, 4),)),
        "weight_three": bell_draw(keys[12], (2 * H, H), (2 * H) ** -0.5, 0.125, ((1, 4),)),
        "cotangent": bell_draw(keys[13], (GROUPS * SEEDS, H), 1.0, 6.0, ((0, 32), (1, 4))),
    }


def mean_rows(below, own, near, degree, filled):
    valid = jnp.arange(FAN, dtype=jnp.int32)[None, :] < degree[:, None]
    if filled is not None:
        valid = valid & filled[near]
    weights = valid.astype(jnp.float32)
    neighbours = below[near].astype(jnp.float32)
    summed = own.astype(jnp.float32) + jnp.sum(neighbours * weights[:, :, None], axis=1)
    counted = 1.0 + jnp.sum(weights, axis=1)
    return (summed / counted[:, None]).astype(jnp.bfloat16), weights, counted


def activate(preact):
    return (preact * jax.nn.sigmoid(preact)).astype(jnp.bfloat16)


def slope(preact):
    sig = jax.nn.sigmoid(preact)
    return sig * (1.0 + preact * (1.0 - sig))


def back_step(dpre, weight, near, weights, counted, preact_below):
    rows = dpre.shape[0]
    width = weight.shape[0] // 2
    spread = jnp.dot(dpre, weight.T, preferred_element_type=jnp.float32)
    dself = spread[:, :width]
    dmean = spread[:, width:]
    scaled = (dmean / counted[:, None]).astype(jnp.bfloat16)
    scaled_wide = scaled.astype(jnp.float32)
    terms = (weights[:, :, None] * scaled_wide[:, None, :]).reshape(-1, width)
    below = jnp.zeros((preact_below.shape[0], width), jnp.float32)
    below = below.at[near.reshape(-1)].add(terms)
    below = below.at[:rows].add(dself + scaled_wide)
    return (below * slope(preact_below)).astype(jnp.bfloat16)


def reference(features, sent_ids, block_sizes, self_ids, near_one, degree_one, near_two, degree_two, near_three, degree_three, weight_one, weight_two, weight_three, cotangent):
    owners = sent_ids.shape[0]
    groups = sent_ids.shape[1]
    slots = sent_ids.shape[2]
    base = (jnp.arange(owners, dtype=jnp.int32) * ROWS_DEV)[:, None]

    def piece(array, group, rows):
        return lax.dynamic_slice_in_dim(array, (group * rows).astype(jnp.int32), rows, 0)

    def one_group(carry, group):
        picks = lax.dynamic_index_in_dim(sent_ids, group, 1, keepdims=False)
        sizes = lax.dynamic_index_in_dim(block_sizes, group, 1, keepdims=False)
        keeps = jnp.arange(slots, dtype=jnp.int32)[None, :] < sizes[:, None]
        fetched = features[(base + picks).reshape(-1)].reshape(owners, slots, F)
        inputs = jnp.where(keeps[:, :, None], fetched, jnp.zeros((), jnp.bfloat16)).reshape(-1, F)
        filled = keeps.reshape(-1)
        own_one = inputs[piece(self_ids, group, OUTER_ROWS)]
        nb_one = piece(near_one, group, OUTER_ROWS)
        mean_one, wts_one, cnt_one = mean_rows(inputs, own_one, nb_one, piece(degree_one, group, OUTER_ROWS), filled)
        joined_one = jnp.concatenate([own_one, mean_one], axis=1)
        preact_one = jnp.dot(joined_one, weight_one, preferred_element_type=jnp.float32)
        hidden_one = activate(preact_one)
        own_two = hidden_one[:MID_ROWS]
        nb_two = piece(near_two, group, MID_ROWS)
        mean_two, wts_two, cnt_two = mean_rows(hidden_one, own_two, nb_two, piece(degree_two, group, MID_ROWS), None)
        joined_two = jnp.concatenate([own_two, mean_two], axis=1)
        preact_two = jnp.dot(joined_two, weight_two, preferred_element_type=jnp.float32)
        hidden_two = activate(preact_two)
        own_three = hidden_two[:SEEDS]
        nb_three = piece(near_three, group, SEEDS)
        mean_three, wts_three, cnt_three = mean_rows(hidden_two, own_three, nb_three, piece(degree_three, group, SEEDS), None)
        joined_three = jnp.concatenate([own_three, mean_three], axis=1)
        preact_three = jnp.dot(joined_three, weight_three, preferred_element_type=jnp.float32)
        embedding = preact_three.astype(jnp.bfloat16)
        dpre_three = piece(cotangent, group, SEEDS)
        grad_three = jnp.dot(joined_three.T, dpre_three, preferred_element_type=jnp.float32)
        dpre_two = back_step(dpre_three, weight_three, nb_three, wts_three, cnt_three, preact_two)
        grad_two = jnp.dot(joined_two.T, dpre_two, preferred_element_type=jnp.float32)
        dpre_one = back_step(dpre_two, weight_two, nb_two, wts_two, cnt_two, preact_one)
        grad_one = jnp.dot(joined_one.T, dpre_one, preferred_element_type=jnp.float32)
        return (carry[0] + grad_one, carry[1] + grad_two, carry[2] + grad_three), embedding

    start = (jnp.zeros((2 * F, H), jnp.float32), jnp.zeros((2 * H, H), jnp.float32), jnp.zeros((2 * H, H), jnp.float32))
    totals, embedded = lax.scan(one_group, start, jnp.arange(groups, dtype=jnp.int32))
    return embedded.reshape(-1, H), totals[0], totals[1], totals[2]
```

```python
import functools

import jax
import jax.numpy as jnp
from jax import lax
from jax.experimental import pallas as pl
from jax.experimental.pallas import tpu as pltpu
from jax.sharding import PartitionSpec as P

MESH = pl.DeviceIdType.MESH
F32 = jnp.float32
BF16 = jnp.bfloat16
SLOT = 16


def dot(a, b, left=1, right=0):
    return lax.dot_general(a, b, (((left,), (right,)), ((), ())), preferred_element_type=F32)


def slope(preact):
    sigma = jax.nn.sigmoid(preact)
    return sigma * (1.0 + preact * (1.0 - sigma))


def rows_at(index, size):
    return pl.ds(pl.multiple_of(index * size, size), size)


def step_of(rows, most):
    size = min(rows, most)
    while rows % size:
        size -= 1
    return size


def count_matches(ids, column_list, dst, rows, width):
    high = step_of(rows, 16)
    wide = step_of(width, 1024)

    def body(index, carry):
        part = ids[rows_at(index, high), :]
        for start in range(0, width, wide):
            place = lax.broadcasted_iota(jnp.int32, (high, wide), 1) + start
            total = jnp.zeros((high, wide), F32)
            for column in column_list:
                total = total + jnp.where(part[:, column : column + 1] == place, 1.0, 0.0)
            dst[rows_at(index, high), start : start + wide] = total.astype(BF16)
        return carry

    lax.fori_loop(0, rows // high, body, 0)


def kernel(
    stores, groups, slots,
    ids, near_one, near_two, near_three, cot, feat_hbm, one_hbm, two_hbm, three_hbm,
    emb_out, one_out, two_out, three_out,
    feat, hot, picked, arrived, filled, tile_one, tile_self, tile_two, tile_three,
    w_one, w_two, w_three, j_one, j_two, j_three, pre_one, pre_two, hid_one, hid_two,
    sp3_send, sp3_recv, sp2_send, sp2_recv, below3, dpre_two, dpre_one, full,
    px_send, px_recv, blk, rr,
    load_sem, in_send, in_recv,
    ag1_send, ag1_recv, ag2_send, ag2_recv, ag3_send, ag3_recv,
    sp_send_sem, sp_recv_sem, px_ssem, px_rsem, rr_ssem, rr_rsem,
):
    devices = stores * groups
    z = lax.axis_index("store")
    t = lax.axis_index("trainer")
    me = z * groups + t
    chip, core = t // 2, lax.rem(t, 2)
    chips = groups // 2
    right, left, across = (lax.rem(z + k, stores) for k in (1, 3, 2))
    width = cot.shape[1]
    seeds, mid, outer = cot.shape[0], near_two.shape[0], near_one.shape[0]
    cells = devices * SLOT

    def remote(src, dst, send_sem, recv_sem, store, trainer):
        return pltpu.make_async_remote_copy(
            src_ref=src, dst_ref=dst, send_sem=send_sem, recv_sem=recv_sem,
            device_id=(store, trainer), device_id_type=MESH,
        )

    def await_bytes(ref, sem):
        pltpu.make_async_copy(ref, ref, sem).wait()

    barrier = pltpu.get_barrier_semaphore()

    def greet(index, carry):
        other = lax.rem(me + index, devices)
        pl.semaphore_signal(
            barrier, inc=1, device_id=(other // groups, lax.rem(other, groups)), device_id_type=MESH
        )
        return carry

    lax.fori_loop(1, devices, greet, 0)

    loads = [pltpu.make_async_copy(feat_hbm, feat, load_sem.at[0])]
    for place, (hbm, held) in enumerate(((one_hbm, w_one), (two_hbm, w_two), (three_hbm, w_three))):
        for store in range(stores):
            for half in range(2):
                source = half * stores * width + store * width
                loads.append(
                    pltpu.make_async_copy(
                        hbm.at[pl.ds(source, width), :],
                        held.at[store, pl.ds(half * width, width), :],
                        load_sem.at[1 + (place * stores + store) * 2 + half],
                    )
                )
    for load in loads:
        load.start()

    count_matches(ids, [0], hot, groups * SLOT, feat.shape[0])
    loads[0].wait()
    pl.semaphore_wait(barrier, devices - 1)

    def fetch(index, carry):
        store = lax.rem(z + index, stores)
        columns = pl.ds(pl.multiple_of(store * width, width), width)
        rows = step_of(groups * SLOT, 256)
        for start in range(0, groups * SLOT, rows):
            part = dot(hot[start : start + rows, :], feat[:, columns])
            counts = ids[start : start + rows, 1:2].astype(F32)
            picked[store, start : start + rows, :] = (part + counts).astype(BF16)

        def send(number, inner):
            trainer = lax.rem(t + number * 13, groups)

            @pl.when(jnp.logical_or(store != z, trainer != t))
            def _():
                remote(
                    picked.at[store, rows_at(trainer, SLOT), :], arrived.at[rows_at(me, SLOT), :],
                    in_send.at[store], in_recv.at[z], store, trainer,
                ).start()

            return inner

        lax.fori_loop(0, groups, send, 0)
        return carry

    lax.fori_loop(0, stores, fetch, 0)
    own_block = pltpu.make_async_copy(
        picked.at[z, rows_at(t, SLOT), :], arrived.at[rows_at(me, SLOT), :], in_recv.at[z]
    )
    own_block.start()
    for load in loads[1:]:
        load.wait()

    others = ((right, 0), (left, 1), (across, 2))

    def send_spread(dpre, weight, send, recv, number):
        for store, place in others:
            send[place] = dot(dpre[...], weight[store], 1, 1).astype(BF16)
            remote(
                send.at[place], recv.at[place],
                sp_send_sem.at[number, place], sp_recv_sem.at[number, place], store, t,
            ).start()

    def take_spread(dpre, weight, recv, number):
        total = dot(dpre[...], weight[z], 1, 1)
        for place in range(3):
            await_bytes(recv.at[place], sp_recv_sem.at[number, place])
            total = total + recv[place].astype(F32)
        return total

    send_spread(cot, w_three, sp3_send, sp3_recv, 0)

    fan = near_two.shape[1]
    count_matches(near_one, list(range(fan)), tile_one, outer, cells)
    count_matches(near_one, [fan], tile_self, outer, cells)
    count_matches(near_two, list(range(fan)), tile_two, mid, outer)
    count_matches(near_three, list(range(fan)), tile_three, seeds, mid)

    def counted(near):
        return 1.0 + jnp.sum(jnp.where(near[...] >= 0, 1.0, 0.0), axis=1, keepdims=True)

    def spread_below(total, near, tile, below_rows):
        rows = near.shape[0]
        scaled = (total[:, width:] / counted(near)).astype(BF16)
        below = dot(tile[...], scaled, 0, 0)
        upper = below[:rows] + (total[:, :width] + scaled.astype(F32))
        return jnp.concatenate([upper, below[rows:]], axis=0)

    below3[...] = spread_below(take_spread(cot, w_three, sp3_recv, 0), near_three, tile_three, mid)

    def start_gather(held, index, rows, send_sem, recv_sem):
        piece = held.at[z, rows_at(index, rows), :]
        remote(piece, piece, send_sem.at[0, index], recv_sem.at[0, index], right, t).start()
        remote(piece, piece, send_sem.at[1, index], recv_sem.at[1, index], left, t).start()

    def take_gather(held, chunks, rows, send_sem, recv_sem, use):
        for index in range(chunks):
            here = rows_at(index, rows)
            for side, (source, onward) in enumerate(((left, right), (right, left))):
                piece = held.at[source, here, :]
                await_bytes(piece, recv_sem.at[side, index])
                if index % 2 == side:
                    remote(piece, piece, send_sem.at[2, index], recv_sem.at[2, index], onward, t).start()
            for source in (left, right):
                use(source, here)
        for index in range(chunks):
            here = rows_at(index, rows)
            await_bytes(held.at[across, here, :], recv_sem.at[2, index])
            use(across, here)

    def finish_gather(held, chunks, rows, send_sem):
        for way in range(3):
            for index in range(chunks):
                await_bytes(held.at[z, rows_at(index, rows), :], send_sem.at[way, index])

    for store in range(stores):
        await_bytes(arrived.at[pl.ds(store * groups * SLOT, groups * SLOT), :], in_recv.at[store])

    def mark(index, carry):
        here = rows_at(index, SLOT)
        block = arrived[here, 0 : filled.shape[1]].astype(F32)
        place = lax.broadcasted_iota(jnp.int32, block.shape, 0).astype(F32)
        filled[here, :] = jnp.where(place < block[slots : slots + 1, :], 1.0, 0.0).astype(BF16)
        return carry

    lax.fori_loop(0, devices, mark, 0)

    chunks_one = ag1_send.shape[1]
    rows_one = outer // chunks_one

    def layer_one(index, carry):
        here = rows_at(index, rows_one)
        own = dot(tile_self[here, :], arrived[...])
        valid = 1.0 + dot(tile_one[here, :], filled[...])
        valid = jnp.concatenate([valid] * (width // valid.shape[1]), axis=1)
        mean = (own + dot(tile_one[here, :], arrived[...])) / valid
        j_one[z, here, :] = jnp.concatenate([own, mean], axis=1).astype(BF16)
        start_gather(j_one, index, rows_one, ag1_send, ag1_recv)
        pre_one[here, :] = dot(j_one[z, here, :], w_one[z])
        return carry

    lax.fori_loop(0, chunks_one, layer_one, 0)

    def use_one(source, here):
        pre_one[here, :] += dot(j_one[source, here, :], w_one[source])

    take_gather(j_one, chunks_one, rows_one, ag1_send, ag1_recv, use_one)
    hid_one[...] = (pre_one[...] * jax.nn.sigmoid(pre_one[...])).astype(BF16)

    def join(hidden, near, tile, joined, chunks, send_sem, recv_sem):
        rows = near.shape[0]
        own = hidden[0:rows, :]
        mean = (own.astype(F32) + dot(tile[...], hidden[...])) / counted(near)
        joined[z] = jnp.concatenate([own, mean.astype(BF16)], axis=1)
        for index in range(chunks):
            start_gather(joined, index, rows // chunks, send_sem, recv_sem)

    chunks_two, chunks_three = ag2_send.shape[1], ag3_send.shape[1]
    rows_two, rows_three = mid // chunks_two, seeds // chunks_three
    join(hid_one, near_two, tile_two, j_two, chunks_two, ag2_send, ag2_recv)
    pre_two[...] = dot(j_two[z], w_two[z])

    def use_two(source, here):
        pre_two[here, :] += dot(j_two[source, here, :], w_two[source])

    take_gather(j_two, chunks_two, rows_two, ag2_send, ag2_recv, use_two)
    dpre_two[...] = (below3[...] * slope(pre_two[...])).astype(BF16)
    send_spread(dpre_two, w_two, sp2_send, sp2_recv, 1)
    hid_two[...] = (pre_two[...] * jax.nn.sigmoid(pre_two[...])).astype(BF16)
    join(hid_two, near_three, tile_three, j_three, chunks_three, ag3_send, ag3_recv)

    height = full.shape[1]
    per_slice = width // height

    def start_grad(number, joined, dpre):
        def products(store, carry):
            part = dot(joined[store], dpre[...], 0, 0)
            for half in range(2):
                for index in range(per_slice):
                    start = half * width + index * height
                    full[half * (groups // 2) + store * per_slice + index] = part[start : start + height, :]
            return carry

        lax.fori_loop(0, stores, products, 0)

        def pack(index, carry):
            px_send[number, index] = full[index * 2 + 1 - core].astype(BF16)
            return carry

        lax.fori_loop(0, chips, pack, 0)
        remote(
            px_send.at[number], px_recv.at[number], px_ssem.at[number], px_rsem.at[number], z, t + 1 - 2 * core
        ).start()
        await_bytes(px_recv.at[number], px_rsem.at[number])

        def spread(index, carry):
            target = lax.rem(chip + index, chips)
            total = full[target * 2 + core] + px_recv[number, target].astype(F32)
            blk[number, target] = total.astype(BF16)

            @pl.when(index > 0)
            def _():
                remote(
                    blk.at[number, target], rr.at[number, chip],
                    rr_ssem.at[number], rr_rsem.at[number], z, target * 2 + core,
                ).start()

            @pl.when(index == 0)
            def _():
                rr[number, chip] = total.astype(BF16)

            return carry

        lax.fori_loop(0, chips, spread, 0)

    def finish_grad(number, out):
        await_bytes(rr.at[number, pl.ds(0, chips - 1)], rr_rsem.at[number])
        out[...] = jnp.sum(rr[number].astype(F32), axis=0)

    start_grad(1, j_two, dpre_two)
    below2 = spread_below(take_spread(dpre_two, w_two, sp2_recv, 1), near_two, tile_two, outer)
    dpre_one[...] = (below2 * slope(pre_one[...])).astype(BF16)
    start_grad(0, j_one, dpre_one)

    emb = [dot(j_three[z], w_three[z])]

    def use_three(source, here):
        emb[0] = emb[0] + dot(j_three[source], w_three[source])

    def keep(source, here):
        return None

    take_gather(j_three, chunks_three, rows_three, ag3_send, ag3_recv, keep)
    for source in (left, right, across):
        use_three(source, None)
    emb_out[...] = emb[0].astype(BF16)
    start_grad(2, j_three, cot)

    finish_grad(1, two_out)
    finish_grad(0, one_out)
    finish_grad(2, three_out)

    for index in range(stores):
        store = lax.rem(z + index, stores)
        amount = groups - (1 if index == 0 else 0)
        await_bytes(picked.at[store, pl.ds(0, amount * SLOT), :], in_send.at[store])
    finish_gather(j_one, chunks_one, rows_one, ag1_send)
    finish_gather(j_two, chunks_two, rows_two, ag2_send)
    finish_gather(j_three, chunks_three, rows_three, ag3_send)
    for place in range(3):
        await_bytes(sp3_send.at[place], sp_send_sem.at[0, place])
        await_bytes(sp2_send.at[place], sp_send_sem.at[1, place])
    for number in range(3):
        await_bytes(px_send.at[number], px_ssem.at[number])
        await_bytes(blk.at[number, pl.ds(0, chips - 1)], rr_ssem.at[number])


def run(
    stores, groups, features, sent_ids, block_sizes, self_ids, near_one, degree_one, near_two, degree_two,
    near_three, degree_three, weight_one, weight_two, weight_three, cotangent,
):
    slots = sent_ids.shape[2]
    outer, mid, seeds = near_one.shape[0], near_two.shape[0], near_three.shape[0]
    fan = near_one.shape[1]
    fwidth = features.shape[1]
    width = cotangent.shape[1]
    devices = stores * groups
    cells = devices * SLOT
    height = 2 * fwidth // groups

    place = lax.broadcasted_iota(jnp.int32, (groups, SLOT), 1)
    sizes = block_sizes[0][:, None]
    padded = jnp.pad(sent_ids[0], ((0, 0), (0, SLOT - slots)))
    ids = jnp.stack(
        [jnp.where(place < sizes, padded, -1), jnp.where(place == slots, sizes, 0)], axis=-1
    ).reshape(groups * SLOT, 2)

    def used(near, degree):
        column = lax.broadcasted_iota(jnp.int32, near.shape, 1)
        return jnp.where(column < degree[:, None], near, -1)

    def moved(index):
        return index // slots * SLOT + lax.rem(index, slots)

    ids_one = jnp.concatenate([used(moved(near_one), degree_one), moved(self_ids)[:, None]], axis=1)
    vmem = pl.BlockSpec(memory_space=pltpu.VMEM)
    hbm = pl.BlockSpec(memory_space=pl.ANY)
    lanes = min(128, width)
    c1, c2, c3 = 4, 2, 2
    dma = pltpu.SemaphoreType.DMA
    chips = groups // 2
    scratch = [
        pltpu.VMEM(features.shape, BF16),
        pltpu.VMEM((groups * SLOT, features.shape[0]), BF16),
        pltpu.VMEM((stores, groups * SLOT, width), BF16),
        pltpu.VMEM((cells, width), BF16),
        pltpu.VMEM((cells, lanes), BF16),
        pltpu.VMEM((outer, cells), BF16),
        pltpu.VMEM((outer, cells), BF16),
        pltpu.VMEM((mid, outer), BF16),
        pltpu.VMEM((seeds, mid), BF16),
    ]
    scratch += [pltpu.VMEM((stores, 2 * width, width), BF16)] * 3
    scratch += [pltpu.VMEM((stores, rows, 2 * width), BF16) for rows in (outer, mid, seeds)]
    scratch += [pltpu.VMEM((rows, width), F32) for rows in (outer, mid)]
    scratch += [pltpu.VMEM((rows, width), BF16) for rows in (outer, mid)]
    scratch += [pltpu.VMEM((3, seeds, 2 * width), BF16)] * 2 + [pltpu.VMEM((3, mid, 2 * width), BF16)] * 2
    scratch += [
        pltpu.VMEM((mid, width), F32),
        pltpu.VMEM((mid, width), BF16),
        pltpu.VMEM((outer, width), BF16),
        pltpu.VMEM((groups, height, width), F32),
    ]
    scratch += [pltpu.VMEM((3, chips, height, width), BF16)] * 4
    scratch += [dma((1 + 6 * stores,)), dma((stores,)), dma((stores,))]
    scratch += [dma((3, chunks)) for chunks in (c1, c1, c2, c2, c3, c3)]
    scratch += [dma((2, 3)), dma((2, 3)), dma((3,)), dma((3,)), dma((3,)), dma((3,))]
    return pl.pallas_call(
        functools.partial(kernel, stores, groups, slots),
        out_shape=(
            jax.ShapeDtypeStruct((seeds, width), BF16),
            jax.ShapeDtypeStruct((height, width), F32),
            jax.ShapeDtypeStruct((height, width), F32),
            jax.ShapeDtypeStruct((height, width), F32),
        ),
        in_specs=[vmem] * 5 + [hbm] * 4,
        out_specs=(vmem,) * 4,
        scratch_shapes=scratch,
        compiler_params=pltpu.CompilerParams(
            collective_id=0, has_side_effects=True, vmem_limit_bytes=60 * 1024 * 1024
        ),
    )(
        ids, ids_one, used(near_two, degree_two), used(near_three, degree_three), cotangent,
        features, weight_one, weight_two, weight_three,
    )


def solution(mesh):
    stores, groups = mesh.shape["store"], mesh.shape["trainer"]
    both = ("store", "trainer")
    placed = (
        P(both, None), P(both, None, None), P(both, None), P("trainer"), P("trainer", None), P("trainer"),
        P("trainer", None), P("trainer"), P("trainer", None), P("trainer"),
        P(None, "store"), P(None, "store"), P(None, "store"), P("trainer", "store"),
    )
    return jax.shard_map(
        functools.partial(run, stores, groups),
        mesh=mesh, in_specs=placed, out_specs=(P("trainer", "store"),) * 4, check_vma=False,
    )
```

```python
import functools

import jax
import jax.numpy as jnp
from jax import lax
from jax.experimental import pallas as pl
from jax.experimental.pallas import tpu as pltpu
from jax.sharding import PartitionSpec as P

MESH = pl.DeviceIdType.MESH
F32 = jnp.float32
BF16 = jnp.bfloat16
SLOT = 16


def dot(a, b, left=1, right=0):
    return lax.dot_general(a, b, (((left,), (right,)), ((), ())), preferred_element_type=F32)


def slope(preact):
    sigma = jax.nn.sigmoid(preact)
    return sigma * (1.0 + preact * (1.0 - sigma))


def rows_at(index, size):
    return pl.ds(pl.multiple_of(index * size, size), size)


def step_of(rows, most):
    size = min(rows, most)
    while rows % size:
        size -= 1
    return size


def count_matches(ids, column_list, dst, rows, width):
    high = step_of(rows, 16)
    wide = step_of(width, 1024)

    def body(index, carry):
        part = ids[rows_at(index, high), :]
        for start in range(0, width, wide):
            place = lax.broadcasted_iota(jnp.int32, (high, wide), 1) + start
            total = jnp.zeros((high, wide), F32)
            for column in column_list:
                total = total + jnp.where(part[:, column : column + 1] == place, 1.0, 0.0)
            dst[rows_at(index, high), start : start + wide] = total.astype(BF16)
        return carry

    lax.fori_loop(0, rows // high, body, 0)


def kernel(
    stores, groups, slots,
    sent, sizes, self_ids, near_one_t, degree_one, near_two_t, degree_two, near_three_t, degree_three,
    cot, feat_hbm, one_hbm, two_hbm, three_hbm,
    emb_out, one_out, two_out, three_out,
    near_one, near_two, near_three, extra, feat, hot, picked, arrived, filled, tile_one, tile_self, tile_two, tile_three,
    w_one, w_two, w_three, j_one, j_two, j_three, pre_one, pre_two, hid_one, hid_two,
    sp3_send, sp3_recv, sp2_send, sp2_recv, below3, dpre_two, dpre_one, full,
    px_send, px_recv, blk, rr,
    load_sem, in_send, in_recv,
    ag1_send, ag1_recv, ag2_send, ag2_recv, ag3_send, ag3_recv,
    sp_send_sem, sp_recv_sem, px_ssem, px_rsem, rr_ssem, rr_rsem,
):
    devices = stores * groups
    z = lax.axis_index("store")
    t = lax.axis_index("trainer")
    me = z * groups + t
    chip, core = t // 2, lax.rem(t, 2)
    chips = groups // 2
    right, left, across = (lax.rem(z + k, stores) for k in (1, 3, 2))
    width = cot.shape[1]
    seeds, mid, outer = cot.shape[0], near_two.shape[0], near_one.shape[0]
    cells = devices * SLOT
    pending = []

    def remote(src, dst, send_sem, recv_sem, store, trainer):
        return pltpu.make_async_remote_copy(
            src_ref=src, dst_ref=dst, send_sem=send_sem, recv_sem=recv_sem,
            device_id=(store, trainer), device_id_type=MESH,
        )

    def await_bytes(ref, sem):
        pltpu.make_async_copy(ref, ref, sem).wait()

    barrier = pltpu.get_barrier_semaphore()

    def greet(index, carry):
        other = lax.rem(me + index, devices)
        pl.semaphore_signal(
            barrier, inc=1, device_id=(other // groups, lax.rem(other, groups)), device_id_type=MESH
        )
        return carry

    lax.fori_loop(1, devices, greet, 0)

    loads = [pltpu.make_async_copy(feat_hbm, feat, load_sem.at[0])]
    for place, (hbm, held) in enumerate(((one_hbm, w_one), (two_hbm, w_two), (three_hbm, w_three))):
        for store in range(stores):
            for half in range(2):
                source = half * stores * width + store * width
                loads.append(
                    pltpu.make_async_copy(
                        hbm.at[pl.ds(source, width), :],
                        held.at[store, pl.ds(half * width, width), :],
                        load_sem.at[1 + (place * stores + store) * 2 + half],
                    )
                )
    for load in loads:
        load.start()

    slot = lax.broadcasted_iota(jnp.int32, (SLOT, groups), 0)
    amounts = jnp.broadcast_to(sizes[...], (SLOT, groups))
    wanted = jnp.concatenate([sent[index] for index in range(slots)] + [jnp.full((SLOT - slots, groups), -1, jnp.int32)], axis=0)
    wanted = jnp.where(slot < amounts, wanted, -1)
    notes = jnp.where(slot == slots, amounts, 0).astype(F32)
    wide = step_of(feat.shape[0], 1024)
    for group in range(groups):
        here = pl.ds(group * SLOT, SLOT)
        extra[here, :] = jnp.broadcast_to(notes[:, group : group + 1], (SLOT, extra.shape[1]))
        for start in range(0, feat.shape[0], wide):
            place = lax.broadcasted_iota(jnp.int32, (SLOT, wide), 1) + start
            hot[here, start : start + wide] = jnp.where(wanted[:, group : group + 1] == place, 1.0, 0.0).astype(BF16)
    loads[0].wait()
    pl.semaphore_wait(barrier, devices - 1)

    def fetch(index, carry):
        store = lax.rem(z + index, stores)
        columns = pl.ds(pl.multiple_of(store * width, width), width)
        rows = step_of(groups * SLOT, 256)
        for start in range(0, groups * SLOT, rows):
            part = dot(hot[start : start + rows, :], feat[:, columns])
            counts = jnp.concatenate([extra[start : start + rows, :]] * (width // extra.shape[1]), axis=1)
            picked[store, start : start + rows, :] = (part + counts).astype(BF16)

        def send(number, inner):
            trainer = lax.rem(t + number * 13, groups)

            @pl.when(jnp.logical_or(store != z, trainer != t))
            def _():
                remote(
                    picked.at[store, rows_at(trainer, SLOT), :], arrived.at[rows_at(me, SLOT), :],
                    in_send.at[store], in_recv.at[z], store, trainer,
                ).start()

            return inner

        lax.fori_loop(0, groups, send, 0)
        return carry

    lax.fori_loop(0, stores, fetch, 0)
    own_block = pltpu.make_async_copy(
        picked.at[z, rows_at(t, SLOT), :], arrived.at[rows_at(me, SLOT), :], in_recv.at[z]
    )
    own_block.start()

    def leave_blocks():
        for index in range(stores):
            store = lax.rem(z + index, stores)
            amount = groups - (1 if index == 0 else 0)
            await_bytes(picked.at[store, pl.ds(0, amount * SLOT), :], in_send.at[store])

    pending.append(leave_blocks)
    for load in loads[1:]:
        load.wait()

    others = ((right, 0), (left, 1), (across, 2))

    def send_spread(dpre, weight, send, recv, number):
        for store, place in others:
            send[place] = dot(dpre[...], weight[store], 1, 1).astype(BF16)
            remote(
                send.at[place], recv.at[place],
                sp_send_sem.at[number, place], sp_recv_sem.at[number, place], store, t,
            ).start()
            pending.append(lambda place=place: await_bytes(send.at[place], sp_send_sem.at[number, place]))

    def take_spread(dpre, weight, recv, number):
        total = dot(dpre[...], weight[z], 1, 1)
        for place in range(3):
            await_bytes(recv.at[place], sp_recv_sem.at[number, place])
            total = total + recv[place].astype(F32)
        return total

    send_spread(cot, w_three, sp3_send, sp3_recv, 0)

    fan = near_two_t.shape[0]

    def moved(index):
        return index + (SLOT - slots) * ((index * ((1 << 19) // slots + 1)) >> 19)

    def upright(near, degree, own, dst):
        rows = near.shape[1]
        place = lax.broadcasted_iota(jnp.int32, (fan, rows), 0)
        parts = [jnp.where(place < degree[...][None, :], near, -1)] + own
        parts.append(jnp.full((SLOT - fan - len(own), rows), -1, jnp.int32))
        dst[...] = jnp.concatenate(parts, axis=0).T

    upright(moved(near_one_t[...]), degree_one, [moved(self_ids[...][None, :])], near_one)
    upright(near_two_t[...], degree_two, [], near_two)
    upright(near_three_t[...], degree_three, [], near_three)
    count_matches(near_one, list(range(fan)), tile_one, outer, cells)
    count_matches(near_one, [fan], tile_self, outer, cells)
    count_matches(near_two, list(range(fan)), tile_two, mid, outer)
    count_matches(near_three, list(range(fan)), tile_three, seeds, mid)

    def counted(near):
        return 1.0 + jnp.sum(jnp.where(near[...] >= 0, 1.0, 0.0), axis=1, keepdims=True)

    def spread_below(total, near, tile, below_rows):
        rows = near.shape[0]
        scaled = (total[:, width:] / counted(near)).astype(BF16)
        below = dot(tile[...], scaled, 0, 0)
        upper = below[:rows] + (total[:, :width] + scaled.astype(F32))
        return jnp.concatenate([upper, below[rows:]], axis=0)

    below3[...] = spread_below(take_spread(cot, w_three, sp3_recv, 0), near_three, tile_three, mid)

    def start_gather(held, index, rows, send_sem, recv_sem):
        piece = held.at[z, rows_at(index, rows), :]
        remote(piece, piece, send_sem.at[0, index], recv_sem.at[0, index], right, t).start()
        remote(piece, piece, send_sem.at[1, index], recv_sem.at[1, index], left, t).start()

    def take_gather(held, chunks, rows, send_sem, recv_sem, use):
        for index in range(chunks):
            here = rows_at(index, rows)
            for side, (source, onward) in enumerate(((left, right), (right, left))):
                piece = held.at[source, here, :]
                await_bytes(piece, recv_sem.at[side, index])
                if index % 2 == side:
                    remote(piece, piece, send_sem.at[2, index], recv_sem.at[2, index], onward, t).start()
            for source in (left, right):
                use(source, here)
        for index in range(chunks):
            here = rows_at(index, rows)
            await_bytes(held.at[across, here, :], recv_sem.at[2, index])
            use(across, here)
        for way in range(3):
            for index in range(chunks):
                pending.append(
                    lambda way=way, here=rows_at(index, rows), index=index: await_bytes(
                        held.at[z, here, :], send_sem.at[way, index]
                    )
                )

    for store in range(stores):
        await_bytes(arrived.at[pl.ds(store * groups * SLOT, groups * SLOT), :], in_recv.at[store])

    def mark(index, carry):
        here = rows_at(index, SLOT)
        block = arrived[here, 0 : filled.shape[1]].astype(F32)
        place = lax.broadcasted_iota(jnp.int32, block.shape, 0).astype(F32)
        filled[here, :] = jnp.where(place < block[slots : slots + 1, :], 1.0, 0.0).astype(BF16)
        return carry

    lax.fori_loop(0, devices, mark, 0)

    chunks_one = ag1_send.shape[1]
    rows_one = outer // chunks_one

    def layer_one(index, carry):
        here = rows_at(index, rows_one)
        own = dot(tile_self[here, :], arrived[...])
        valid = 1.0 + dot(tile_one[here, :], filled[...])
        valid = jnp.concatenate([valid] * (width // valid.shape[1]), axis=1)
        mean = (own + dot(tile_one[here, :], arrived[...])) / valid
        j_one[z, here, :] = jnp.concatenate([own, mean], axis=1).astype(BF16)
        start_gather(j_one, index, rows_one, ag1_send, ag1_recv)
        pre_one[here, :] = dot(j_one[z, here, :], w_one[z])
        return carry

    lax.fori_loop(0, chunks_one, layer_one, 0)

    def use_one(source, here):
        pre_one[here, :] += dot(j_one[source, here, :], w_one[source])

    take_gather(j_one, chunks_one, rows_one, ag1_send, ag1_recv, use_one)
    hid_one[...] = (pre_one[...] * jax.nn.sigmoid(pre_one[...])).astype(BF16)

    def join(hidden, near, tile, joined, chunks, send_sem, recv_sem):
        rows = near.shape[0]
        own = hidden[0:rows, :]
        mean = (own.astype(F32) + dot(tile[...], hidden[...])) / counted(near)
        joined[z] = jnp.concatenate([own, mean.astype(BF16)], axis=1)
        for index in range(chunks):
            start_gather(joined, index, rows // chunks, send_sem, recv_sem)

    chunks_two, chunks_three = ag2_send.shape[1], ag3_send.shape[1]
    rows_two, rows_three = mid // chunks_two, seeds // chunks_three
    join(hid_one, near_two, tile_two, j_two, chunks_two, ag2_send, ag2_recv)
    pre_two[...] = dot(j_two[z], w_two[z])

    def use_two(source, here):
        pre_two[here, :] += dot(j_two[source, here, :], w_two[source])

    take_gather(j_two, chunks_two, rows_two, ag2_send, ag2_recv, use_two)
    dpre_two[...] = (below3[...] * slope(pre_two[...])).astype(BF16)
    send_spread(dpre_two, w_two, sp2_send, sp2_recv, 1)
    hid_two[...] = (pre_two[...] * jax.nn.sigmoid(pre_two[...])).astype(BF16)
    join(hid_two, near_three, tile_three, j_three, chunks_three, ag3_send, ag3_recv)

    height = full.shape[1]
    per_slice = width // height

    def start_grad(number, joined, dpre):
        def products(store, carry):
            part = dot(joined[store], dpre[...], 0, 0)
            for half in range(2):
                for index in range(per_slice):
                    start = half * width + index * height
                    full[half * (groups // 2) + store * per_slice + index] = part[start : start + height, :]
            return carry

        lax.fori_loop(0, stores, products, 0)

        def pack(index, carry):
            px_send[number, index] = full[index * 2 + 1 - core].astype(BF16)
            return carry

        lax.fori_loop(0, chips, pack, 0)
        remote(
            px_send.at[number], px_recv.at[number], px_ssem.at[number], px_rsem.at[number], z, t + 1 - 2 * core
        ).start()
        pending.append(lambda: await_bytes(px_send.at[number], px_ssem.at[number]))
        await_bytes(px_recv.at[number], px_rsem.at[number])

        def spread(index, carry):
            target = lax.rem(chip + index, chips)
            total = full[target * 2 + core] + px_recv[number, target].astype(F32)
            blk[number, target] = total.astype(BF16)

            @pl.when(index > 0)
            def _():
                remote(
                    blk.at[number, target], rr.at[number, chip],
                    rr_ssem.at[number], rr_rsem.at[number], z, target * 2 + core,
                ).start()

            @pl.when(index == 0)
            def _():
                rr[number, chip] = total.astype(BF16)

            return carry

        lax.fori_loop(0, chips, spread, 0)
        pending.append(lambda: await_bytes(blk.at[number, pl.ds(0, chips - 1)], rr_ssem.at[number]))

    def finish_grad(number, out):
        await_bytes(rr.at[number, pl.ds(0, chips - 1)], rr_rsem.at[number])
        out[...] = jnp.sum(rr[number].astype(F32), axis=0)

    start_grad(1, j_two, dpre_two)
    below2 = spread_below(take_spread(dpre_two, w_two, sp2_recv, 1), near_two, tile_two, outer)
    dpre_one[...] = (below2 * slope(pre_one[...])).astype(BF16)
    start_grad(0, j_one, dpre_one)

    emb = [dot(j_three[z], w_three[z])]

    def use_three(source, here):
        emb[0] = emb[0] + dot(j_three[source], w_three[source])

    def keep(source, here):
        return None

    take_gather(j_three, chunks_three, rows_three, ag3_send, ag3_recv, keep)
    for source in (left, right, across):
        use_three(source, None)
    emb_out[...] = emb[0].astype(BF16)
    start_grad(2, j_three, cot)

    finish_grad(1, two_out)
    finish_grad(0, one_out)
    finish_grad(2, three_out)

    for leave in pending:
        leave()


def copies(*refs):
    half = len(refs) // 2
    for source, target in zip(refs[:half], refs[half:]):
        target[...] = source[...]


def run(
    stores, groups, features, sent_ids, block_sizes, self_ids, near_one, degree_one, near_two, degree_two,
    near_three, degree_three, weight_one, weight_two, weight_three, cotangent,
):
    slots = sent_ids.shape[2]
    outer, mid, seeds = near_one.shape[0], near_two.shape[0], near_three.shape[0]
    fan = near_one.shape[1]
    fwidth = features.shape[1]
    width = cotangent.shape[1]
    devices = stores * groups
    cells = devices * SLOT
    height = 2 * fwidth // groups

    vmem = pl.BlockSpec(memory_space=pltpu.VMEM)
    hbm = pl.BlockSpec(memory_space=pl.ANY)
    lanes = min(128, width)
    c1, c2, c3 = 4, 2, 2
    dma = pltpu.SemaphoreType.DMA
    chips = groups // 2
    scratch = [pltpu.VMEM((rows, SLOT), jnp.int32) for rows in (outer, mid, seeds)]
    scratch += [
        pltpu.VMEM((groups * SLOT, lanes), F32),
        pltpu.VMEM(features.shape, BF16),
        pltpu.VMEM((groups * SLOT, features.shape[0]), BF16),
        pltpu.VMEM((stores, groups * SLOT, width), BF16),
        pltpu.VMEM((cells, width), BF16),
        pltpu.VMEM((cells, lanes), BF16),
        pltpu.VMEM((outer, cells), BF16),
        pltpu.VMEM((outer, cells), BF16),
        pltpu.VMEM((mid, outer), BF16),
        pltpu.VMEM((seeds, mid), BF16),
    ]
    scratch += [pltpu.VMEM((stores, 2 * width, width), BF16)] * 3
    scratch += [pltpu.VMEM((stores, rows, 2 * width), BF16) for rows in (outer, mid, seeds)]
    scratch += [pltpu.VMEM((rows, width), F32) for rows in (outer, mid)]
    scratch += [pltpu.VMEM((rows, width), BF16) for rows in (outer, mid)]
    scratch += [pltpu.VMEM((3, seeds, 2 * width), BF16)] * 2 + [pltpu.VMEM((3, mid, 2 * width), BF16)] * 2
    scratch += [
        pltpu.VMEM((mid, width), F32),
        pltpu.VMEM((mid, width), BF16),
        pltpu.VMEM((outer, width), BF16),
        pltpu.VMEM((groups, height, width), F32),
    ]
    scratch += [pltpu.VMEM((3, chips, height, width), BF16)] * 4
    scratch += [dma((1 + 6 * stores,)), dma((stores,)), dma((stores,))]
    scratch += [dma((3, chunks)) for chunks in (c1, c1, c2, c2, c3, c3)]
    scratch += [dma((2, 3)), dma((2, 3)), dma((3,)), dma((3,)), dma((3,)), dma((3,))]
    shapes = (
        jax.ShapeDtypeStruct((seeds, width), BF16),
        jax.ShapeDtypeStruct((height, width), F32),
        jax.ShapeDtypeStruct((height, width), F32),
        jax.ShapeDtypeStruct((height, width), F32),
    )
    results = pl.pallas_call(
        functools.partial(kernel, stores, groups, slots),
        out_shape=shapes,
        in_specs=[vmem] * 10 + [hbm] * 4,
        out_specs=(vmem,) * 4,
        scratch_shapes=scratch,
        compiler_params=pltpu.CompilerParams(
            collective_id=0, has_side_effects=True, vmem_limit_bytes=60 * 1024 * 1024
        ),
    )(
        jnp.transpose(sent_ids, (2, 0, 1)), block_sizes, self_ids,
        near_one.T, degree_one, near_two.T, degree_two, near_three.T, degree_three,
        cotangent, features, weight_one, weight_two, weight_three,
    )
    return pl.pallas_call(copies, out_shape=shapes, in_specs=[vmem] * 4, out_specs=(vmem,) * 4)(*results)


def solution(mesh):
    stores, groups = mesh.shape["store"], mesh.shape["trainer"]
    both = ("store", "trainer")
    placed = (
        P(both, None), P(both, None, None), P(both, None), P("trainer"), P("trainer", None), P("trainer"),
        P("trainer", None), P("trainer"), P("trainer", None), P("trainer"),
        P(None, "store"), P(None, "store"), P(None, "store"), P("trainer", "store"),
    )
    return jax.shard_map(
        functools.partial(run, stores, groups),
        mesh=mesh, in_specs=placed, out_specs=(P("trainer", "store"),) * 4, check_vma=False,
    )
```

```python
import functools

import jax
import jax.numpy as jnp
from jax import lax
from jax.experimental import pallas as pl
from jax.experimental.pallas import tpu as pltpu
from jax.sharding import PartitionSpec as P

MESH = pl.DeviceIdType.MESH
F32 = jnp.float32
BF16 = jnp.bfloat16
SLOT = 16


def dot(a, b, left=1, right=0):
    return lax.dot_general(a, b, (((left,), (right,)), ((), ())), preferred_element_type=F32)


def slope(preact):
    sigma = jax.nn.sigmoid(preact)
    return sigma * (1.0 + preact * (1.0 - sigma))


def rows_at(index, size):
    return pl.ds(pl.multiple_of(index * size, size), size)


def step_of(rows, most):
    size = min(rows, most)
    while rows % size:
        size -= 1
    return size


def count_matches(ids, column_list, dst, rows, width):
    high = step_of(rows, 16)
    wide = step_of(width, 1024)

    def body(index, carry):
        part = ids[rows_at(index, high), :]
        for start in range(0, width, wide):
            place = lax.broadcasted_iota(jnp.int32, (high, wide), 1) + start
            total = jnp.zeros((high, wide), F32)
            for column in column_list:
                total = total + jnp.where(part[:, column : column + 1] == place, 1.0, 0.0)
            dst[rows_at(index, high), start : start + wide] = total.astype(BF16)
        return carry

    lax.fori_loop(0, rows // high, body, 0)


def kernel(
    stores, groups, slots,
    sent, sizes, self_ids, near_one_t, degree_one, near_two_t, degree_two, near_three_t, degree_three,
    cot, feat_hbm, one_hbm, two_hbm, three_hbm,
    emb_out, one_out, two_out, three_out,
    near_one, near_two, near_three, extra, feat, hot, picked, arrived, filled,
    tile_one, tile_self, tile_two, tile_three, w_one, w_rows,
    j_one, j_two, j_three, pre_one, pre_two, hid_one, hid_two, cots, dpres, spread_two, below3, dpre_one,
    part_two, got_two, part_three, got_three,
    full, px_send, px_recv, blk, rr, move_send, move_recv,
    load_sem, in_send, in_recv, ag1_send, ag1_recv, agd_send, agd_recv,
    cot_ssem, cot_rsem, wz_ssem, wz_rsem, wp_ssem, wp_rsem, ws_ssem, ws_rsem,
    rs_ssem, rs_rsem, px_ssem, px_rsem, rr_ssem, rr_rsem, mv_ssem, mv_rsem,
):
    devices = stores * groups
    z = lax.axis_index("store")
    t = lax.axis_index("trainer")
    me = z * groups + t
    chip, core = t // 2, lax.rem(t, 2)
    chips = groups // 2
    sibling = t + 1 - 2 * core
    right, left, across = (lax.rem(z + k, stores) for k in (1, 3, 2))
    others = ((across, 2), (right, 0), (left, 1))
    width = cot.shape[1]
    seeds, mid, outer = cot.shape[0], near_two.shape[0], near_one.shape[0]
    cells = devices * SLOT
    fan = near_two_t.shape[0]
    pending = []

    def remote(src, dst, send_sem, recv_sem, store, trainer):
        return pltpu.make_async_remote_copy(
            src_ref=src, dst_ref=dst, send_sem=send_sem, recv_sem=recv_sem,
            device_id=(store, trainer), device_id_type=MESH,
        )

    def await_bytes(ref, sem):
        pltpu.make_async_copy(ref, ref, sem).wait()

    barrier = pltpu.get_barrier_semaphore()

    def greet(index, carry):
        other = lax.rem(me + index, devices)
        pl.semaphore_signal(
            barrier, inc=1, device_id=(other // groups, lax.rem(other, groups)), device_id_type=MESH
        )
        return carry

    lax.fori_loop(1, devices, greet, 0)

    share = w_rows.shape[4]

    def piece_of(hbm, store):
        return hbm.at[pl.ds(pl.multiple_of(core * stores * width + store * width + chip * share, share), share), :]

    loads = [pltpu.make_async_copy(feat_hbm, feat, load_sem.at[0])]
    for place, hbm in enumerate((two_hbm, three_hbm)):
        loads.append(pltpu.make_async_copy(piece_of(hbm, z), w_rows.at[place, core, chip, z], load_sem.at[1 + place]))
    loads.append(pltpu.make_async_copy(cot, cots.at[z], load_sem.at[3]))
    for store in range(stores):
        for half in range(2):
            loads.append(
                pltpu.make_async_copy(
                    one_hbm.at[pl.ds((half * stores + store) * width, width), :],
                    w_one.at[store, pl.ds(half * width, width), :],
                    load_sem.at[4 + store * 2 + half],
                )
            )
    for load in loads:
        load.start()

    slot = lax.broadcasted_iota(jnp.int32, (SLOT, groups), 0)
    amounts = jnp.broadcast_to(sizes[...], (SLOT, groups))
    wanted = jnp.concatenate([sent[index] for index in range(slots)] + [jnp.full((SLOT - slots, groups), -1, jnp.int32)], axis=0)
    wanted = jnp.where(slot < amounts, wanted, -1)
    notes = jnp.where(slot == slots, amounts, 0).astype(F32)
    wide = step_of(feat.shape[0], 1024)
    for group in range(groups):
        here = pl.ds(group * SLOT, SLOT)
        extra[here, :] = jnp.broadcast_to(notes[:, group : group + 1], (SLOT, extra.shape[1]))
        for start in range(0, feat.shape[0], wide):
            place = lax.broadcasted_iota(jnp.int32, (SLOT, wide), 1) + start
            hot[here, start : start + wide] = jnp.where(wanted[:, group : group + 1] == place, 1.0, 0.0).astype(BF16)
    loads[0].wait()
    pl.semaphore_wait(barrier, devices - 1)

    for store, place in others:
        remote(cot, cots.at[z], cot_ssem.at[place], cot_rsem.at[place], store, t).start()
        pending.append(lambda place=place: await_bytes(cot, cot_ssem.at[place]))
        for number, hbm in enumerate((two_hbm, three_hbm)):
            spot = w_rows.at[number, core, chip, z]
            remote(piece_of(hbm, store), spot, wz_ssem.at[number, place], wz_rsem.at[number, place], store, t).start()
            pending.append(lambda number=number, place=place, spot=spot: await_bytes(spot, wz_ssem.at[number, place]))

    def fetch(index, carry):
        store = lax.rem(z + index, stores)
        columns = pl.ds(pl.multiple_of(store * width, width), width)
        rows = step_of(groups * SLOT, 256)
        for start in range(0, groups * SLOT, rows):
            part = dot(hot[start : start + rows, :], feat[:, columns])
            counts = jnp.concatenate([extra[start : start + rows, :]] * (width // extra.shape[1]), axis=1)
            picked[store, start : start + rows, :] = (part + counts).astype(BF16)

        def send(number, inner):
            trainer = lax.rem(t + number * 13, groups)

            @pl.when(jnp.logical_or(store != z, trainer != t))
            def _():
                remote(
                    picked.at[store, rows_at(trainer, SLOT), :], arrived.at[rows_at(me, SLOT), :],
                    in_send.at[store], in_recv.at[z], store, trainer,
                ).start()

            return inner

        lax.fori_loop(0, groups, send, 0)
        return carry

    lax.fori_loop(0, stores, fetch, 0)
    own_block = pltpu.make_async_copy(
        picked.at[z, rows_at(t, SLOT), :], arrived.at[rows_at(me, SLOT), :], in_recv.at[z]
    )
    own_block.start()

    def leave_blocks():
        for index in range(stores):
            store = lax.rem(z + index, stores)
            amount = groups - (1 if index == 0 else 0)
            await_bytes(picked.at[store, pl.ds(0, amount * SLOT), :], in_send.at[store])

    pending.append(leave_blocks)
    for load in loads[1:]:
        load.wait()

    def moved(index):
        return index + (SLOT - slots) * ((index * ((1 << 19) // slots + 1)) >> 19)

    def upright(near, degree, own, dst):
        rows = near.shape[1]
        place = lax.broadcasted_iota(jnp.int32, (fan, rows), 0)
        parts = [jnp.where(place < degree[...][None, :], near, -1)] + own
        parts.append(jnp.full((SLOT - fan - len(own), rows), -1, jnp.int32))
        dst[...] = jnp.concatenate(parts, axis=0).T

    upright(moved(near_one_t[...]), degree_one, [moved(self_ids[...][None, :])], near_one)
    upright(near_two_t[...], degree_two, [], near_two)
    upright(near_three_t[...], degree_three, [], near_three)
    count_matches(near_one, list(range(fan)), tile_one, outer, cells)
    count_matches(near_one, [fan], tile_self, outer, cells)
    count_matches(near_two, list(range(fan)), tile_two, mid, outer)
    count_matches(near_three, list(range(fan)), tile_three, seeds, mid)

    def counted(near):
        return 1.0 + jnp.sum(jnp.where(near[...] >= 0, 1.0, 0.0), axis=1, keepdims=True)

    def spread_below(total, near, tile):
        rows = near.shape[0]
        scaled = (total[:, width:] / counted(near)).astype(BF16)
        below = dot(tile[...], scaled, 0, 0)
        upper = below[:rows] + (total[:, :width] + scaled.astype(F32))
        return jnp.concatenate([upper, below[rows:]], axis=0)

    def start_gather(held, index, rows, send_sem, recv_sem):
        piece = held.at[z, rows_at(index, rows), :]
        remote(piece, piece, send_sem.at[0, index], recv_sem.at[0, index], right, t).start()
        remote(piece, piece, send_sem.at[1, index], recv_sem.at[1, index], left, t).start()

    def take_gather(held, chunks, rows, send_sem, recv_sem, use, between):
        for index in range(chunks):
            here = rows_at(index, rows)
            for side, (source, onward) in enumerate(((left, right), (right, left))):
                piece = held.at[source, here, :]
                await_bytes(piece, recv_sem.at[side, index])
                if index % 2 == side:
                    remote(piece, piece, send_sem.at[2, index], recv_sem.at[2, index], onward, t).start()
            for source in (left, right):
                use(source, here)
        between()
        for index in range(chunks):
            here = rows_at(index, rows)
            await_bytes(held.at[across, here, :], recv_sem.at[2, index])
            use(across, here)
        for way in range(3):
            for index in range(chunks):
                pending.append(
                    lambda way=way, here=rows_at(index, rows), index=index: await_bytes(
                        held.at[z, here, :], send_sem.at[way, index]
                    )
                )

    def mark(index, carry):
        here = rows_at(index, SLOT)
        block = arrived[here, 0 : filled.shape[1]].astype(F32)
        place = lax.broadcasted_iota(jnp.int32, block.shape, 0).astype(F32)
        filled[here, :] = jnp.where(place < block[slots : slots + 1, :], 1.0, 0.0).astype(BF16)
        return carry

    for store in range(stores):
        await_bytes(arrived.at[pl.ds(store * groups * SLOT, groups * SLOT), :], in_recv.at[store])
        lax.fori_loop(store * groups, (store + 1) * groups, mark, 0)

    chunks_one = ag1_send.shape[1]
    rows_one = outer // chunks_one

    def layer_one(index, carry):
        here = rows_at(index, rows_one)
        own = dot(tile_self[here, :], arrived[...])
        valid = 1.0 + dot(tile_one[here, :], filled[...])
        valid = jnp.concatenate([valid] * (width // valid.shape[1]), axis=1)
        mean = (own + dot(tile_one[here, :], arrived[...])) / valid
        j_one[z, here, :] = jnp.concatenate([own, mean], axis=1).astype(BF16)
        start_gather(j_one, index, rows_one, ag1_send, ag1_recv)
        pre_one[here, :] = dot(j_one[z, here, :], w_one[z])
        return carry

    lax.fori_loop(0, chunks_one, layer_one, 0)

    for number in range(2):
        for store, place in others:
            await_bytes(w_rows.at[number, core, chip, store], wz_rsem.at[number, place])

        def pass_on(index, carry, number=number):
            target = lax.rem(chip + index, chips)
            spot = w_rows.at[number, core, chip]
            remote(spot, spot, wp_ssem.at[number], wp_rsem.at[number], z, target * 2 + core).start()
            return carry

        lax.fori_loop(1, chips, pass_on, 0)
        pending.append(lambda number=number: await_bytes(w_rows.at[number, core, pl.ds(0, chips - 1)], wp_ssem.at[number]))

    def use_one(source, here):
        pre_one[here, :] += dot(j_one[source, here, :], w_one[source])

    def swap_weights():
        for number in range(2):
            spot = w_rows.at[number, core]
            await_bytes(w_rows.at[number, core, pl.ds(0, chips - 1)], wp_rsem.at[number])
            remote(spot, spot, ws_ssem.at[number], ws_rsem.at[number], z, sibling).start()
            pending.append(lambda spot=spot, number=number: await_bytes(spot, ws_ssem.at[number]))

    take_gather(j_one, chunks_one, rows_one, ag1_send, ag1_recv, use_one, swap_weights)
    hid_one[...] = (pre_one[...] * jax.nn.sigmoid(pre_one[...])).astype(BF16)
    for number in range(2):
        await_bytes(w_rows.at[number, 1 - core], ws_rsem.at[number])

    def rows_of(number, store):
        return w_rows[number, :, :, store].reshape(2 * width, width)

    def join(hidden, near, tile, joined):
        rows = near.shape[0]
        own = hidden[0:rows, :]
        mean = (own.astype(F32) + dot(tile[...], hidden[...])) / counted(near)
        joined[...] = jnp.concatenate([own, mean.astype(BF16)], axis=1)

    def send_partials(joined, number, part, got):
        for store, place in others:
            part[place] = dot(joined[...], rows_of(number, store)).astype(BF16)
            remote(
                part.at[place], got.at[place], rs_ssem.at[number, place], rs_rsem.at[number, place], store, t
            ).start()
            pending.append(lambda place=place: await_bytes(part.at[place], rs_ssem.at[number, place]))

    def take_partials(joined, number, got):
        total = dot(joined[...], rows_of(number, z))
        for place in range(3):
            await_bytes(got.at[place], rs_rsem.at[number, place])
            total = total + got[place].astype(F32)
        return total

    join(hid_one, near_two, tile_two, j_two)
    send_partials(j_two, 0, part_two, got_two)
    for store, place in others:
        await_bytes(cots.at[store], cot_rsem.at[place])
    spread = dot(cots[0], rows_of(1, 0), 1, 1)
    for store in range(1, stores):
        spread = spread + dot(cots[store], rows_of(1, store), 1, 1)
    below3[...] = spread_below(spread, near_three, tile_three)
    pre_two[...] = take_partials(j_two, 0, got_two)
    dpres[z] = (below3[...] * slope(pre_two[...])).astype(BF16)
    chunks_two = agd_send.shape[1]
    rows_two = mid // chunks_two
    for index in range(chunks_two):
        start_gather(dpres, index, rows_two, agd_send, agd_recv)
    hid_two[...] = (pre_two[...] * jax.nn.sigmoid(pre_two[...])).astype(BF16)
    join(hid_two, near_three, tile_three, j_three)

    height = full.shape[2]
    per_slice = width // height

    def pack(number):
        def body(index, carry):
            px_send[number, index] = full[number, index * 2 + 1 - core].astype(BF16)
            return carry

        lax.fori_loop(0, chips, body, 0)
        remote(
            px_send.at[number], px_recv.at[number], px_ssem.at[number], px_rsem.at[number], z, sibling
        ).start()
        pending.append(lambda: await_bytes(px_send.at[number], px_ssem.at[number]))

    def grad_of_columns(number, joined, dpre):
        def products(store, carry):
            part = dot(joined[store], dpre[...], 0, 0)
            for half in range(2):
                for index in range(per_slice):
                    start = half * width + index * height
                    full[number, half * (groups // 2) + store * per_slice + index] = part[start : start + height, :]
            return carry

        lax.fori_loop(0, stores, products, 0)
        pack(number)

    def grad_of_rows(number, joined, columns):
        def products(store, carry):
            part = dot(joined[...], columns[store], 0, 0)
            for index in range(2 * per_slice):
                full[number, index * stores + store] = part[index * height : (index + 1) * height, :]
            return carry

        lax.fori_loop(0, stores, products, 0)
        pack(number)

    def share_grad(number):
        await_bytes(px_recv.at[number], px_rsem.at[number])

        def body(index, carry):
            target = lax.rem(chip + index, chips)
            total = full[number, target * 2 + core] + px_recv[number, target].astype(F32)
            blk[number, target] = total.astype(BF16)

            @pl.when(index > 0)
            def _():
                remote(
                    blk.at[number, target], rr.at[number, chip],
                    rr_ssem.at[number], rr_rsem.at[number], z, target * 2 + core,
                ).start()

            @pl.when(index == 0)
            def _():
                rr[number, chip] = total.astype(BF16)

            return carry

        lax.fori_loop(0, chips, body, 0)
        pending.append(lambda: await_bytes(blk.at[number, pl.ds(0, chips - 1)], rr_ssem.at[number]))

    def summed(number):
        await_bytes(rr.at[number, pl.ds(0, chips - 1)], rr_rsem.at[number])
        return jnp.sum(rr[number].astype(F32), axis=0)

    block, to_store = t // stores, lax.rem(t, stores)
    to_trainer = jnp.where(
        block < per_slice, z * per_slice + block, groups // 2 + z * per_slice + block - per_slice
    )
    moves = jnp.logical_or(to_store != z, to_trainer != t)

    def move(number):
        move_send[number] = summed(number)
        sems = mv_ssem.at[number], mv_rsem.at[number]

        @pl.when(moves)
        def _():
            remote(move_send.at[number], move_recv.at[number], *sems, to_store, to_trainer).start()

        @pl.when(jnp.logical_not(moves))
        def _():
            pltpu.make_async_copy(move_send.at[number], move_recv.at[number], mv_rsem.at[number]).start()

        def leave():
            @pl.when(moves)
            def _():
                await_bytes(move_send.at[number], mv_ssem.at[number])

        pending.append(leave)

    def take_move(number, out):
        await_bytes(move_recv.at[number], mv_rsem.at[number])
        out[...] = move_recv[number]

    grad_of_rows(1, j_three, cots)
    spread_two[...] = dot(dpres[z], rows_of(0, z), 1, 1)

    def use_two(source, here):
        spread_two[here, :] += dot(dpres[source, here, :], rows_of(0, source), 1, 1)

    take_gather(dpres, chunks_two, rows_two, agd_send, agd_recv, use_two, lambda: share_grad(1))
    grad_of_rows(0, j_two, dpres)
    below2 = spread_below(spread_two[...], near_two, tile_two)
    dpre_one[...] = (below2 * slope(pre_one[...])).astype(BF16)
    share_grad(0)
    grad_of_columns(2, j_one, dpre_one)
    send_partials(j_three, 1, part_three, got_three)
    move(1)
    share_grad(2)
    emb_out[...] = take_partials(j_three, 1, got_three).astype(BF16)
    move(0)
    take_move(1, three_out)
    one_out[...] = summed(2)
    take_move(0, two_out)

    for leave in pending:
        leave()


def copies(*refs):
    half = len(refs) // 2
    for source, target in zip(refs[:half], refs[half:]):
        target[...] = source[...]


def run(
    stores, groups, features, sent_ids, block_sizes, self_ids, near_one, degree_one, near_two, degree_two,
    near_three, degree_three, weight_one, weight_two, weight_three, cotangent,
):
    slots = sent_ids.shape[2]
    outer, mid, seeds = near_one.shape[0], near_two.shape[0], near_three.shape[0]
    fan = near_one.shape[1]
    fwidth = features.shape[1]
    width = cotangent.shape[1]
    devices = stores * groups
    cells = devices * SLOT
    height = 2 * fwidth // groups

    vmem = pl.BlockSpec(memory_space=pltpu.VMEM)
    hbm = pl.BlockSpec(memory_space=pl.ANY)
    lanes = min(128, width)
    chunks_one, chunks_two = 4, 2
    dma = pltpu.SemaphoreType.DMA
    chips = groups // 2
    scratch = [pltpu.VMEM((rows, SLOT), jnp.int32) for rows in (outer, mid, seeds)]
    scratch += [
        pltpu.VMEM((groups * SLOT, lanes), F32),
        pltpu.VMEM(features.shape, BF16),
        pltpu.VMEM((groups * SLOT, features.shape[0]), BF16),
        pltpu.VMEM((stores, groups * SLOT, width), BF16),
        pltpu.VMEM((cells, width), BF16),
        pltpu.VMEM((cells, lanes), BF16),
        pltpu.VMEM((outer, cells), BF16),
        pltpu.VMEM((outer, cells), BF16),
        pltpu.VMEM((mid, outer), BF16),
        pltpu.VMEM((seeds, mid), BF16),
        pltpu.VMEM((stores, 2 * width, width), BF16),
        pltpu.VMEM((2, 2, chips, stores, width // chips, width), BF16),
        pltpu.VMEM((stores, outer, 2 * width), BF16),
        pltpu.VMEM((mid, 2 * width), BF16),
        pltpu.VMEM((seeds, 2 * width), BF16),
        pltpu.VMEM((outer, width), F32),
        pltpu.VMEM((mid, width), F32),
        pltpu.VMEM((outer, width), BF16),
        pltpu.VMEM((mid, width), BF16),
        pltpu.VMEM((stores, seeds, width), BF16),
        pltpu.VMEM((stores, mid, width), BF16),
        pltpu.VMEM((mid, 2 * width), F32),
        pltpu.VMEM((mid, width), F32),
        pltpu.VMEM((outer, width), BF16),
    ]
    scratch += [pltpu.VMEM((3, mid, width), BF16)] * 2 + [pltpu.VMEM((3, seeds, width), BF16)] * 2
    scratch += [pltpu.VMEM((3, groups, height, width), F32)]
    scratch += [pltpu.VMEM((3, chips, height, width), BF16)] * 4
    scratch += [pltpu.VMEM((2, height, width), F32)] * 2
    scratch += [dma((4 + 2 * stores,)), dma((stores,)), dma((stores,))]
    scratch += [dma((3, chunks)) for chunks in (chunks_one, chunks_one, chunks_two, chunks_two)]
    scratch += [dma((3,))] * 2 + [dma((2, 3))] * 2 + [dma((2,))] * 4 + [dma((2, 3))] * 2
    scratch += [dma((3,))] * 4 + [dma((2,))] * 2
    shapes = (
        jax.ShapeDtypeStruct((seeds, width), BF16),
        jax.ShapeDtypeStruct((height, width), F32),
        jax.ShapeDtypeStruct((height, width), F32),
        jax.ShapeDtypeStruct((height, width), F32),
    )
    results = pl.pallas_call(
        functools.partial(kernel, stores, groups, slots),
        out_shape=shapes,
        in_specs=[vmem] * 10 + [hbm] * 4,
        out_specs=(vmem,) * 4,
        scratch_shapes=scratch,
        compiler_params=pltpu.CompilerParams(
            collective_id=0, has_side_effects=True, vmem_limit_bytes=60 * 1024 * 1024
        ),
    )(
        jnp.transpose(sent_ids, (2, 0, 1)), block_sizes, self_ids,
        near_one.T, degree_one, near_two.T, degree_two, near_three.T, degree_three,
        cotangent, features, weight_one, weight_two, weight_three,
    )
    return pl.pallas_call(copies, out_shape=shapes, in_specs=[vmem] * 4, out_specs=(vmem,) * 4)(*results)


def solution(mesh):
    stores, groups = mesh.shape["store"], mesh.shape["trainer"]
    both = ("store", "trainer")
    placed = (
        P(both, None), P(both, None, None), P(both, None), P("trainer"), P("trainer", None), P("trainer"),
        P("trainer", None), P("trainer"), P("trainer", None), P("trainer"),
        P(None, "store"), P(None, "store"), P(None, "store"), P("trainer", "store"),
    )
    return jax.shard_map(
        functools.partial(run, stores, groups),
        mesh=mesh, in_specs=placed, out_specs=(P("trainer", "store"),) * 4, check_vma=False,
    )
```

```python
import functools
import math

import jax
import jax.numpy as jnp
from jax import lax
from jax.experimental import pallas as pl
from jax.experimental.pallas import tpu as pltpu
from jax.sharding import PartitionSpec as P

MESH = pl.DeviceIdType.MESH
F32 = jnp.float32
BF16 = jnp.bfloat16
SLOT = 16


def dot(a, b, left=1, right=0):
    return lax.dot_general(a, b, (((left,), (right,)), ((), ())), preferred_element_type=F32)


def slope(preact):
    sigma = jax.nn.sigmoid(preact)
    return sigma * (1.0 + preact * (1.0 - sigma))


def rows_at(index, size):
    return pl.ds(pl.multiple_of(index * size, size), size)


def step_of(rows, most):
    size = min(rows, most)
    while rows % size:
        size -= 1
    return size


def count_matches(ids, column_list, dst, rows, width):
    high = step_of(rows, 16)
    wide = step_of(width, 1024)

    def body(index, carry):
        part = ids[rows_at(index, high), :]
        for start in range(0, width, wide):
            place = lax.broadcasted_iota(jnp.int32, (high, wide), 1) + start
            total = jnp.zeros((high, wide), F32)
            for column in column_list:
                total = total + jnp.where(part[:, column : column + 1] == place, 1.0, 0.0)
            dst[rows_at(index, high), start : start + wide] = total.astype(BF16)
        return carry

    lax.fori_loop(0, rows // high, body, 0)


def kernel(
    stores, groups, slots,
    sent, sizes, self_ids, near_one_t, degree_one, near_two_t, degree_two, near_three_t, degree_three,
    cot, feat_hbm, one_hbm, two_hbm, three_hbm,
    emb_out, one_out, two_out, three_out,
    near_one, near_two, near_three, extra, feat, hot, picked, arrived, filled,
    tile_one, tile_self, tile_two, tile_three, w_one, w_rows,
    j_one, j_two, j_three, pre_one, pre_two, hid_one, hid_two, cots, dpres, spread_two, below3, dpre_one,
    part_two, got_two, part_three, got_three,
    full, px_send, px_recv, blk, rr, line, thin, last, move_send, move_recv,
    load_sem, in_send, in_recv, ag1_send, ag1_recv, agd_send, agd_recv,
    cot_ssem, cot_rsem, wz_ssem, wz_rsem, wp_ssem, wp_rsem, ws_ssem, ws_rsem,
    rs_ssem, rs_rsem, px_ssem, px_rsem, rr_ssem, rr_rsem, ls_ssem, ls_rsem, mv_ssem, mv_rsem,
):
    devices = stores * groups
    z = lax.axis_index("store")
    t = lax.axis_index("trainer")
    me = z * groups + t
    chip, core = t // 2, lax.rem(t, 2)
    chips = groups // 2
    sibling = t + 1 - 2 * core
    right, left, across = (lax.rem(z + k, stores) for k in (1, 3, 2))
    others = ((across, 2), (right, 0), (left, 1))
    width = cot.shape[1]
    seeds, mid, outer = cot.shape[0], near_two.shape[0], near_one.shape[0]
    cells = devices * SLOT
    fan = near_two_t.shape[0]
    pending = []

    def remote(src, dst, send_sem, recv_sem, store, trainer):
        return pltpu.make_async_remote_copy(
            src_ref=src, dst_ref=dst, send_sem=send_sem, recv_sem=recv_sem,
            device_id=(store, trainer), device_id_type=MESH,
        )

    def await_bytes(ref, sem):
        pltpu.make_async_copy(ref, ref, sem).wait()

    barrier = pltpu.get_barrier_semaphore()

    def greet(index, carry):
        other = lax.rem(me + index, devices)
        pl.semaphore_signal(
            barrier, inc=1, device_id=(other // groups, lax.rem(other, groups)), device_id_type=MESH
        )
        return carry

    lax.fori_loop(1, devices, greet, 0)

    share = w_rows.shape[4]

    def piece_of(hbm, store):
        return hbm.at[pl.ds(pl.multiple_of(core * stores * width + store * width + chip * share, share), share), :]

    loads = [pltpu.make_async_copy(feat_hbm, feat, load_sem.at[0])]
    for place, hbm in enumerate((two_hbm, three_hbm)):
        loads.append(pltpu.make_async_copy(piece_of(hbm, z), w_rows.at[place, core, chip, z], load_sem.at[1 + place]))
    loads.append(pltpu.make_async_copy(cot, cots.at[z], load_sem.at[3]))
    for store in range(stores):
        for half in range(2):
            loads.append(
                pltpu.make_async_copy(
                    one_hbm.at[pl.ds((half * stores + store) * width, width), :],
                    w_one.at[store, pl.ds(half * width, width), :],
                    load_sem.at[4 + store * 2 + half],
                )
            )
    for load in loads:
        load.start()

    slot = lax.broadcasted_iota(jnp.int32, (SLOT, groups), 0)
    amounts = jnp.broadcast_to(sizes[...], (SLOT, groups))
    wanted = jnp.concatenate([sent[index] for index in range(slots)] + [jnp.full((SLOT - slots, groups), -1, jnp.int32)], axis=0)
    wanted = jnp.where(slot < amounts, wanted, -1)
    notes = jnp.where(slot == slots, amounts, 0).astype(F32)
    wide = step_of(feat.shape[0], 1024)
    for group in range(groups):
        here = pl.ds(group * SLOT, SLOT)
        extra[here, :] = jnp.broadcast_to(notes[:, group : group + 1], (SLOT, extra.shape[1]))
        for start in range(0, feat.shape[0], wide):
            place = lax.broadcasted_iota(jnp.int32, (SLOT, wide), 1) + start
            hot[here, start : start + wide] = jnp.where(wanted[:, group : group + 1] == place, 1.0, 0.0).astype(BF16)
    loads[0].wait()
    pl.semaphore_wait(barrier, devices - 1)

    for store, place in others:
        remote(cot, cots.at[z], cot_ssem.at[place], cot_rsem.at[place], store, t).start()
        pending.append(lambda place=place: await_bytes(cot, cot_ssem.at[place]))
        for number, hbm in enumerate((two_hbm, three_hbm)):
            spot = w_rows.at[number, core, chip, z]
            remote(piece_of(hbm, store), spot, wz_ssem.at[number, place], wz_rsem.at[number, place], store, t).start()
            pending.append(lambda number=number, place=place, spot=spot: await_bytes(spot, wz_ssem.at[number, place]))

    def fetch(index, carry):
        store = lax.rem(z + index, stores)
        columns = pl.ds(pl.multiple_of(store * width, width), width)
        rows = step_of(groups * SLOT, 256)
        for start in range(0, groups * SLOT, rows):
            part = dot(hot[start : start + rows, :], feat[:, columns])
            counts = jnp.concatenate([extra[start : start + rows, :]] * (width // extra.shape[1]), axis=1)
            picked[store, start : start + rows, :] = (part + counts).astype(BF16)

        def send(number, inner):
            trainer = lax.rem(t + number * 13, groups)

            @pl.when(jnp.logical_or(store != z, trainer != t))
            def _():
                remote(
                    picked.at[store, rows_at(trainer, SLOT), :], arrived.at[rows_at(me, SLOT), :],
                    in_send.at[store], in_recv.at[z], store, trainer,
                ).start()

            return inner

        lax.fori_loop(0, groups, send, 0)
        return carry

    lax.fori_loop(0, stores, fetch, 0)
    own_block = pltpu.make_async_copy(
        picked.at[z, rows_at(t, SLOT), :], arrived.at[rows_at(me, SLOT), :], in_recv.at[z]
    )
    own_block.start()

    def leave_blocks():
        for index in range(stores):
            store = lax.rem(z + index, stores)
            amount = groups - (1 if index == 0 else 0)
            await_bytes(picked.at[store, pl.ds(0, amount * SLOT), :], in_send.at[store])

    pending.append(leave_blocks)
    for load in loads[1:]:
        load.wait()

    def moved(index):
        return index + (SLOT - slots) * ((index * ((1 << 19) // slots + 1)) >> 19)

    def upright(near, degree, own, dst):
        rows = near.shape[1]
        place = lax.broadcasted_iota(jnp.int32, (fan, rows), 0)
        parts = [jnp.where(place < degree[...][None, :], near, -1)] + own
        parts.append(jnp.full((SLOT - fan - len(own), rows), -1, jnp.int32))
        dst[...] = jnp.concatenate(parts, axis=0).T

    upright(moved(near_one_t[...]), degree_one, [moved(self_ids[...][None, :])], near_one)
    upright(near_two_t[...], degree_two, [], near_two)
    upright(near_three_t[...], degree_three, [], near_three)
    count_matches(near_one, list(range(fan)), tile_one, outer, cells)
    count_matches(near_one, [fan], tile_self, outer, cells)
    count_matches(near_two, list(range(fan)), tile_two, mid, outer)
    count_matches(near_three, list(range(fan)), tile_three, seeds, mid)

    def counted(near):
        return 1.0 + jnp.sum(jnp.where(near[...] >= 0, 1.0, 0.0), axis=1, keepdims=True)

    def spread_below(total, near, tile):
        rows = near.shape[0]
        scaled = (total[:, width:] / counted(near)).astype(BF16)
        below = dot(tile[...], scaled, 0, 0)
        upper = below[:rows] + (total[:, :width] + scaled.astype(F32))
        return jnp.concatenate([upper, below[rows:]], axis=0)

    def start_gather(held, index, rows, send_sem, recv_sem):
        piece = held.at[z, rows_at(index, rows), :]
        remote(piece, piece, send_sem.at[0, index], recv_sem.at[0, index], right, t).start()
        remote(piece, piece, send_sem.at[1, index], recv_sem.at[1, index], left, t).start()

    def take_gather(held, chunks, rows, send_sem, recv_sem, use, between):
        for index in range(chunks):
            here = rows_at(index, rows)
            for side, (source, onward) in enumerate(((left, right), (right, left))):
                piece = held.at[source, here, :]
                await_bytes(piece, recv_sem.at[side, index])
                if index % 2 == side:
                    remote(piece, piece, send_sem.at[2, index], recv_sem.at[2, index], onward, t).start()
            for source in (left, right):
                use(source, here)
        between()
        for index in range(chunks):
            here = rows_at(index, rows)
            await_bytes(held.at[across, here, :], recv_sem.at[2, index])
            use(across, here)
        for way in range(3):
            for index in range(chunks):
                pending.append(
                    lambda way=way, here=rows_at(index, rows), index=index: await_bytes(
                        held.at[z, here, :], send_sem.at[way, index]
                    )
                )

    def mark(index, carry):
        here = rows_at(index, SLOT)
        block = arrived[here, 0 : filled.shape[1]].astype(F32)
        place = lax.broadcasted_iota(jnp.int32, block.shape, 0).astype(F32)
        filled[here, :] = jnp.where(place < block[slots : slots + 1, :], 1.0, 0.0).astype(BF16)
        return carry

    for store in range(stores):
        await_bytes(arrived.at[pl.ds(store * groups * SLOT, groups * SLOT), :], in_recv.at[store])
        lax.fori_loop(store * groups, (store + 1) * groups, mark, 0)

    chunks_one = ag1_send.shape[1]
    rows_one = outer // chunks_one

    def layer_one(index, carry):
        here = rows_at(index, rows_one)
        own = dot(tile_self[here, :], arrived[...])
        valid = 1.0 + dot(tile_one[here, :], filled[...])
        valid = jnp.concatenate([valid] * (width // valid.shape[1]), axis=1)
        mean = (own + dot(tile_one[here, :], arrived[...])) / valid
        j_one[z, here, :] = jnp.concatenate([own, mean], axis=1).astype(BF16)
        start_gather(j_one, index, rows_one, ag1_send, ag1_recv)
        pre_one[here, :] = dot(j_one[z, here, :], w_one[z])
        return carry

    lax.fori_loop(0, chunks_one, layer_one, 0)

    for number in range(2):
        for store, place in others:
            await_bytes(w_rows.at[number, core, chip, store], wz_rsem.at[number, place])

        def pass_on(index, carry, number=number):
            target = lax.rem(chip + index, chips)
            spot = w_rows.at[number, core, chip]
            remote(spot, spot, wp_ssem.at[number], wp_rsem.at[number], z, target * 2 + core).start()
            return carry

        lax.fori_loop(1, chips, pass_on, 0)
        pending.append(lambda number=number: await_bytes(w_rows.at[number, core, pl.ds(0, chips - 1)], wp_ssem.at[number]))

    def use_one(source, here):
        pre_one[here, :] += dot(j_one[source, here, :], w_one[source])

    def swap_weights():
        for number in range(2):
            spot = w_rows.at[number, core]
            await_bytes(w_rows.at[number, core, pl.ds(0, chips - 1)], wp_rsem.at[number])
            remote(spot, spot, ws_ssem.at[number], ws_rsem.at[number], z, sibling).start()
            pending.append(lambda spot=spot, number=number: await_bytes(spot, ws_ssem.at[number]))

    take_gather(j_one, chunks_one, rows_one, ag1_send, ag1_recv, use_one, swap_weights)
    hid_one[...] = (pre_one[...] * jax.nn.sigmoid(pre_one[...])).astype(BF16)
    for number in range(2):
        await_bytes(w_rows.at[number, 1 - core], ws_rsem.at[number])

    def rows_of(number, store):
        return w_rows[number, :, :, store].reshape(2 * width, width)

    def join(hidden, near, tile, joined):
        rows = near.shape[0]
        own = hidden[0:rows, :]
        mean = (own.astype(F32) + dot(tile[...], hidden[...])) / counted(near)
        joined[...] = jnp.concatenate([own, mean.astype(BF16)], axis=1)

    def send_partials(joined, number, part, got, chunks):
        rows = part.shape[1] // chunks
        for index in range(chunks):
            here = pl.ds(index * rows, rows)
            for store, place in others:
                part[place, here, :] = dot(joined[here, :], rows_of(number, store)).astype(BF16)
                sems = rs_ssem.at[number, index, place], rs_rsem.at[number, index, place]
                remote(part.at[place, here, :], got.at[place, here, :], *sems, store, t).start()
                pending.append(lambda place=place, here=here, sem=sems[0]: await_bytes(part.at[place, here, :], sem))

    def take_partials(joined, number, got, index, rows):
        here = pl.ds(index * rows, rows)
        total = dot(joined[here, :], rows_of(number, z))
        for place in range(3):
            await_bytes(got.at[place, here, :], rs_rsem.at[number, index, place])
            total = total + got[place, here, :].astype(F32)
        return total

    join(hid_one, near_two, tile_two, j_two)
    chunks_two = agd_send.shape[1]
    rows_two = mid // chunks_two
    send_partials(j_two, 0, part_two, got_two, chunks_two)
    for store, place in others:
        await_bytes(cots.at[store], cot_rsem.at[place])
    spread = dot(cots[0], rows_of(1, 0), 1, 1)
    for store in range(1, stores):
        spread = spread + dot(cots[store], rows_of(1, store), 1, 1)
    below3[...] = spread_below(spread, near_three, tile_three)
    for index in range(chunks_two):
        here = rows_at(index, rows_two)
        pre_two[here, :] = take_partials(j_two, 0, got_two, index, rows_two)
        dpres[z, here, :] = (below3[here, :] * slope(pre_two[here, :])).astype(BF16)
        start_gather(dpres, index, rows_two, agd_send, agd_recv)
    hid_two[...] = (pre_two[...] * jax.nn.sigmoid(pre_two[...])).astype(BF16)
    join(hid_two, near_three, tile_three, j_three)

    height = full.shape[2]
    per_slice = width // height

    def pack(number):
        def body(index, carry):
            px_send[number, index] = full[number, index * 2 + 1 - core].astype(BF16)
            return carry

        lax.fori_loop(0, chips, body, 0)
        remote(
            px_send.at[number], px_recv.at[number], px_ssem.at[number], px_rsem.at[number], z, sibling
        ).start()
        pending.append(lambda: await_bytes(px_send.at[number], px_ssem.at[number]))

    def grad_of_columns(number, joined, dpre):
        def products(store, carry):
            part = dot(joined[store], dpre[...], 0, 0)
            for half in range(2):
                for index in range(per_slice):
                    start = half * width + index * height
                    full[number, half * (groups // 2) + store * per_slice + index] = part[start : start + height, :]
            return carry

        lax.fori_loop(0, stores, products, 0)
        pack(number)

    def grad_of_rows(number, joined, columns):
        def products(store, carry):
            part = dot(joined[...], columns[store], 0, 0)
            for index in range(2 * per_slice):
                full[number, index * stores + store] = part[index * height : (index + 1) * height, :]
            return carry

        lax.fori_loop(0, stores, products, 0)
        pack(number)

    side = rr.shape[2]
    place_x, place_y = chip // side, lax.rem(chip, side)
    spots = (place_x, place_y)

    def partner(way, index):
        target = lax.rem(spots[way] + index, side)
        column = (target, place_y) if way == 0 else (place_x, target)
        return target, (column[0] * side + column[1]) * 2 + core

    def share_first(number):
        await_bytes(px_recv.at[number], px_rsem.at[number])

        def body(index, carry):
            total = full[number, index * 2 + core] + px_recv[number, index].astype(F32)
            first, second = index // side, lax.rem(index, side)
            blk[number, 0, first, second] = total[: height // 2].astype(BF16)
            blk[number, 1, second, first] = total[height // 2 :].astype(BF16)
            return carry

        lax.fori_loop(0, chips, body, 0)
        for way in range(2):
            for index in range(1, side):
                target, trainer = partner(way, index)
                remote(
                    blk.at[number, way, target], rr.at[number, way, index],
                    rr_ssem.at[number, way, index], rr_rsem.at[number, way, index], z, trainer,
                ).start()
                pending.append(
                    lambda way=way, index=index, target=target: await_bytes(
                        blk.at[number, way, target], rr_ssem.at[number, way, index]
                    )
                )

    def share_second(number):
        for way in range(2):
            total = blk[number, way, spots[way]].astype(F32)
            for index in range(1, side):
                await_bytes(rr.at[number, way, index], rr_rsem.at[number, way, index])
                total = total + rr[number, way, index].astype(F32)
            line[number, way] = total
            thin[number, way] = total.astype(BF16)
            for index in range(1, side):
                target, trainer = partner(1 - way, index)
                remote(
                    thin.at[number, way, target], last.at[number, way, index],
                    ls_ssem.at[number, way, index], ls_rsem.at[number, way, index], z, trainer,
                ).start()
                pending.append(
                    lambda way=way, index=index, target=target: await_bytes(
                        thin.at[number, way, target], ls_ssem.at[number, way, index]
                    )
                )

    def summed(number):
        halves = []
        for way in range(2):
            total = line[number, way, spots[1 - way]]
            for index in range(1, side):
                await_bytes(last.at[number, way, index], ls_rsem.at[number, way, index])
                total = total + last[number, way, index].astype(F32)
            halves.append(total)
        return jnp.concatenate(halves, axis=0)

    block, to_store = t // stores, lax.rem(t, stores)
    to_trainer = jnp.where(
        block < per_slice, z * per_slice + block, groups // 2 + z * per_slice + block - per_slice
    )
    moves = jnp.logical_or(to_store != z, to_trainer != t)

    def move(number):
        move_send[number] = summed(number).astype(BF16)
        sems = mv_ssem.at[number], mv_rsem.at[number]

        @pl.when(moves)
        def _():
            remote(move_send.at[number], move_recv.at[number], *sems, to_store, to_trainer).start()

        @pl.when(jnp.logical_not(moves))
        def _():
            pltpu.make_async_copy(move_send.at[number], move_recv.at[number], mv_rsem.at[number]).start()

        def leave():
            @pl.when(moves)
            def _():
                await_bytes(move_send.at[number], mv_ssem.at[number])

        pending.append(leave)

    def take_move(number, out):
        await_bytes(move_recv.at[number], mv_rsem.at[number])
        out[...] = move_recv[number].astype(F32)

    grad_of_rows(1, j_three, cots)
    spread_two[...] = dot(dpres[z], rows_of(0, z), 1, 1)

    def use_two(source, here):
        spread_two[here, :] += dot(dpres[source, here, :], rows_of(0, source), 1, 1)

    take_gather(dpres, chunks_two, rows_two, agd_send, agd_recv, use_two, lambda: share_first(1))
    send_partials(j_three, 1, part_three, got_three, 1)
    grad_of_rows(0, j_two, dpres)
    below2 = spread_below(spread_two[...], near_two, tile_two)
    dpre_one[...] = (below2 * slope(pre_one[...])).astype(BF16)
    share_first(0)
    grad_of_columns(2, j_one, dpre_one)
    share_second(1)
    share_first(2)
    share_second(0)
    move(1)
    move(0)
    share_second(2)
    take_move(1, three_out)
    take_move(0, two_out)
    emb_out[...] = take_partials(j_three, 1, got_three, 0, seeds).astype(BF16)
    one_out[...] = summed(2)

    for leave in pending:
        leave()


def copies(*refs):
    half = len(refs) // 2
    for source, target in zip(refs[:half], refs[half:]):
        target[...] = source[...]


def run(
    stores, groups, features, sent_ids, block_sizes, self_ids, near_one, degree_one, near_two, degree_two,
    near_three, degree_three, weight_one, weight_two, weight_three, cotangent,
):
    slots = sent_ids.shape[2]
    outer, mid, seeds = near_one.shape[0], near_two.shape[0], near_three.shape[0]
    fan = near_one.shape[1]
    fwidth = features.shape[1]
    width = cotangent.shape[1]
    devices = stores * groups
    cells = devices * SLOT
    height = 2 * fwidth // groups

    vmem = pl.BlockSpec(memory_space=pltpu.VMEM)
    hbm = pl.BlockSpec(memory_space=pl.ANY)
    lanes = min(128, width)
    chunks_one, chunks_two = 4, 2
    dma = pltpu.SemaphoreType.DMA
    chips = groups // 2
    side = math.isqrt(chips)
    scratch = [pltpu.VMEM((rows, SLOT), jnp.int32) for rows in (outer, mid, seeds)]
    scratch += [
        pltpu.VMEM((groups * SLOT, lanes), F32),
        pltpu.VMEM(features.shape, BF16),
        pltpu.VMEM((groups * SLOT, features.shape[0]), BF16),
        pltpu.VMEM((stores, groups * SLOT, width), BF16),
        pltpu.VMEM((cells, width), BF16),
        pltpu.VMEM((cells, lanes), BF16),
        pltpu.VMEM((outer, cells), BF16),
        pltpu.VMEM((outer, cells), BF16),
        pltpu.VMEM((mid, outer), BF16),
        pltpu.VMEM((seeds, mid), BF16),
        pltpu.VMEM((stores, 2 * width, width), BF16),
        pltpu.VMEM((2, 2, chips, stores, width // chips, width), BF16),
        pltpu.VMEM((stores, outer, 2 * width), BF16),
        pltpu.VMEM((mid, 2 * width), BF16),
        pltpu.VMEM((seeds, 2 * width), BF16),
        pltpu.VMEM((outer, width), F32),
        pltpu.VMEM((mid, width), F32),
        pltpu.VMEM((outer, width), BF16),
        pltpu.VMEM((mid, width), BF16),
        pltpu.VMEM((stores, seeds, width), BF16),
        pltpu.VMEM((stores, mid, width), BF16),
        pltpu.VMEM((mid, 2 * width), F32),
        pltpu.VMEM((mid, width), F32),
        pltpu.VMEM((outer, width), BF16),
    ]
    scratch += [pltpu.VMEM((3, mid, width), BF16)] * 2 + [pltpu.VMEM((3, seeds, width), BF16)] * 2
    scratch += [pltpu.VMEM((3, groups, height, width), F32)]
    scratch += [pltpu.VMEM((3, chips, height, width), BF16)] * 2
    scratch += [pltpu.VMEM((3, 2, side, side, height // 2, width), BF16)] * 2
    scratch += [pltpu.VMEM((3, 2, side, height // 2, width), kind) for kind in (F32, BF16, BF16)]
    scratch += [pltpu.VMEM((2, height, width), BF16)] * 2
    scratch += [dma((4 + 2 * stores,)), dma((stores,)), dma((stores,))]
    scratch += [dma((3, chunks)) for chunks in (chunks_one, chunks_one, chunks_two, chunks_two)]
    scratch += [dma((3,))] * 2 + [dma((2, 3))] * 2 + [dma((2,))] * 4 + [dma((2, chunks_two, 3))] * 2
    scratch += [dma((3,))] * 2 + [dma((3, 2, side))] * 4 + [dma((2,))] * 2
    shapes = (
        jax.ShapeDtypeStruct((seeds, width), BF16),
        jax.ShapeDtypeStruct((height, width), F32),
        jax.ShapeDtypeStruct((height, width), F32),
        jax.ShapeDtypeStruct((height, width), F32),
    )
    results = pl.pallas_call(
        functools.partial(kernel, stores, groups, slots),
        out_shape=shapes,
        in_specs=[vmem] * 10 + [hbm] * 4,
        out_specs=(vmem,) * 4,
        scratch_shapes=scratch,
        compiler_params=pltpu.CompilerParams(
            collective_id=0, has_side_effects=True, vmem_limit_bytes=60 * 1024 * 1024
        ),
    )(
        jnp.transpose(sent_ids, (2, 0, 1)), block_sizes, self_ids,
        near_one.T, degree_one, near_two.T, degree_two, near_three.T, degree_three,
        cotangent, features, weight_one, weight_two, weight_three,
    )
    return pl.pallas_call(copies, out_shape=shapes, in_specs=[vmem] * 4, out_specs=(vmem,) * 4)(*results)


def solution(mesh):
    stores, groups = mesh.shape["store"], mesh.shape["trainer"]
    both = ("store", "trainer")
    placed = (
        P(both, None), P(both, None, None), P(both, None), P("trainer"), P("trainer", None), P("trainer"),
        P("trainer", None), P("trainer"), P("trainer", None), P("trainer"),
        P(None, "store"), P(None, "store"), P(None, "store"), P("trainer", "store"),
    )
    return jax.shard_map(
        functools.partial(run, stores, groups),
        mesh=mesh, in_specs=placed, out_specs=(P("trainer", "store"),) * 4, check_vma=False,
    )
```

```python
import functools
import math

import jax
import jax.numpy as jnp
from jax import lax
from jax.experimental import pallas as pl
from jax.experimental.pallas import tpu as pltpu
from jax.sharding import PartitionSpec as P

MESH = pl.DeviceIdType.MESH
F32 = jnp.float32
BF16 = jnp.bfloat16
SLOT = 16


def dot(a, b, left=1, right=0):
    return lax.dot_general(a, b, (((left,), (right,)), ((), ())), preferred_element_type=F32)


def slope(preact):
    sigma = jax.nn.sigmoid(preact)
    return sigma * (1.0 + preact * (1.0 - sigma))


def rows_at(index, size):
    return pl.ds(pl.multiple_of(index * size, size), size)


def step_of(rows, most):
    size = min(rows, most)
    while rows % size:
        size -= 1
    return size


def count_matches(ids, wanted, rows, width):
    high = step_of(rows, 128)
    wide = step_of(width, 256)

    def body(index, carry):
        here = rows_at(index, high)
        part = ids[here, :].astype(jnp.int16)
        for start in range(0, width, wide):
            place = (lax.broadcasted_iota(jnp.int32, (high, wide), 1) + start).astype(jnp.int16)
            for column_list, dst in wanted:
                total = None
                for column in column_list:
                    found = jnp.where(part[:, column : column + 1] == place, BF16(1), BF16(0))
                    total = found if total is None else total + found
                dst[here, start : start + wide] = total
        return carry

    lax.fori_loop(0, rows // high, body, 0)


def kernel(
    stores, groups, slots,
    sent, sizes, self_ids, near_one_t, degree_one, near_two_t, degree_two, near_three_t, degree_three,
    cot, feat_hbm, one_hbm, two_hbm, three_hbm,
    emb_out, one_out, two_out, three_out,
    near_one, near_two, near_three, asked, extra, feat, hot, picked, landed, dense, inputs, fills, filled, valid, sums,
    tile_one, tile_self, tile_two, tile_three, w_one, w_rows,
    j_one, j_two, j_three, pre_one, pre_two, hid_one, hid_two, cots, dpres, spread_two, below3, dpre_one,
    part_two, got_two, part_three, got_three,
    full, px_send, px_recv, blk, rr, line, thin, last, move_send, move_recv,
    load_sem, in_send, in_recv, cn_ssem, cn_rsem, ag1_send, ag1_recv, agd_send, agd_recv,
    cot_ssem, cot_rsem, wz_ssem, wz_rsem, wp_ssem, wp_rsem, ws_ssem, ws_rsem,
    rs_ssem, rs_rsem, px_ssem, px_rsem, rr_ssem, rr_rsem, ls_ssem, ls_rsem, mv_ssem, mv_rsem,
):
    devices = stores * groups
    z = lax.axis_index("store")
    t = lax.axis_index("trainer")
    me = z * groups + t
    chip, core = t // 2, lax.rem(t, 2)
    chips = groups // 2
    sibling = t + 1 - 2 * core
    right, left, across = (lax.rem(z + k, stores) for k in (1, 3, 2))
    others = ((across, 2), (right, 0), (left, 1))
    width = cot.shape[1]
    seeds, mid, outer = cot.shape[0], near_two.shape[0], near_one.shape[0]
    kept = groups * slots
    cells = stores * kept
    fan = near_two_t.shape[0]
    pending = []

    def remote(src, dst, send_sem, recv_sem, store, trainer):
        return pltpu.make_async_remote_copy(
            src_ref=src, dst_ref=dst, send_sem=send_sem, recv_sem=recv_sem,
            device_id=(store, trainer), device_id_type=MESH,
        )

    def await_bytes(ref, sem):
        pltpu.make_async_copy(ref, ref, sem).wait()

    barrier = pltpu.get_barrier_semaphore()

    def greet(index, carry):
        other = lax.rem(me + index, devices)
        pl.semaphore_signal(
            barrier, inc=1, device_id=(other // groups, lax.rem(other, groups)), device_id_type=MESH
        )
        return carry

    lax.fori_loop(1, devices, greet, 0)

    share = w_rows.shape[4]

    def piece_of(hbm, store):
        return hbm.at[pl.ds(pl.multiple_of(core * stores * width + store * width + chip * share, share), share), :]

    loads = [pltpu.make_async_copy(feat_hbm, feat, load_sem.at[0])]
    for place, hbm in enumerate((two_hbm, three_hbm)):
        loads.append(pltpu.make_async_copy(piece_of(hbm, z), w_rows.at[place, core, chip, z], load_sem.at[1 + place]))
    loads.append(pltpu.make_async_copy(cot, cots.at[z], load_sem.at[3]))
    for store in range(stores):
        for half in range(2):
            loads.append(
                pltpu.make_async_copy(
                    one_hbm.at[pl.ds((half * stores + store) * width, width), :],
                    w_one.at[store, pl.ds(half * width, width), :],
                    load_sem.at[4 + store * 2 + half],
                )
            )
    for load in loads:
        load.start()

    slot = lax.broadcasted_iota(jnp.int32, (SLOT, groups), 0)
    amounts = jnp.broadcast_to(sizes[...], (SLOT, groups))
    wanted = jnp.concatenate([sent[index] for index in range(slots)] + [jnp.full((SLOT - slots, groups), -1, jnp.int32)], axis=0)
    wanted = jnp.where(slot < amounts, wanted, -1)
    notes = jnp.where(slot == slots, amounts, 0).astype(F32)
    for group in range(groups):
        here = pl.ds(group * SLOT, SLOT)
        extra[here, :] = jnp.broadcast_to(notes[:, group : group + 1], (SLOT, extra.shape[1]))
        asked[here, :] = jnp.broadcast_to(wanted[:, group : group + 1], (SLOT, SLOT))
    count_matches(asked, [([0], hot)], groups * SLOT, feat.shape[0])
    loads[0].wait()
    pl.semaphore_wait(barrier, devices - 1)

    for store, place in others:
        remote(cot, cots.at[z], cot_ssem.at[place], cot_rsem.at[place], store, t).start()
        pending.append(lambda place=place: await_bytes(cot, cot_ssem.at[place]))
        for number, hbm in enumerate((two_hbm, three_hbm)):
            spot = w_rows.at[number, core, chip, z]
            remote(piece_of(hbm, store), spot, wz_ssem.at[number, place], wz_rsem.at[number, place], store, t).start()
            pending.append(lambda number=number, place=place, spot=spot: await_bytes(spot, wz_ssem.at[number, place]))

    def fetch(quarter, carry):
        columns = pl.ds(pl.multiple_of(quarter * width, width), width)
        rows = step_of(groups * SLOT, 256)
        for start in range(0, groups * SLOT, rows):
            part = dot(hot[start : start + rows, :], feat[:, columns])
            counts = jnp.concatenate([extra[start : start + rows, :]] * (width // extra.shape[1]), axis=1)
            picked[quarter, start : start + rows, :] = (part + counts).astype(BF16)

        def send(number, inner):
            trainer = lax.rem(t + number * 13, groups)
            remote(
                picked.at[quarter, rows_at(trainer, SLOT), :], landed.at[quarter, rows_at(t, SLOT), :],
                in_send.at[quarter], in_recv.at[quarter], z, trainer,
            ).start()
            return inner

        lax.fori_loop(1, groups, send, 0)
        pltpu.make_async_copy(
            picked.at[quarter, rows_at(t, SLOT), :], landed.at[quarter, rows_at(t, SLOT), :], in_recv.at[quarter]
        ).start()
        return carry

    lax.fori_loop(0, stores, fetch, 0)

    def leave_blocks():
        for quarter in range(stores):
            await_bytes(picked.at[quarter, pl.ds(0, (groups - 1) * SLOT), :], in_send.at[quarter])

    pending.append(leave_blocks)

    def moved(index):
        return index + (SLOT - slots) * ((index * ((1 << 19) // slots + 1)) >> 19)

    from_row = moved(lax.broadcasted_iota(jnp.int32, (kept, 1), 0))
    place = lax.broadcasted_iota(jnp.int32, (kept, groups * SLOT), 1)
    dense[...] = jnp.where(from_row == place, 1.0, 0.0).astype(BF16)
    ring_one = lambda source, index: inputs.at[index, pl.ds(pl.multiple_of(source * kept, kept), kept), :]

    def start_gather(piece_at, index, send_sem, recv_sem):
        piece = piece_at(z, index)
        remote(piece, piece, send_sem.at[0, index], recv_sem.at[0, index], right, t).start()
        remote(piece, piece, send_sem.at[1, index], recv_sem.at[1, index], left, t).start()

    def take_gather(piece_at, chunks, send_sem, recv_sem, near, far, between):
        for index in range(chunks):
            for side_at, (source, onward) in enumerate(((left, right), (right, left))):
                piece = piece_at(source, index)
                await_bytes(piece, recv_sem.at[side_at, index])
                if index % 2 == side_at:
                    remote(piece, piece, send_sem.at[2, index], recv_sem.at[2, index], onward, t).start()
            near(index)
        between()
        for index in range(chunks):
            await_bytes(piece_at(across, index), recv_sem.at[2, index])
            far(index)
        for way in range(3):
            for index in range(chunks):
                pending.append(
                    lambda way=way, index=index: await_bytes(piece_at(z, index), send_sem.at[way, index])
                )

    def pass_inputs(quarter):
        await_bytes(landed.at[quarter], in_recv.at[quarter])
        inputs[quarter, pl.ds(pl.multiple_of(z * kept, kept), kept), :] = dot(dense[...], landed[quarter]).astype(BF16)
        start_gather(ring_one, quarter, ag1_send, ag1_recv)

    pass_inputs(0)
    owner = lax.broadcasted_iota(jnp.int32, (groups, 1), 0)
    place = lax.broadcasted_iota(jnp.int32, (groups, groups * SLOT), 1)
    note = jnp.where(owner * SLOT + slots == place, 1.0, 0.0).astype(BF16)
    fills[z] = dot(note, landed[0, :, 0 : fills.shape[2]]).astype(BF16)
    for store, place in others:
        remote(fills.at[z], fills.at[z], cn_ssem.at[place], cn_rsem.at[place], store, t).start()
        pending.append(lambda place=place: await_bytes(fills.at[z], cn_ssem.at[place]))
    pass_inputs(1)
    for load in loads[1:]:
        load.wait()

    def upright(near, degree, own, dst):
        rows = near.shape[1]
        place = lax.broadcasted_iota(jnp.int32, (fan, rows), 0)
        parts = [jnp.where(place < degree[...][None, :], near, -1)] + own
        parts.append(jnp.full((SLOT - fan - len(own), rows), -1, jnp.int32))
        dst[...] = jnp.concatenate(parts, axis=0).T

    upright(near_one_t[...], degree_one, [self_ids[...][None, :]], near_one)
    upright(near_two_t[...], degree_two, [], near_two)
    upright(near_three_t[...], degree_three, [], near_three)
    slots_used = list(range(fan))
    count_matches(near_one, [(slots_used, tile_one), ([fan], tile_self)], outer, cells)
    count_matches(near_two, [(slots_used, tile_two)], mid, outer)
    count_matches(near_three, [(slots_used, tile_three)], seeds, mid)
    for quarter in range(2, stores):
        pass_inputs(quarter)

    def counted(near):
        return 1.0 + jnp.sum(jnp.where(near[...] >= 0, 1.0, 0.0), axis=1, keepdims=True)

    def spread_below(total, near, tile):
        rows = near.shape[0]
        scaled = (total[:, width:] / counted(near)).astype(BF16)
        below = dot(tile[...], scaled, 0, 0)
        upper = below[:rows] + (total[:, :width] + scaled.astype(F32))
        return jnp.concatenate([upper, below[rows:]], axis=0)

    for number in range(2):
        for store, place in others:
            await_bytes(w_rows.at[number, core, chip, store], wz_rsem.at[number, place])

        def pass_on(index, carry, number=number):
            target = lax.rem(chip + index, chips)
            spot = w_rows.at[number, core, chip]
            remote(spot, spot, wp_ssem.at[number], wp_rsem.at[number], z, target * 2 + core).start()
            return carry

        lax.fori_loop(1, chips, pass_on, 0)
        pending.append(lambda number=number: await_bytes(w_rows.at[number, core, pl.ds(0, chips - 1)], wp_ssem.at[number]))

    def note_filled():
        for store, place in others:
            await_bytes(fills.at[store], cn_rsem.at[place])
        row = lax.broadcasted_iota(jnp.int32, (kept, 1), 0)
        owner = (row * ((1 << 19) // slots + 1)) >> 19
        place = lax.broadcasted_iota(jnp.int32, (kept, groups), 1)
        pick = jnp.where(owner == place, 1.0, 0.0).astype(BF16)
        spot = (row - owner * slots).astype(F32)
        for store in range(stores):
            amount = dot(pick, fills[store])
            filled[store * kept : (store + 1) * kept, :] = jnp.where(spot < amount, 1.0, 0.0).astype(BF16)
        valid[...] = 1.0 + dot(tile_one[...], filled[...])

    rows_one = outer // 2

    def plane_part(tile, here, quarter, store):
        spot = pl.ds(pl.multiple_of(store * kept, kept), kept)
        return dot(tile[here, spot], inputs[quarter, spot, :])

    def start_sums(quarter):
        def body(index, carry):
            here = rows_at(index, rows_one)
            for place, tile in enumerate((tile_self, tile_one)):
                sums[quarter, place, here, :] = (
                    plane_part(tile, here, quarter, z)
                    + plane_part(tile, here, quarter, left)
                    + plane_part(tile, here, quarter, right)
                )
            return carry

        lax.fori_loop(0, 2, body, 0)

    def layer_one(quarter):
        def body(index, carry):
            here = rows_at(index, rows_one)
            own = sums[quarter, 0, here, :] + plane_part(tile_self, here, quarter, across)
            total = own + (sums[quarter, 1, here, :] + plane_part(tile_one, here, quarter, across))
            mean = total / jnp.concatenate([valid[here, :]] * (width // valid.shape[1]), axis=1)
            j_one[quarter, here, :] = jnp.concatenate([own, mean], axis=1).astype(BF16)
            part = dot(j_one[quarter, here, :], w_one[quarter])
            pre_one[here, :] = part if quarter == 0 else pre_one[here, :] + part
            return carry

        lax.fori_loop(0, 2, body, 0)

    def swap_weights():
        for number in range(2):
            spot = w_rows.at[number, core]
            await_bytes(w_rows.at[number, core, pl.ds(0, chips - 1)], wp_rsem.at[number])
            remote(spot, spot, ws_ssem.at[number], ws_rsem.at[number], z, sibling).start()
            pending.append(lambda spot=spot, number=number: await_bytes(spot, ws_ssem.at[number]))

    def before_sums():
        swap_weights()
        note_filled()

    take_gather(ring_one, stores, ag1_send, ag1_recv, start_sums, layer_one, before_sums)
    hid_one[...] = (pre_one[...] * jax.nn.sigmoid(pre_one[...])).astype(BF16)
    for number in range(2):
        await_bytes(w_rows.at[number, 1 - core], ws_rsem.at[number])

    def rows_of(number, store):
        return w_rows[number, :, :, store].reshape(2 * width, width)

    def join(hidden, near, tile, joined):
        rows = near.shape[0]
        own = hidden[0:rows, :]
        mean = (own.astype(F32) + dot(tile[...], hidden[...])) / counted(near)
        joined[...] = jnp.concatenate([own, mean.astype(BF16)], axis=1)

    def send_partials(joined, number, part, got, chunks):
        rows = part.shape[1] // chunks
        for index in range(chunks):
            here = pl.ds(index * rows, rows)
            for store, place in others:
                part[place, here, :] = dot(joined[here, :], rows_of(number, store)).astype(BF16)
                sems = rs_ssem.at[number, index, place], rs_rsem.at[number, index, place]
                remote(part.at[place, here, :], got.at[place, here, :], *sems, store, t).start()
                pending.append(lambda place=place, here=here, sem=sems[0]: await_bytes(part.at[place, here, :], sem))

    def take_partials(joined, number, got, index, rows):
        here = pl.ds(index * rows, rows)
        total = dot(joined[here, :], rows_of(number, z))
        for place in range(3):
            await_bytes(got.at[place, here, :], rs_rsem.at[number, index, place])
            total = total + got[place, here, :].astype(F32)
        return total

    join(hid_one, near_two, tile_two, j_two)
    chunks_two = agd_send.shape[1]
    rows_two = mid // chunks_two
    ring_two = lambda source, index: dpres.at[source, rows_at(index, rows_two), :]
    send_partials(j_two, 0, part_two, got_two, chunks_two)
    for store, place in others:
        await_bytes(cots.at[store], cot_rsem.at[place])
    spread = dot(cots[0], rows_of(1, 0), 1, 1)
    for store in range(1, stores):
        spread = spread + dot(cots[store], rows_of(1, store), 1, 1)
    below3[...] = spread_below(spread, near_three, tile_three)
    for index in range(chunks_two):
        here = rows_at(index, rows_two)
        pre_two[here, :] = take_partials(j_two, 0, got_two, index, rows_two)
        dpres[z, here, :] = (below3[here, :] * slope(pre_two[here, :])).astype(BF16)
        start_gather(ring_two, index, agd_send, agd_recv)
    hid_two[...] = (pre_two[...] * jax.nn.sigmoid(pre_two[...])).astype(BF16)
    join(hid_two, near_three, tile_three, j_three)

    height = full.shape[2]
    per_slice = width // height

    def pack(number):
        def body(index, carry):
            px_send[number, index] = full[number, index * 2 + 1 - core].astype(BF16)
            return carry

        lax.fori_loop(0, chips, body, 0)
        remote(
            px_send.at[number], px_recv.at[number], px_ssem.at[number], px_rsem.at[number], z, sibling
        ).start()
        pending.append(lambda: await_bytes(px_send.at[number], px_ssem.at[number]))

    def grad_of_columns(number, joined, dpre):
        def products(store, carry):
            part = dot(joined[store], dpre[...], 0, 0)
            for half in range(2):
                for index in range(per_slice):
                    start = half * width + index * height
                    full[number, half * (groups // 2) + store * per_slice + index] = part[start : start + height, :]
            return carry

        lax.fori_loop(0, stores, products, 0)
        pack(number)

    def grad_of_rows(number, joined, columns):
        def products(store, carry):
            part = dot(joined[...], columns[store], 0, 0)
            for index in range(2 * per_slice):
                full[number, index * stores + store] = part[index * height : (index + 1) * height, :]
            return carry

        lax.fori_loop(0, stores, products, 0)
        pack(number)

    side = rr.shape[2]
    place_x, place_y = chip // side, lax.rem(chip, side)
    spots = (place_x, place_y)

    def partner(way, index):
        target = lax.rem(spots[way] + index, side)
        column = (target, place_y) if way == 0 else (place_x, target)
        return target, (column[0] * side + column[1]) * 2 + core

    def share_first(number):
        await_bytes(px_recv.at[number], px_rsem.at[number])

        def body(index, carry):
            total = full[number, index * 2 + core] + px_recv[number, index].astype(F32)
            first, second = index // side, lax.rem(index, side)
            blk[number, 0, first, second] = total[: height // 2].astype(BF16)
            blk[number, 1, second, first] = total[height // 2 :].astype(BF16)
            return carry

        lax.fori_loop(0, chips, body, 0)
        for way in range(2):
            for index in range(1, side):
                target, trainer = partner(way, index)
                remote(
                    blk.at[number, way, target], rr.at[number, way, index],
                    rr_ssem.at[number, way, index], rr_rsem.at[number, way, index], z, trainer,
                ).start()
                pending.append(
                    lambda way=way, index=index, target=target: await_bytes(
                        blk.at[number, way, target], rr_ssem.at[number, way, index]
                    )
                )

    def share_second(number):
        for way in range(2):
            total = blk[number, way, spots[way]].astype(F32)
            for index in range(1, side):
                await_bytes(rr.at[number, way, index], rr_rsem.at[number, way, index])
                total = total + rr[number, way, index].astype(F32)
            line[number, way] = total
            thin[number, way] = total.astype(BF16)
            for index in range(1, side):
                target, trainer = partner(1 - way, index)
                remote(
                    thin.at[number, way, target], last.at[number, way, index],
                    ls_ssem.at[number, way, index], ls_rsem.at[number, way, index], z, trainer,
                ).start()
                pending.append(
                    lambda way=way, index=index, target=target: await_bytes(
                        thin.at[number, way, target], ls_ssem.at[number, way, index]
                    )
                )

    def summed(number):
        halves = []
        for way in range(2):
            total = line[number, way, spots[1 - way]]
            for index in range(1, side):
                await_bytes(last.at[number, way, index], ls_rsem.at[number, way, index])
                total = total + last[number, way, index].astype(F32)
            halves.append(total)
        return jnp.concatenate(halves, axis=0)

    block, to_store = t // stores, lax.rem(t, stores)
    to_trainer = jnp.where(
        block < per_slice, z * per_slice + block, groups // 2 + z * per_slice + block - per_slice
    )
    moves = jnp.logical_or(to_store != z, to_trainer != t)

    def move(number):
        move_send[number] = summed(number).astype(BF16)
        sems = mv_ssem.at[number], mv_rsem.at[number]

        @pl.when(moves)
        def _():
            remote(move_send.at[number], move_recv.at[number], *sems, to_store, to_trainer).start()

        @pl.when(jnp.logical_not(moves))
        def _():
            pltpu.make_async_copy(move_send.at[number], move_recv.at[number], mv_rsem.at[number]).start()

        def leave():
            @pl.when(moves)
            def _():
                await_bytes(move_send.at[number], mv_ssem.at[number])

        pending.append(leave)

    def take_move(number, out):
        await_bytes(move_recv.at[number], mv_rsem.at[number])
        out[...] = move_recv[number].astype(F32)

    grad_of_rows(1, j_three, cots)

    def spread_part(here, source):
        return dot(dpres[source, here, :], rows_of(0, source), 1, 1)

    def near_two_spread(index):
        here = rows_at(index, rows_two)
        spread_two[here, :] = spread_part(here, z) + spread_part(here, left) + spread_part(here, right)

    def far_two_spread(index):
        here = rows_at(index, rows_two)
        spread_two[here, :] += spread_part(here, across)

    take_gather(ring_two, chunks_two, agd_send, agd_recv, near_two_spread, far_two_spread, lambda: share_first(1))
    send_partials(j_three, 1, part_three, got_three, 1)
    grad_of_rows(0, j_two, dpres)
    below2 = spread_below(spread_two[...], near_two, tile_two)
    dpre_one[...] = (below2 * slope(pre_one[...])).astype(BF16)
    share_first(0)
    grad_of_columns(2, j_one, dpre_one)
    share_second(1)
    share_first(2)
    share_second(0)
    move(1)
    move(0)
    share_second(2)
    take_move(1, three_out)
    take_move(0, two_out)
    emb_out[...] = take_partials(j_three, 1, got_three, 0, seeds).astype(BF16)
    one_out[...] = summed(2)

    for leave in pending:
        leave()


def copies(*refs):
    half = len(refs) // 2
    for source, target in zip(refs[:half], refs[half:]):
        target[...] = source[...]


def run(
    stores, groups, features, sent_ids, block_sizes, self_ids, near_one, degree_one, near_two, degree_two,
    near_three, degree_three, weight_one, weight_two, weight_three, cotangent,
):
    slots = sent_ids.shape[2]
    outer, mid, seeds = near_one.shape[0], near_two.shape[0], near_three.shape[0]
    fan = near_one.shape[1]
    fwidth = features.shape[1]
    width = cotangent.shape[1]
    devices = stores * groups
    cells = devices * slots
    height = 2 * fwidth // groups

    vmem = pl.BlockSpec(memory_space=pltpu.VMEM)
    hbm = pl.BlockSpec(memory_space=pl.ANY)
    lanes = min(128, width)
    chunks_two = 2
    dma = pltpu.SemaphoreType.DMA
    chips = groups // 2
    side = math.isqrt(chips)
    scratch = [pltpu.VMEM((rows, SLOT), jnp.int32) for rows in (outer, mid, seeds, groups * SLOT)]
    scratch += [
        pltpu.VMEM((groups * SLOT, lanes), F32),
        pltpu.VMEM(features.shape, BF16),
        pltpu.VMEM((groups * SLOT, features.shape[0]), BF16),
        pltpu.VMEM((stores, groups * SLOT, width), BF16),
        pltpu.VMEM((stores, groups * SLOT, width), BF16),
        pltpu.VMEM((groups * slots, groups * SLOT), BF16),
        pltpu.VMEM((stores, cells, width), BF16),
        pltpu.VMEM((stores, groups, lanes), BF16),
        pltpu.VMEM((cells, lanes), BF16),
        pltpu.VMEM((outer, lanes), F32),
        pltpu.VMEM((stores, 2, outer, width), F32),
        pltpu.VMEM((outer, cells), BF16),
        pltpu.VMEM((outer, cells), BF16),
        pltpu.VMEM((mid, outer), BF16),
        pltpu.VMEM((seeds, mid), BF16),
        pltpu.VMEM((stores, 2 * width, width), BF16),
        pltpu.VMEM((2, 2, chips, stores, width // chips, width), BF16),
        pltpu.VMEM((stores, outer, 2 * width), BF16),
        pltpu.VMEM((mid, 2 * width), BF16),
        pltpu.VMEM((seeds, 2 * width), BF16),
        pltpu.VMEM((outer, width), F32),
        pltpu.VMEM((mid, width), F32),
        pltpu.VMEM((outer, width), BF16),
        pltpu.VMEM((mid, width), BF16),
        pltpu.VMEM((stores, seeds, width), BF16),
        pltpu.VMEM((stores, mid, width), BF16),
        pltpu.VMEM((mid, 2 * width), F32),
        pltpu.VMEM((mid, width), F32),
        pltpu.VMEM((outer, width), BF16),
    ]
    scratch += [pltpu.VMEM((3, mid, width), BF16)] * 2 + [pltpu.VMEM((3, seeds, width), BF16)] * 2
    scratch += [pltpu.VMEM((3, groups, height, width), F32)]
    scratch += [pltpu.VMEM((3, chips, height, width), BF16)] * 2
    scratch += [pltpu.VMEM((3, 2, side, side, height // 2, width), BF16)] * 2
    scratch += [pltpu.VMEM((3, 2, side, height // 2, width), kind) for kind in (F32, BF16, BF16)]
    scratch += [pltpu.VMEM((2, height, width), BF16)] * 2
    scratch += [dma((4 + 2 * stores,)), dma((stores,)), dma((stores,)), dma((3,)), dma((3,))]
    scratch += [dma((3, chunks)) for chunks in (stores, stores, chunks_two, chunks_two)]
    scratch += [dma((3,))] * 2 + [dma((2, 3))] * 2 + [dma((2,))] * 4 + [dma((2, chunks_two, 3))] * 2
    scratch += [dma((3,))] * 2 + [dma((3, 2, side))] * 4 + [dma((2,))] * 2
    shapes = (
        jax.ShapeDtypeStruct((seeds, width), BF16),
        jax.ShapeDtypeStruct((height, width), F32),
        jax.ShapeDtypeStruct((height, width), F32),
        jax.ShapeDtypeStruct((height, width), F32),
    )
    results = pl.pallas_call(
        functools.partial(kernel, stores, groups, slots),
        out_shape=shapes,
        in_specs=[vmem] * 10 + [hbm] * 4,
        out_specs=(vmem,) * 4,
        scratch_shapes=scratch,
        compiler_params=pltpu.CompilerParams(
            collective_id=0, has_side_effects=True, vmem_limit_bytes=60 * 1024 * 1024
        ),
    )(
        jnp.transpose(sent_ids, (2, 0, 1)), block_sizes, self_ids,
        near_one.T, degree_one, near_two.T, degree_two, near_three.T, degree_three,
        cotangent, features, weight_one, weight_two, weight_three,
    )
    return pl.pallas_call(copies, out_shape=shapes, in_specs=[vmem] * 4, out_specs=(vmem,) * 4)(*results)


def solution(mesh):
    stores, groups = mesh.shape["store"], mesh.shape["trainer"]
    both = ("store", "trainer")
    placed = (
        P(both, None), P(both, None, None), P(both, None), P("trainer"), P("trainer", None), P("trainer"),
        P("trainer", None), P("trainer"), P("trainer", None), P("trainer"),
        P(None, "store"), P(None, "store"), P(None, "store"), P("trainer", "store"),
    )
    return jax.shard_map(
        functools.partial(run, stores, groups),
        mesh=mesh, in_specs=placed, out_specs=(P("trainer", "store"),) * 4, check_vma=False,
    )
```

```python
import functools
import math

import jax
import jax.numpy as jnp
from jax import lax
from jax.experimental import pallas as pl
from jax.experimental.pallas import tpu as pltpu
from jax.sharding import PartitionSpec as P

MESH = pl.DeviceIdType.MESH
F32 = jnp.float32
BF16 = jnp.bfloat16
SLOT = 16


def dot(a, b, left=1, right=0):
    return lax.dot_general(a, b, (((left,), (right,)), ((), ())), preferred_element_type=F32)


def slope(preact):
    sigma = jax.nn.sigmoid(preact)
    return sigma * (1.0 + preact * (1.0 - sigma))


def rows_at(index, size):
    return pl.ds(pl.multiple_of(index * size, size), size)


def step_of(rows, most):
    size = min(rows, most)
    while rows % size:
        size -= 1
    return size


def count_matches(ids, wanted, rows, width):
    high = step_of(rows, 128)
    wide = step_of(width, 256)

    def body(index, carry):
        here = rows_at(index, high)
        part = ids[here, :].astype(jnp.int16)
        for start in range(0, width, wide):
            place = (lax.broadcasted_iota(jnp.int32, (high, wide), 1) + start).astype(jnp.int16)
            for column_list, dst in wanted:
                total = None
                for column in column_list:
                    found = jnp.where(part[:, column : column + 1] == place, BF16(1), BF16(0))
                    total = found if total is None else total + found
                dst[here, start : start + wide] = total
        return carry

    lax.fori_loop(0, rows // high, body, 0)


def kernel(
    stores, groups, slots,
    sent, sizes, self_ids, near_one_t, degree_one, near_two_t, degree_two, near_three_t, degree_three,
    cot, feat_hbm, one_hbm, two_hbm, three_hbm,
    emb_out, one_out, two_out, three_out,
    near_one, near_two, near_three, asked, extra, feat, hot, picked, landed, dense, inputs, fills, filled, valid, sums,
    tile_one, tile_self, tile_two, tile_three, w_one, w_rows,
    j_one, j_two, j_three, pre_one, pre_two, hid_one, hid_two, cots, dpres, spread_two, below3, dpre_one,
    part_two, got_two, part_three, got_three,
    full, px_send, px_recv, blk, rr, line, thin, last, move_send, move_recv,
    load_sem, in_send, in_recv, cn_ssem, cn_rsem, ag1_send, ag1_recv, agd_send, agd_recv,
    cot_ssem, cot_rsem, wz_ssem, wz_rsem, wp_ssem, wp_rsem, ws_ssem, ws_rsem,
    rs_ssem, rs_rsem, px_ssem, px_rsem, rr_ssem, rr_rsem, ls_ssem, ls_rsem, mv_ssem, mv_rsem,
):
    devices = stores * groups
    z = lax.axis_index("store")
    t = lax.axis_index("trainer")
    me = z * groups + t
    chip, core = t // 2, lax.rem(t, 2)
    chips = groups // 2
    sibling = t + 1 - 2 * core
    right, left, across = (lax.rem(z + k, stores) for k in (1, 3, 2))
    others = ((across, 2), (right, 0), (left, 1))
    width = cot.shape[1]
    seeds, mid, outer = cot.shape[0], near_two.shape[0], near_one.shape[0]
    kept = groups * slots
    cells = stores * kept
    fan = near_two_t.shape[0]
    pending = []

    def remote(src, dst, send_sem, recv_sem, store, trainer):
        return pltpu.make_async_remote_copy(
            src_ref=src, dst_ref=dst, send_sem=send_sem, recv_sem=recv_sem,
            device_id=(store, trainer), device_id_type=MESH,
        )

    def await_bytes(ref, sem):
        pltpu.make_async_copy(ref, ref, sem).wait()

    barrier = pltpu.get_barrier_semaphore()

    def greet(index, carry):
        other = lax.rem(me + index, devices)
        pl.semaphore_signal(
            barrier, inc=1, device_id=(other // groups, lax.rem(other, groups)), device_id_type=MESH
        )
        return carry

    lax.fori_loop(1, devices, greet, 0)

    share = w_rows.shape[4]

    def piece_of(hbm, store):
        return hbm.at[pl.ds(pl.multiple_of(core * stores * width + store * width + chip * share, share), share), :]

    loads = [pltpu.make_async_copy(feat_hbm, feat, load_sem.at[0])]
    for place, hbm in enumerate((two_hbm, three_hbm)):
        loads.append(pltpu.make_async_copy(piece_of(hbm, z), w_rows.at[place, core, chip, z], load_sem.at[1 + place]))
    loads.append(pltpu.make_async_copy(cot, cots.at[z], load_sem.at[3]))
    for store in range(stores):
        for half in range(2):
            loads.append(
                pltpu.make_async_copy(
                    one_hbm.at[pl.ds((half * stores + store) * width, width), :],
                    w_one.at[store, pl.ds(half * width, width), :],
                    load_sem.at[4 + store * 2 + half],
                )
            )
    for load in loads:
        load.start()

    slot = lax.broadcasted_iota(jnp.int32, (SLOT, groups), 0)
    amounts = jnp.broadcast_to(sizes[...], (SLOT, groups))
    wanted = jnp.concatenate([sent[index] for index in range(slots)] + [jnp.full((SLOT - slots, groups), -1, jnp.int32)], axis=0)
    wanted = jnp.where(slot < amounts, wanted, -1)
    notes = jnp.where(slot == slots, amounts, 0).astype(F32)
    for group in range(groups):
        here = pl.ds(group * SLOT, SLOT)
        extra[here, :] = jnp.broadcast_to(notes[:, group : group + 1], (SLOT, extra.shape[1]))
        asked[here, :] = jnp.broadcast_to(wanted[:, group : group + 1], (SLOT, SLOT))
    count_matches(asked, [([0], hot)], groups * SLOT, feat.shape[0])
    loads[0].wait()
    pl.semaphore_wait(barrier, devices - 1)

    for store, place in others:
        remote(cot, cots.at[z], cot_ssem.at[place], cot_rsem.at[place], store, t).start()
        pending.append(lambda place=place: await_bytes(cot, cot_ssem.at[place]))
        for number, hbm in enumerate((two_hbm, three_hbm)):
            spot = w_rows.at[number, core, chip, z]
            remote(piece_of(hbm, store), spot, wz_ssem.at[number, place], wz_rsem.at[number, place], store, t).start()
            pending.append(lambda number=number, place=place, spot=spot: await_bytes(spot, wz_ssem.at[number, place]))

    def fetch(quarter, carry):
        columns = pl.ds(pl.multiple_of(quarter * width, width), width)
        rows = step_of(groups * SLOT, 256)
        for start in range(0, groups * SLOT, rows):
            part = dot(hot[start : start + rows, :], feat[:, columns])
            counts = jnp.concatenate([extra[start : start + rows, :]] * (width // extra.shape[1]), axis=1)
            picked[quarter, start : start + rows, :] = (part + counts).astype(BF16)

        def send(number, inner):
            trainer = lax.rem(t + number * 13, groups)
            remote(
                picked.at[quarter, rows_at(trainer, SLOT), :], landed.at[quarter, rows_at(t, SLOT), :],
                in_send.at[quarter], in_recv.at[quarter], z, trainer,
            ).start()
            return inner

        lax.fori_loop(1, groups, send, 0)
        pltpu.make_async_copy(
            picked.at[quarter, rows_at(t, SLOT), :], landed.at[quarter, rows_at(t, SLOT), :], in_recv.at[quarter]
        ).start()
        return carry

    lax.fori_loop(0, stores, fetch, 0)

    def leave_blocks():
        for quarter in range(stores):
            await_bytes(picked.at[quarter, pl.ds(0, (groups - 1) * SLOT), :], in_send.at[quarter])

    pending.append(leave_blocks)

    def moved(index):
        return index + (SLOT - slots) * ((index * ((1 << 19) // slots + 1)) >> 19)

    from_row = moved(lax.broadcasted_iota(jnp.int32, (kept, 1), 0))
    place = lax.broadcasted_iota(jnp.int32, (kept, groups * SLOT), 1)
    dense[...] = jnp.where(from_row == place, 1.0, 0.0).astype(BF16)
    ring_one = lambda source, index: inputs.at[index, pl.ds(pl.multiple_of(source * kept, kept), kept), :]

    def start_gather(piece_at, index, send_sem, recv_sem):
        piece = piece_at(z, index)
        remote(piece, piece, send_sem.at[0, index], recv_sem.at[0, index], right, t).start()
        remote(piece, piece, send_sem.at[1, index], recv_sem.at[1, index], left, t).start()

    def take_gather(piece_at, chunks, send_sem, recv_sem, near, far, between):
        for index in range(chunks):
            for side_at, (source, onward) in enumerate(((left, right), (right, left))):
                piece = piece_at(source, index)
                await_bytes(piece, recv_sem.at[side_at, index])
                if index % 2 == side_at:
                    remote(piece, piece, send_sem.at[2, index], recv_sem.at[2, index], onward, t).start()
            near(index)
        between()
        for index in range(chunks):
            await_bytes(piece_at(across, index), recv_sem.at[2, index])
            far(index)
        for way in range(3):
            for index in range(chunks):
                pending.append(
                    lambda way=way, index=index: await_bytes(piece_at(z, index), send_sem.at[way, index])
                )

    def pass_inputs(quarter):
        await_bytes(landed.at[quarter], in_recv.at[quarter])
        inputs[quarter, pl.ds(pl.multiple_of(z * kept, kept), kept), :] = dot(dense[...], landed[quarter]).astype(BF16)
        start_gather(ring_one, quarter, ag1_send, ag1_recv)

    pass_inputs(0)
    owner = lax.broadcasted_iota(jnp.int32, (groups, 1), 0)
    place = lax.broadcasted_iota(jnp.int32, (groups, groups * SLOT), 1)
    note = jnp.where(owner * SLOT + slots == place, 1.0, 0.0).astype(BF16)
    fills[z] = dot(note, landed[0, :, 0 : fills.shape[2]]).astype(BF16)
    for store, place in others:
        remote(fills.at[z], fills.at[z], cn_ssem.at[place], cn_rsem.at[place], store, t).start()
        pending.append(lambda place=place: await_bytes(fills.at[z], cn_ssem.at[place]))
    pass_inputs(1)
    for load in loads[1:]:
        load.wait()

    def upright(near, degree, own, dst):
        rows = near.shape[1]
        place = lax.broadcasted_iota(jnp.int32, (fan, rows), 0)
        parts = [jnp.where(place < degree[...][None, :], near, -1)] + own
        parts.append(jnp.full((SLOT - fan - len(own), rows), -1, jnp.int32))
        dst[...] = jnp.concatenate(parts, axis=0).T

    upright(near_one_t[...], degree_one, [self_ids[...][None, :]], near_one)
    upright(near_two_t[...], degree_two, [], near_two)
    upright(near_three_t[...], degree_three, [], near_three)
    slots_used = list(range(fan))
    count_matches(near_one, [(slots_used, tile_one), ([fan], tile_self)], outer, cells)
    count_matches(near_two, [(slots_used, tile_two)], mid, outer)
    count_matches(near_three, [(slots_used, tile_three)], seeds, mid)
    for quarter in range(2, stores):
        pass_inputs(quarter)

    def counted(near):
        return 1.0 + jnp.sum(jnp.where(near[...] >= 0, 1.0, 0.0), axis=1, keepdims=True)

    def spread_below(total, near, tile):
        rows = near.shape[0]
        scaled = (total[:, width:] / counted(near)).astype(BF16)
        below = dot(tile[...], scaled, 0, 0)
        upper = below[:rows] + (total[:, :width] + scaled.astype(F32))
        return jnp.concatenate([upper, below[rows:]], axis=0)

    for number in range(2):
        for store, place in others:
            await_bytes(w_rows.at[number, core, chip, store], wz_rsem.at[number, place])

        def pass_on(index, carry, number=number):
            target = lax.rem(chip + index, chips)
            spot = w_rows.at[number, core, chip]
            remote(spot, spot, wp_ssem.at[number], wp_rsem.at[number], z, target * 2 + core).start()
            return carry

        lax.fori_loop(1, chips, pass_on, 0)
        pending.append(lambda number=number: await_bytes(w_rows.at[number, core, pl.ds(0, chips - 1)], wp_ssem.at[number]))

    def note_filled():
        for store, place in others:
            await_bytes(fills.at[store], cn_rsem.at[place])
        row = lax.broadcasted_iota(jnp.int32, (kept, 1), 0)
        owner = (row * ((1 << 19) // slots + 1)) >> 19
        place = lax.broadcasted_iota(jnp.int32, (kept, groups), 1)
        pick = jnp.where(owner == place, 1.0, 0.0).astype(BF16)
        spot = (row - owner * slots).astype(F32)
        for store in range(stores):
            amount = dot(pick, fills[store])
            filled[store * kept : (store + 1) * kept, :] = jnp.where(spot < amount, 1.0, 0.0).astype(BF16)
        valid[...] = 1.0 + dot(tile_one[...], filled[...])

    rows_one = outer // 2

    def plane_part(tile, here, quarter, store):
        spot = pl.ds(pl.multiple_of(store * kept, kept), kept)
        return dot(tile[here, spot], inputs[quarter, spot, :])

    def start_sums(quarter):
        def body(index, carry):
            here = rows_at(index, rows_one)
            for place, tile in enumerate((tile_self, tile_one)):
                sums[quarter, place, here, :] = (
                    plane_part(tile, here, quarter, z)
                    + plane_part(tile, here, quarter, left)
                    + plane_part(tile, here, quarter, right)
                )
            return carry

        lax.fori_loop(0, 2, body, 0)

    def layer_one(quarter):
        def body(index, carry):
            here = rows_at(index, rows_one)
            own = sums[quarter, 0, here, :] + plane_part(tile_self, here, quarter, across)
            total = own + (sums[quarter, 1, here, :] + plane_part(tile_one, here, quarter, across))
            mean = total / jnp.concatenate([valid[here, :]] * (width // valid.shape[1]), axis=1)
            j_one[quarter, here, :] = jnp.concatenate([own, mean], axis=1).astype(BF16)
            part = dot(j_one[quarter, here, :], w_one[quarter])
            pre_one[here, :] = part if quarter == 0 else pre_one[here, :] + part
            return carry

        lax.fori_loop(0, 2, body, 0)

    def swap_weights():
        for number in range(2):
            spot = w_rows.at[number, core]
            await_bytes(w_rows.at[number, core, pl.ds(0, chips - 1)], wp_rsem.at[number])
            remote(spot, spot, ws_ssem.at[number], ws_rsem.at[number], z, sibling).start()
            pending.append(lambda spot=spot, number=number: await_bytes(spot, ws_ssem.at[number]))

    def before_sums():
        swap_weights()
        note_filled()

    take_gather(ring_one, stores, ag1_send, ag1_recv, start_sums, layer_one, before_sums)
    hid_one[...] = (pre_one[...] * jax.nn.sigmoid(pre_one[...])).astype(BF16)
    for number in range(2):
        await_bytes(w_rows.at[number, 1 - core], ws_rsem.at[number])

    def rows_of(number, store):
        return w_rows[number, :, :, store].reshape(2 * width, width)

    def join(hidden, near, tile, joined):
        rows = near.shape[0]
        own = hidden[0:rows, :]
        mean = (own.astype(F32) + dot(tile[...], hidden[...])) / counted(near)
        joined[...] = jnp.concatenate([own, mean.astype(BF16)], axis=1)

    def send_partials(joined, number, part, got, chunks):
        rows = part.shape[1] // chunks
        for index in range(chunks):
            here = pl.ds(index * rows, rows)
            for store, place in others:
                part[place, here, :] = dot(joined[here, :], rows_of(number, store)).astype(BF16)
                sems = rs_ssem.at[number, index, place], rs_rsem.at[number, index, place]
                remote(part.at[place, here, :], got.at[place, here, :], *sems, store, t).start()
                pending.append(lambda place=place, here=here, sem=sems[0]: await_bytes(part.at[place, here, :], sem))

    def take_partials(joined, number, got, index, rows):
        here = pl.ds(index * rows, rows)
        total = dot(joined[here, :], rows_of(number, z))
        for place in range(3):
            await_bytes(got.at[place, here, :], rs_rsem.at[number, index, place])
            total = total + got[place, here, :].astype(F32)
        return total

    join(hid_one, near_two, tile_two, j_two)
    chunks_two = agd_send.shape[1]
    rows_two = mid // chunks_two
    ring_two = lambda source, index: dpres.at[source, rows_at(index, rows_two), :]
    send_partials(j_two, 0, part_two, got_two, chunks_two)
    for store, place in others:
        await_bytes(cots.at[store], cot_rsem.at[place])
    spread = dot(cots[0], rows_of(1, 0), 1, 1)
    for store in range(1, stores):
        spread = spread + dot(cots[store], rows_of(1, store), 1, 1)
    below3[...] = spread_below(spread, near_three, tile_three)
    for index in range(chunks_two):
        here = rows_at(index, rows_two)
        pre_two[here, :] = take_partials(j_two, 0, got_two, index, rows_two)
        dpres[z, here, :] = (below3[here, :] * slope(pre_two[here, :])).astype(BF16)
        start_gather(ring_two, index, agd_send, agd_recv)
    hid_two[...] = (pre_two[...] * jax.nn.sigmoid(pre_two[...])).astype(BF16)
    join(hid_two, near_three, tile_three, j_three)

    height = full.shape[2]
    per_slice = width // height

    def pass_over(number, first, amount):
        spot = pl.ds(first, amount)
        remote(
            px_send.at[number, spot], px_recv.at[number, spot], px_ssem.at[number], px_rsem.at[number], z, sibling
        ).start()

    def left_over(number):
        pending.append(lambda: await_bytes(px_send.at[number], px_ssem.at[number]))

    pairs = per_slice // 2 if per_slice % 2 == 0 else 0

    def grad_of_columns(number, joined, dpre):
        def products(store, carry):
            part = dot(joined[store], dpre[...], 0, 0)
            for half in range(2):
                for index in range(per_slice):
                    start = half * width + index * height
                    full[number, half * (groups // 2) + store * per_slice + index] = part[start : start + height, :]
            for half in range(2):
                for index in range(pairs):
                    block = half * (groups // 2) + store * per_slice + 2 * index + 1 - core
                    px_send[number, store * per_slice + half * pairs + index] = full[number, block].astype(BF16)
            if pairs:
                pass_over(number, store * per_slice, per_slice)
            return carry

        lax.fori_loop(0, stores, products, 0)
        if not pairs:
            for index in range(chips):
                px_send[number, index] = full[number, index * 2 + 1 - core].astype(BF16)
            pass_over(number, 0, chips)
        left_over(number)

    def column_slot(index):
        if not pairs:
            return index
        half, rest = index // (chips // 2), lax.rem(index, chips // 2)
        return rest // pairs * per_slice + half * pairs + lax.rem(rest, pairs)

    def grad_of_rows(number, joined, columns, store):
        part = dot(joined[...], columns[store], 0, 0)
        passed = lax.rem(store, 2) != core
        first = store // 2 * 2 * per_slice

        @pl.when(passed)
        def _():
            for index in range(2 * per_slice):
                px_send[number, first + index] = part[index * height : (index + 1) * height, :].astype(BF16)
            pass_over(number, first, 2 * per_slice)

        @pl.when(jnp.logical_not(passed))
        def _():
            for index in range(2 * per_slice):
                full[number, index * stores + store] = part[index * height : (index + 1) * height, :]

    def row_slot(index):
        return lax.rem(index, stores // 2) * 2 * per_slice + index // (stores // 2)

    side = rr.shape[2]
    place_x, place_y = chip // side, lax.rem(chip, side)
    spots = (place_x, place_y)

    def partner(way, index):
        target = lax.rem(spots[way] + index, side)
        column = (target, place_y) if way == 0 else (place_x, target)
        return target, (column[0] * side + column[1]) * 2 + core

    def share_first(number, slot_of):
        await_bytes(px_recv.at[number], px_rsem.at[number])

        def body(index, carry):
            total = full[number, index * 2 + core] + px_recv[number, slot_of(index)].astype(F32)
            first, second = index // side, lax.rem(index, side)
            blk[number, 0, first, second] = total[: height // 2].astype(BF16)
            blk[number, 1, second, first] = total[height // 2 :].astype(BF16)
            return carry

        lax.fori_loop(0, chips, body, 0)
        for way in range(2):
            for index in range(1, side):
                target, trainer = partner(way, index)
                remote(
                    blk.at[number, way, target], rr.at[number, way, index],
                    rr_ssem.at[number, way, index], rr_rsem.at[number, way, index], z, trainer,
                ).start()
                pending.append(
                    lambda way=way, index=index, target=target: await_bytes(
                        blk.at[number, way, target], rr_ssem.at[number, way, index]
                    )
                )

    def share_second(number):
        for way in range(2):
            total = blk[number, way, spots[way]].astype(F32)
            for index in range(1, side):
                await_bytes(rr.at[number, way, index], rr_rsem.at[number, way, index])
                total = total + rr[number, way, index].astype(F32)
            line[number, way] = total
            thin[number, way] = total.astype(BF16)
            for index in range(1, side):
                target, trainer = partner(1 - way, index)
                remote(
                    thin.at[number, way, target], last.at[number, way, index],
                    ls_ssem.at[number, way, index], ls_rsem.at[number, way, index], z, trainer,
                ).start()
                pending.append(
                    lambda way=way, index=index, target=target: await_bytes(
                        thin.at[number, way, target], ls_ssem.at[number, way, index]
                    )
                )

    def summed(number):
        halves = []
        for way in range(2):
            total = line[number, way, spots[1 - way]]
            for index in range(1, side):
                await_bytes(last.at[number, way, index], ls_rsem.at[number, way, index])
                total = total + last[number, way, index].astype(F32)
            halves.append(total)
        return jnp.concatenate(halves, axis=0)

    block, to_store = t // stores, lax.rem(t, stores)
    to_trainer = jnp.where(
        block < per_slice, z * per_slice + block, groups // 2 + z * per_slice + block - per_slice
    )
    moves = jnp.logical_or(to_store != z, to_trainer != t)

    def move(number):
        move_send[number] = summed(number).astype(BF16)
        sems = mv_ssem.at[number], mv_rsem.at[number]

        @pl.when(moves)
        def _():
            remote(move_send.at[number], move_recv.at[number], *sems, to_store, to_trainer).start()

        @pl.when(jnp.logical_not(moves))
        def _():
            pltpu.make_async_copy(move_send.at[number], move_recv.at[number], mv_rsem.at[number]).start()

        def leave():
            @pl.when(moves)
            def _():
                await_bytes(move_send.at[number], mv_ssem.at[number])

        pending.append(leave)

    def take_move(number, out):
        await_bytes(move_recv.at[number], mv_rsem.at[number])
        out[...] = move_recv[number].astype(F32)

    for turn in range(stores):
        grad_of_rows(1, j_three, cots, lax.rem(core + 1 + turn * 2 + turn // 2, stores))
    left_over(1)

    def spread_part(here, source):
        return dot(dpres[source, here, :], rows_of(0, source), 1, 1)

    def near_two_spread(index):
        here = rows_at(index, rows_two)
        spread_two[here, :] = spread_part(here, z) + spread_part(here, left) + spread_part(here, right)

    def far_two_spread(index):
        here = rows_at(index, rows_two)
        spread_two[here, :] += spread_part(here, across)

    def meanwhile():
        share_first(1, row_slot)
        for store in (left, right, z):
            grad_of_rows(0, j_two, dpres, store)

    take_gather(ring_two, chunks_two, agd_send, agd_recv, near_two_spread, far_two_spread, meanwhile)
    grad_of_rows(0, j_two, dpres, across)
    left_over(0)
    below2 = spread_below(spread_two[...], near_two, tile_two)
    dpre_one[...] = (below2 * slope(pre_one[...])).astype(BF16)
    share_first(0, row_slot)
    grad_of_columns(2, j_one, dpre_one)
    share_second(1)
    send_partials(j_three, 1, part_three, got_three, 1)
    share_first(2, column_slot)
    share_second(0)
    move(1)
    move(0)
    share_second(2)
    take_move(1, three_out)
    take_move(0, two_out)
    emb_out[...] = take_partials(j_three, 1, got_three, 0, seeds).astype(BF16)
    one_out[...] = summed(2)

    for leave in pending:
        leave()


def copies(*refs):
    half = len(refs) // 2
    for source, target in zip(refs[:half], refs[half:]):
        target[...] = source[...]


def run(
    stores, groups, features, sent_ids, block_sizes, self_ids, near_one, degree_one, near_two, degree_two,
    near_three, degree_three, weight_one, weight_two, weight_three, cotangent,
):
    slots = sent_ids.shape[2]
    outer, mid, seeds = near_one.shape[0], near_two.shape[0], near_three.shape[0]
    fan = near_one.shape[1]
    fwidth = features.shape[1]
    width = cotangent.shape[1]
    devices = stores * groups
    cells = devices * slots
    height = 2 * fwidth // groups

    vmem = pl.BlockSpec(memory_space=pltpu.VMEM)
    hbm = pl.BlockSpec(memory_space=pl.ANY)
    lanes = min(128, width)
    chunks_two = 4
    dma = pltpu.SemaphoreType.DMA
    chips = groups // 2
    side = math.isqrt(chips)
    scratch = [pltpu.VMEM((rows, SLOT), jnp.int32) for rows in (outer, mid, seeds, groups * SLOT)]
    scratch += [
        pltpu.VMEM((groups * SLOT, lanes), F32),
        pltpu.VMEM(features.shape, BF16),
        pltpu.VMEM((groups * SLOT, features.shape[0]), BF16),
        pltpu.VMEM((stores, groups * SLOT, width), BF16),
        pltpu.VMEM((stores, groups * SLOT, width), BF16),
        pltpu.VMEM((groups * slots, groups * SLOT), BF16),
        pltpu.VMEM((stores, cells, width), BF16),
        pltpu.VMEM((stores, groups, lanes), BF16),
        pltpu.VMEM((cells, lanes), BF16),
        pltpu.VMEM((outer, lanes), F32),
        pltpu.VMEM((stores, 2, outer, width), F32),
        pltpu.VMEM((outer, cells), BF16),
        pltpu.VMEM((outer, cells), BF16),
        pltpu.VMEM((mid, outer), BF16),
        pltpu.VMEM((seeds, mid), BF16),
        pltpu.VMEM((stores, 2 * width, width), BF16),
        pltpu.VMEM((2, 2, chips, stores, width // chips, width), BF16),
        pltpu.VMEM((stores, outer, 2 * width), BF16),
        pltpu.VMEM((mid, 2 * width), BF16),
        pltpu.VMEM((seeds, 2 * width), BF16),
        pltpu.VMEM((outer, width), F32),
        pltpu.VMEM((mid, width), F32),
        pltpu.VMEM((outer, width), BF16),
        pltpu.VMEM((mid, width), BF16),
        pltpu.VMEM((stores, seeds, width), BF16),
        pltpu.VMEM((stores, mid, width), BF16),
        pltpu.VMEM((mid, 2 * width), F32),
        pltpu.VMEM((mid, width), F32),
        pltpu.VMEM((outer, width), BF16),
    ]
    scratch += [pltpu.VMEM((3, mid, width), BF16)] * 2 + [pltpu.VMEM((3, seeds, width), BF16)] * 2
    scratch += [pltpu.VMEM((3, groups, height, width), F32)]
    scratch += [pltpu.VMEM((3, chips, height, width), BF16)] * 2
    scratch += [pltpu.VMEM((3, 2, side, side, height // 2, width), BF16)] * 2
    scratch += [pltpu.VMEM((3, 2, side, height // 2, width), kind) for kind in (F32, BF16, BF16)]
    scratch += [pltpu.VMEM((2, height, width), BF16)] * 2
    scratch += [dma((4 + 2 * stores,)), dma((stores,)), dma((stores,)), dma((3,)), dma((3,))]
    scratch += [dma((3, chunks)) for chunks in (stores, stores, chunks_two, chunks_two)]
    scratch += [dma((3,))] * 2 + [dma((2, 3))] * 2 + [dma((2,))] * 4 + [dma((2, chunks_two, 3))] * 2
    scratch += [dma((3,))] * 2 + [dma((3, 2, side))] * 4 + [dma((2,))] * 2
    shapes = (
        jax.ShapeDtypeStruct((seeds, width), BF16),
        jax.ShapeDtypeStruct((height, width), F32),
        jax.ShapeDtypeStruct((height, width), F32),
        jax.ShapeDtypeStruct((height, width), F32),
    )
    results = pl.pallas_call(
        functools.partial(kernel, stores, groups, slots),
        out_shape=shapes,
        in_specs=[vmem] * 10 + [hbm] * 4,
        out_specs=(vmem,) * 4,
        scratch_shapes=scratch,
        compiler_params=pltpu.CompilerParams(
            collective_id=0, has_side_effects=True, vmem_limit_bytes=60 * 1024 * 1024
        ),
    )(
        jnp.transpose(sent_ids, (2, 0, 1)), block_sizes, self_ids,
        near_one.T, degree_one, near_two.T, degree_two, near_three.T, degree_three,
        cotangent, features, weight_one, weight_two, weight_three,
    )
    return pl.pallas_call(copies, out_shape=shapes, in_specs=[vmem] * 4, out_specs=(vmem,) * 4)(*results)


def solution(mesh):
    stores, groups = mesh.shape["store"], mesh.shape["trainer"]
    both = ("store", "trainer")
    placed = (
        P(both, None), P(both, None, None), P(both, None), P("trainer"), P("trainer", None), P("trainer"),
        P("trainer", None), P("trainer"), P("trainer", None), P("trainer"),
        P(None, "store"), P(None, "store"), P(None, "store"), P("trainer", "store"),
    )
    return jax.shard_map(
        functools.partial(run, stores, groups),
        mesh=mesh, in_specs=placed, out_specs=(P("trainer", "store"),) * 4, check_vma=False,
    )
```

```python
import functools
import math

import jax
import jax.numpy as jnp
from jax import lax
from jax.experimental import pallas as pl
from jax.experimental.pallas import tpu as pltpu
from jax.sharding import PartitionSpec as P

MESH = pl.DeviceIdType.MESH
F32 = jnp.float32
BF16 = jnp.bfloat16
SLOT = 16


def dot(a, b, left=1, right=0):
    return lax.dot_general(a, b, (((left,), (right,)), ((), ())), preferred_element_type=F32)


def slope(preact):
    sigma = jax.nn.sigmoid(preact)
    return sigma * (1.0 + preact * (1.0 - sigma))


def rows_at(index, size):
    return pl.ds(pl.multiple_of(index * size, size), size)


def step_of(rows, most):
    size = min(rows, most)
    while rows % size:
        size -= 1
    return size


def count_matches(ids, wanted, rows, width):
    high = step_of(rows, 128)
    wide = step_of(width, 256)

    def body(index, carry):
        here = rows_at(index, high)
        part = ids[here, :].astype(jnp.int16)
        for start in range(0, width, wide):
            place = (lax.broadcasted_iota(jnp.int32, (high, wide), 1) + start).astype(jnp.int16)
            for column_list, dst in wanted:
                total = None
                for column in column_list:
                    found = jnp.where(part[:, column : column + 1] == place, BF16(1), BF16(0))
                    total = found if total is None else total + found
                dst[here, start : start + wide] = total
        return carry

    lax.fori_loop(0, rows // high, body, 0)


def kernel(
    stores, groups, slots,
    sent, sizes, self_ids, near_one_t, degree_one, near_two_t, degree_two, near_three_t, degree_three,
    cot, feat_hbm, one_hbm, two_hbm, three_hbm,
    emb_out, one_out, two_out, three_out,
    near_one, near_two, near_three, asked, extra, feat, hot, picked, landed, dense, inputs, fills, filled, valid, sums,
    tile_one, tile_self, tile_two, tile_three, w_one, w_rows,
    j_one, j_two, j_three, pre_one, pre_two, hid_one, hid_two, cots, dpres, spread_two, below3, dpre_one,
    part_two, got_two, part_three, got_three,
    full, px_send, px_recv, blk, rr, line, thin, last, move_send, move_recv,
    load_sem, in_send, in_recv, cn_ssem, cn_rsem, ag1_send, ag1_recv, agd_send, agd_recv,
    cot_ssem, cot_rsem, wz_ssem, wz_rsem, wp_ssem, wp_rsem, ws_ssem, ws_rsem,
    rs_ssem, rs_rsem, px_ssem, px_rsem, rr_ssem, rr_rsem, ls_ssem, ls_rsem, mv_ssem, mv_rsem,
):
    devices = stores * groups
    z = lax.axis_index("store")
    t = lax.axis_index("trainer")
    me = z * groups + t
    chip, core = t // 2, lax.rem(t, 2)
    chips = groups // 2
    sibling = t + 1 - 2 * core
    right, left, across = (lax.rem(z + k, stores) for k in (1, 3, 2))
    others = ((across, 2), (right, 0), (left, 1))
    width = cot.shape[1]
    seeds, mid, outer = cot.shape[0], near_two.shape[0], near_one.shape[0]
    kept = groups * slots
    cells = stores * kept
    fan = near_two_t.shape[0]
    pending = []

    def remote(src, dst, send_sem, recv_sem, store, trainer):
        return pltpu.make_async_remote_copy(
            src_ref=src, dst_ref=dst, send_sem=send_sem, recv_sem=recv_sem,
            device_id=(store, trainer), device_id_type=MESH,
        )

    def await_bytes(ref, sem):
        pltpu.make_async_copy(ref, ref, sem).wait()

    barrier = pltpu.get_barrier_semaphore()

    def greet(index, carry):
        other = lax.rem(me + index, devices)
        pl.semaphore_signal(
            barrier, inc=1, device_id=(other // groups, lax.rem(other, groups)), device_id_type=MESH
        )
        return carry

    lax.fori_loop(1, devices, greet, 0)

    share = w_rows.shape[4]

    def piece_of(hbm, store):
        return hbm.at[pl.ds(pl.multiple_of(core * stores * width + store * width + chip * share, share), share), :]

    loads = [pltpu.make_async_copy(feat_hbm, feat, load_sem.at[0])]
    for place, hbm in enumerate((two_hbm, three_hbm)):
        loads.append(pltpu.make_async_copy(piece_of(hbm, z), w_rows.at[place, core, chip, z], load_sem.at[1 + place]))
    loads.append(pltpu.make_async_copy(cot, cots.at[z], load_sem.at[3]))
    for store in range(stores):
        for half in range(2):
            loads.append(
                pltpu.make_async_copy(
                    one_hbm.at[pl.ds((half * stores + store) * width, width), :],
                    w_one.at[store, pl.ds(half * width, width), :],
                    load_sem.at[4 + store * 2 + half],
                )
            )
    for load in loads:
        load.start()

    slot = lax.broadcasted_iota(jnp.int32, (SLOT, groups), 0)
    amounts = jnp.broadcast_to(sizes[...], (SLOT, groups))
    wanted = jnp.concatenate([sent[index] for index in range(slots)] + [jnp.full((SLOT - slots, groups), -1, jnp.int32)], axis=0)
    wanted = jnp.where(slot < amounts, wanted, -1)
    notes = jnp.where(slot == slots, amounts, 0).astype(F32)
    for group in range(groups):
        here = pl.ds(group * SLOT, SLOT)
        extra[here, :] = jnp.broadcast_to(notes[:, group : group + 1], (SLOT, extra.shape[1]))
        asked[here, :] = jnp.broadcast_to(wanted[:, group : group + 1], (SLOT, SLOT))
    count_matches(asked, [([0], hot)], groups * SLOT, feat.shape[0])
    loads[0].wait()
    pl.semaphore_wait(barrier, devices - 1)

    for store, place in others:
        remote(cot, cots.at[z], cot_ssem.at[place], cot_rsem.at[place], store, t).start()
        pending.append(lambda place=place: await_bytes(cot, cot_ssem.at[place]))
        for number, hbm in enumerate((two_hbm, three_hbm)):
            spot = w_rows.at[number, core, chip, z]
            remote(piece_of(hbm, store), spot, wz_ssem.at[number, place], wz_rsem.at[number, place], store, t).start()
            pending.append(lambda number=number, place=place, spot=spot: await_bytes(spot, wz_ssem.at[number, place]))

    def fetch(quarter, carry):
        columns = pl.ds(pl.multiple_of(quarter * width, width), width)
        rows = step_of(groups * SLOT, 256)
        for start in range(0, groups * SLOT, rows):
            part = dot(hot[start : start + rows, :], feat[:, columns])
            counts = jnp.concatenate([extra[start : start + rows, :]] * (width // extra.shape[1]), axis=1)
            picked[quarter, start : start + rows, :] = (part + counts).astype(BF16)

        def send(number, inner):
            trainer = lax.rem(t + number * 13, groups)
            remote(
                picked.at[quarter, rows_at(trainer, SLOT), :], landed.at[quarter, rows_at(t, SLOT), :],
                in_send.at[quarter], in_recv.at[quarter], z, trainer,
            ).start()
            return inner

        lax.fori_loop(1, groups, send, 0)
        pltpu.make_async_copy(
            picked.at[quarter, rows_at(t, SLOT), :], landed.at[quarter, rows_at(t, SLOT), :], in_recv.at[quarter]
        ).start()
        return carry

    lax.fori_loop(0, stores, fetch, 0)

    def leave_blocks():
        for quarter in range(stores):
            await_bytes(picked.at[quarter, pl.ds(0, (groups - 1) * SLOT), :], in_send.at[quarter])

    pending.append(leave_blocks)

    def moved(index):
        return index + (SLOT - slots) * ((index * ((1 << 19) // slots + 1)) >> 19)

    from_row = moved(lax.broadcasted_iota(jnp.int32, (kept, 1), 0))
    place = lax.broadcasted_iota(jnp.int32, (kept, groups * SLOT), 1)
    dense[...] = jnp.where(from_row == place, 1.0, 0.0).astype(BF16)
    ring_one = lambda source, index: inputs.at[index, pl.ds(pl.multiple_of(source * kept, kept), kept), :]

    def start_gather(piece_at, index, send_sem, recv_sem):
        piece = piece_at(z, index)
        remote(piece, piece, send_sem.at[0, index], recv_sem.at[0, index], right, t).start()
        remote(piece, piece, send_sem.at[1, index], recv_sem.at[1, index], left, t).start()

    def take_gather(piece_at, chunks, send_sem, recv_sem, near, far, between):
        for index in range(chunks):
            for side_at, (source, onward) in enumerate(((left, right), (right, left))):
                piece = piece_at(source, index)
                await_bytes(piece, recv_sem.at[side_at, index])
                if index % 2 == side_at:
                    remote(piece, piece, send_sem.at[2, index], recv_sem.at[2, index], onward, t).start()
            near(index)
        between()
        for index in range(chunks):
            await_bytes(piece_at(across, index), recv_sem.at[2, index])
            far(index)
        for way in range(3):
            for index in range(chunks):
                pending.append(
                    lambda way=way, index=index: await_bytes(piece_at(z, index), send_sem.at[way, index])
                )

    def pass_inputs(quarter):
        await_bytes(landed.at[quarter], in_recv.at[quarter])
        inputs[quarter, pl.ds(pl.multiple_of(z * kept, kept), kept), :] = dot(dense[...], landed[quarter]).astype(BF16)
        start_gather(ring_one, quarter, ag1_send, ag1_recv)

    pass_inputs(0)
    owner = lax.broadcasted_iota(jnp.int32, (groups, 1), 0)
    place = lax.broadcasted_iota(jnp.int32, (groups, groups * SLOT), 1)
    note = jnp.where(owner * SLOT + slots == place, 1.0, 0.0).astype(BF16)
    fills[z] = dot(note, landed[0, :, 0 : fills.shape[2]]).astype(BF16)
    for store, place in others:
        remote(fills.at[z], fills.at[z], cn_ssem.at[place], cn_rsem.at[place], store, t).start()
        pending.append(lambda place=place: await_bytes(fills.at[z], cn_ssem.at[place]))
    pass_inputs(1)
    for load in loads[1:]:
        load.wait()

    def upright(near, degree, own, dst):
        rows = near.shape[1]
        place = lax.broadcasted_iota(jnp.int32, (fan, rows), 0)
        parts = [jnp.where(place < degree[...][None, :], near, -1)] + own
        parts.append(jnp.full((SLOT - fan - len(own), rows), -1, jnp.int32))
        dst[...] = jnp.concatenate(parts, axis=0).T

    upright(near_one_t[...], degree_one, [self_ids[...][None, :]], near_one)
    upright(near_two_t[...], degree_two, [], near_two)
    upright(near_three_t[...], degree_three, [], near_three)
    slots_used = list(range(fan))
    count_matches(near_one, [(slots_used, tile_one), ([fan], tile_self)], outer, cells)
    count_matches(near_two, [(slots_used, tile_two)], mid, outer)
    count_matches(near_three, [(slots_used, tile_three)], seeds, mid)
    for quarter in range(2, stores):
        pass_inputs(quarter)

    def counted(near):
        return 1.0 + jnp.sum(jnp.where(near[...] >= 0, 1.0, 0.0), axis=1, keepdims=True)

    def spread_below(total, near, tile):
        rows = near.shape[0]
        scaled = (total[:, width:] / counted(near)).astype(BF16)
        below = dot(tile[...], scaled, 0, 0)
        upper = below[:rows] + (total[:, :width] + scaled.astype(F32))
        return jnp.concatenate([upper, below[rows:]], axis=0)

    for number in range(2):
        for store, place in others:
            await_bytes(w_rows.at[number, core, chip, store], wz_rsem.at[number, place])

        def pass_on(index, carry, number=number):
            target = lax.rem(chip + index, chips)
            spot = w_rows.at[number, core, chip]
            remote(spot, spot, wp_ssem.at[number], wp_rsem.at[number], z, target * 2 + core).start()
            return carry

        lax.fori_loop(1, chips, pass_on, 0)
        pending.append(lambda number=number: await_bytes(w_rows.at[number, core, pl.ds(0, chips - 1)], wp_ssem.at[number]))

    def note_filled():
        for store, place in others:
            await_bytes(fills.at[store], cn_rsem.at[place])
        row = lax.broadcasted_iota(jnp.int32, (kept, 1), 0)
        owner = (row * ((1 << 19) // slots + 1)) >> 19
        place = lax.broadcasted_iota(jnp.int32, (kept, groups), 1)
        pick = jnp.where(owner == place, 1.0, 0.0).astype(BF16)
        spot = (row - owner * slots).astype(F32)
        for store in range(stores):
            amount = dot(pick, fills[store])
            filled[store * kept : (store + 1) * kept, :] = jnp.where(spot < amount, 1.0, 0.0).astype(BF16)
        valid[...] = 1.0 + dot(tile_one[...], filled[...])

    rows_one = outer // 2

    def plane_part(tile, here, quarter, store):
        spot = pl.ds(pl.multiple_of(store * kept, kept), kept)
        return dot(tile[here, spot], inputs[quarter, spot, :])

    def start_sums(quarter):
        def body(index, carry):
            here = rows_at(index, rows_one)
            for place, tile in enumerate((tile_self, tile_one)):
                sums[quarter, place, here, :] = (
                    plane_part(tile, here, quarter, z)
                    + plane_part(tile, here, quarter, left)
                    + plane_part(tile, here, quarter, right)
                )
            return carry

        lax.fori_loop(0, 2, body, 0)

    def layer_one(quarter):
        def body(index, carry):
            here = rows_at(index, rows_one)
            own = sums[quarter, 0, here, :] + plane_part(tile_self, here, quarter, across)
            total = own + (sums[quarter, 1, here, :] + plane_part(tile_one, here, quarter, across))
            mean = total / jnp.concatenate([valid[here, :]] * (width // valid.shape[1]), axis=1)
            j_one[quarter, here, :] = jnp.concatenate([own, mean], axis=1).astype(BF16)
            part = dot(j_one[quarter, here, :], w_one[quarter])
            pre_one[here, :] = part if quarter == 0 else pre_one[here, :] + part
            return carry

        lax.fori_loop(0, 2, body, 0)

    def swap_weights():
        for number in range(2):
            spot = w_rows.at[number, core]
            await_bytes(w_rows.at[number, core, pl.ds(0, chips - 1)], wp_rsem.at[number])
            remote(spot, spot, ws_ssem.at[number], ws_rsem.at[number], z, sibling).start()
            pending.append(lambda spot=spot, number=number: await_bytes(spot, ws_ssem.at[number]))

    def before_sums():
        swap_weights()
        note_filled()

    take_gather(ring_one, stores, ag1_send, ag1_recv, start_sums, layer_one, before_sums)
    hid_one[...] = (pre_one[...] * jax.nn.sigmoid(pre_one[...])).astype(BF16)
    for number in range(2):
        await_bytes(w_rows.at[number, 1 - core], ws_rsem.at[number])

    def rows_of(number, store):
        return w_rows[number, :, :, store].reshape(2 * width, width)

    def join(hidden, near, tile, joined):
        rows = near.shape[0]
        own = hidden[0:rows, :]
        mean = (own.astype(F32) + dot(tile[...], hidden[...])) / counted(near)
        joined[...] = jnp.concatenate([own, mean.astype(BF16)], axis=1)

    def send_partials(joined, number, part, got, chunks):
        rows = part.shape[1] // chunks
        for index in range(chunks):
            here = pl.ds(index * rows, rows)
            for store, place in others:
                part[place, here, :] = dot(joined[here, :], rows_of(number, store)).astype(BF16)
                sems = rs_ssem.at[number, index, place], rs_rsem.at[number, index, place]
                remote(part.at[place, here, :], got.at[place, here, :], *sems, store, t).start()
                pending.append(lambda place=place, here=here, sem=sems[0]: await_bytes(part.at[place, here, :], sem))

    def take_partials(joined, number, got, index, rows, places):
        here = pl.ds(index * rows, rows)
        total = dot(joined[here, :], rows_of(number, z))
        for place in range(places):
            await_bytes(got.at[place, here, :], rs_rsem.at[number, index, place])
            total = total + got[place, here, :].astype(F32)
        return total

    def send_by(index, place, store):
        here = pl.ds(index * rows_two, rows_two)
        sems = rs_ssem.at[0, index, place], rs_rsem.at[0, index, place]
        remote(part_two.at[place, here, :], got_two.at[place, here, :], *sems, store, t).start()
        pending.append(lambda: await_bytes(part_two.at[place, here, :], sems[0]))

    def start_ring():
        for index in range(chunks_two):
            here = pl.ds(index * rows_two, rows_two)
            part_two[2, here, :] = dot(j_two[here, :], rows_of(0, across)).astype(BF16)
            send_by(index, 2, (right, left)[index % 2])
        for index in range(chunks_two):
            here = pl.ds(index * rows_two, rows_two)
            place = 1 - index % 2
            store = (right, left)[place]
            part_two[place, here, :] = dot(j_two[here, :], rows_of(0, store)).astype(BF16)
            send_by(index, place, store)

    def close_ring():
        for index in range(chunks_two):
            here = pl.ds(index * rows_two, rows_two)
            place = index % 2
            store = (right, left)[place]
            total = dot(j_two[here, :], rows_of(0, store))
            await_bytes(got_two.at[2, here, :], rs_rsem.at[0, index, 2])
            part_two[place, here, :] = (total + got_two[2, here, :].astype(F32)).astype(BF16)
            send_by(index, place, store)

    join(hid_one, near_two, tile_two, j_two)
    chunks_two = agd_send.shape[1]
    rows_two = mid // chunks_two
    ring_two = lambda source, index: dpres.at[source, rows_at(index, rows_two), :]
    start_ring()
    for store, place in others:
        await_bytes(cots.at[store], cot_rsem.at[place])
    spread = dot(cots[0], rows_of(1, 0), 1, 1)
    for store in range(1, stores):
        spread = spread + dot(cots[store], rows_of(1, store), 1, 1)
    below3[...] = spread_below(spread, near_three, tile_three)
    close_ring()
    for index in range(chunks_two):
        here = rows_at(index, rows_two)
        pre_two[here, :] = take_partials(j_two, 0, got_two, index, rows_two, 2)
        dpres[z, here, :] = (below3[here, :] * slope(pre_two[here, :])).astype(BF16)
        start_gather(ring_two, index, agd_send, agd_recv)
    hid_two[...] = (pre_two[...] * jax.nn.sigmoid(pre_two[...])).astype(BF16)
    join(hid_two, near_three, tile_three, j_three)

    height = full.shape[2]
    per_slice = width // height

    def pass_over(number, first, amount):
        spot = pl.ds(first, amount)
        remote(
            px_send.at[number, spot], px_recv.at[number, spot], px_ssem.at[number], px_rsem.at[number], z, sibling
        ).start()

    def left_over(number):
        pending.append(lambda: await_bytes(px_send.at[number], px_ssem.at[number]))

    pairs = per_slice // 2 if per_slice % 2 == 0 else 0

    def grad_of_columns(number, joined, dpre):
        def products(store, carry):
            part = dot(joined[store], dpre[...], 0, 0)
            for half in range(2):
                for index in range(per_slice):
                    start = half * width + index * height
                    full[number, half * (groups // 2) + store * per_slice + index] = part[start : start + height, :]
            for half in range(2):
                for index in range(pairs):
                    block = half * (groups // 2) + store * per_slice + 2 * index + 1 - core
                    px_send[number, store * per_slice + half * pairs + index] = full[number, block].astype(BF16)
            if pairs:
                pass_over(number, store * per_slice, per_slice)
            return carry

        lax.fori_loop(0, stores, products, 0)
        if not pairs:
            for index in range(chips):
                px_send[number, index] = full[number, index * 2 + 1 - core].astype(BF16)
            pass_over(number, 0, chips)
        left_over(number)

    def column_slot(index):
        if not pairs:
            return index
        half, rest = index // (chips // 2), lax.rem(index, chips // 2)
        return rest // pairs * per_slice + half * pairs + lax.rem(rest, pairs)

    def grad_of_rows(number, joined, columns, store):
        part = dot(joined[...], columns[store], 0, 0)
        passed = lax.rem(store, 2) != core
        first = store // 2 * 2 * per_slice

        @pl.when(passed)
        def _():
            for index in range(2 * per_slice):
                px_send[number, first + index] = part[index * height : (index + 1) * height, :].astype(BF16)
            pass_over(number, first, 2 * per_slice)

        @pl.when(jnp.logical_not(passed))
        def _():
            for index in range(2 * per_slice):
                full[number, index * stores + store] = part[index * height : (index + 1) * height, :]

    def row_slot(index):
        return lax.rem(index, stores // 2) * 2 * per_slice + index // (stores // 2)

    side = rr.shape[2]
    place_x, place_y = chip // side, lax.rem(chip, side)
    spots = (place_x, place_y)

    def partner(way, index):
        target = lax.rem(spots[way] + index, side)
        column = (target, place_y) if way == 0 else (place_x, target)
        return target, (column[0] * side + column[1]) * 2 + core

    def share_first(number, slot_of):
        await_bytes(px_recv.at[number], px_rsem.at[number])

        def body(index, carry):
            total = full[number, index * 2 + core] + px_recv[number, slot_of(index)].astype(F32)
            first, second = index // side, lax.rem(index, side)
            blk[number, 0, first, second] = total[: height // 2].astype(BF16)
            blk[number, 1, second, first] = total[height // 2 :].astype(BF16)
            return carry

        lax.fori_loop(0, chips, body, 0)
        for way in range(2):
            for index in range(1, side):
                target, trainer = partner(way, index)
                remote(
                    blk.at[number, way, target], rr.at[number, way, index],
                    rr_ssem.at[number, way, index], rr_rsem.at[number, way, index], z, trainer,
                ).start()
                pending.append(
                    lambda way=way, index=index, target=target: await_bytes(
                        blk.at[number, way, target], rr_ssem.at[number, way, index]
                    )
                )

    def share_second(number):
        for way in range(2):
            total = blk[number, way, spots[way]].astype(F32)
            for index in range(1, side):
                await_bytes(rr.at[number, way, index], rr_rsem.at[number, way, index])
                total = total + rr[number, way, index].astype(F32)
            line[number, way] = total
            thin[number, way] = total.astype(BF16)
            for index in range(1, side):
                target, trainer = partner(1 - way, index)
                remote(
                    thin.at[number, way, target], last.at[number, way, index],
                    ls_ssem.at[number, way, index], ls_rsem.at[number, way, index], z, trainer,
                ).start()
                pending.append(
                    lambda way=way, index=index, target=target: await_bytes(
                        thin.at[number, way, target], ls_ssem.at[number, way, index]
                    )
                )

    def summed(number):
        halves = []
        for way in range(2):
            total = line[number, way, spots[1 - way]]
            for index in range(1, side):
                await_bytes(last.at[number, way, index], ls_rsem.at[number, way, index])
                total = total + last[number, way, index].astype(F32)
            halves.append(total)
        return jnp.concatenate(halves, axis=0)

    block, to_store = t // stores, lax.rem(t, stores)
    to_trainer = jnp.where(
        block < per_slice, z * per_slice + block, groups // 2 + z * per_slice + block - per_slice
    )
    moves = jnp.logical_or(to_store != z, to_trainer != t)

    def move(number):
        move_send[number] = summed(number).astype(BF16)
        sems = mv_ssem.at[number], mv_rsem.at[number]

        @pl.when(moves)
        def _():
            remote(move_send.at[number], move_recv.at[number], *sems, to_store, to_trainer).start()

        @pl.when(jnp.logical_not(moves))
        def _():
            pltpu.make_async_copy(move_send.at[number], move_recv.at[number], mv_rsem.at[number]).start()

        def leave():
            @pl.when(moves)
            def _():
                await_bytes(move_send.at[number], mv_ssem.at[number])

        pending.append(leave)

    def take_move(number, out):
        await_bytes(move_recv.at[number], mv_rsem.at[number])
        out[...] = move_recv[number].astype(F32)

    for turn in range(stores):
        grad_of_rows(1, j_three, cots, lax.rem(core + 1 + turn * 2 + turn // 2, stores))
    left_over(1)

    def spread_part(here, source):
        return dot(dpres[source, here, :], rows_of(0, source), 1, 1)

    def near_two_spread(index):
        here = rows_at(index, rows_two)
        spread_two[here, :] = spread_part(here, z) + spread_part(here, left) + spread_part(here, right)

    def far_two_spread(index):
        here = rows_at(index, rows_two)
        spread_two[here, :] += spread_part(here, across)

    def meanwhile():
        share_first(1, row_slot)
        for store in (left, right, z):
            grad_of_rows(0, j_two, dpres, store)

    take_gather(ring_two, chunks_two, agd_send, agd_recv, near_two_spread, far_two_spread, meanwhile)
    grad_of_rows(0, j_two, dpres, across)
    left_over(0)
    below2 = spread_below(spread_two[...], near_two, tile_two)
    dpre_one[...] = (below2 * slope(pre_one[...])).astype(BF16)
    early = list(pending)
    pending.clear()
    share_first(0, row_slot)
    grad_of_columns(2, j_one, dpre_one)
    share_second(1)
    send_partials(j_three, 1, part_three, got_three, 1)
    share_first(2, column_slot)
    share_second(0)
    move(1)
    move(0)
    for leave in early:
        leave()
    share_second(2)
    take_move(1, three_out)
    take_move(0, two_out)
    emb_out[...] = take_partials(j_three, 1, got_three, 0, seeds, 3).astype(BF16)
    one_out[...] = summed(2)

    for leave in pending:
        leave()


def copies(*refs):
    half = len(refs) // 2
    for source, target in zip(refs[:half], refs[half:]):
        target[...] = source[...]


def run(
    stores, groups, features, sent_ids, block_sizes, self_ids, near_one, degree_one, near_two, degree_two,
    near_three, degree_three, weight_one, weight_two, weight_three, cotangent,
):
    slots = sent_ids.shape[2]
    outer, mid, seeds = near_one.shape[0], near_two.shape[0], near_three.shape[0]
    fan = near_one.shape[1]
    fwidth = features.shape[1]
    width = cotangent.shape[1]
    devices = stores * groups
    cells = devices * slots
    height = 2 * fwidth // groups

    vmem = pl.BlockSpec(memory_space=pltpu.VMEM)
    hbm = pl.BlockSpec(memory_space=pl.ANY)
    lanes = min(128, width)
    chunks_two = 4
    dma = pltpu.SemaphoreType.DMA
    chips = groups // 2
    side = math.isqrt(chips)
    scratch = [pltpu.VMEM((rows, SLOT), jnp.int32) for rows in (outer, mid, seeds, groups * SLOT)]
    scratch += [
        pltpu.VMEM((groups * SLOT, lanes), F32),
        pltpu.VMEM(features.shape, BF16),
        pltpu.VMEM((groups * SLOT, features.shape[0]), BF16),
        pltpu.VMEM((stores, groups * SLOT, width), BF16),
        pltpu.VMEM((stores, groups * SLOT, width), BF16),
        pltpu.VMEM((groups * slots, groups * SLOT), BF16),
        pltpu.VMEM((stores, cells, width), BF16),
        pltpu.VMEM((stores, groups, lanes), BF16),
        pltpu.VMEM((cells, lanes), BF16),
        pltpu.VMEM((outer, lanes), F32),
        pltpu.VMEM((stores, 2, outer, width), F32),
        pltpu.VMEM((outer, cells), BF16),
        pltpu.VMEM((outer, cells), BF16),
        pltpu.VMEM((mid, outer), BF16),
        pltpu.VMEM((seeds, mid), BF16),
        pltpu.VMEM((stores, 2 * width, width), BF16),
        pltpu.VMEM((2, 2, chips, stores, width // chips, width), BF16),
        pltpu.VMEM((stores, outer, 2 * width), BF16),
        pltpu.VMEM((mid, 2 * width), BF16),
        pltpu.VMEM((seeds, 2 * width), BF16),
        pltpu.VMEM((outer, width), F32),
        pltpu.VMEM((mid, width), F32),
        pltpu.VMEM((outer, width), BF16),
        pltpu.VMEM((mid, width), BF16),
        pltpu.VMEM((stores, seeds, width), BF16),
        pltpu.VMEM((stores, mid, width), BF16),
        pltpu.VMEM((mid, 2 * width), F32),
        pltpu.VMEM((mid, width), F32),
        pltpu.VMEM((outer, width), BF16),
    ]
    scratch += [pltpu.VMEM((3, mid, width), BF16)] * 2 + [pltpu.VMEM((3, seeds, width), BF16)] * 2
    scratch += [pltpu.VMEM((3, groups, height, width), F32)]
    scratch += [pltpu.VMEM((3, chips, height, width), BF16)] * 2
    scratch += [pltpu.VMEM((3, 2, side, side, height // 2, width), BF16)] * 2
    scratch += [pltpu.VMEM((3, 2, side, height // 2, width), kind) for kind in (F32, BF16, BF16)]
    scratch += [pltpu.VMEM((2, height, width), BF16)] * 2
    scratch += [dma((4 + 2 * stores,)), dma((stores,)), dma((stores,)), dma((3,)), dma((3,))]
    scratch += [dma((3, chunks)) for chunks in (stores, stores, chunks_two, chunks_two)]
    scratch += [dma((3,))] * 2 + [dma((2, 3))] * 2 + [dma((2,))] * 4 + [dma((2, chunks_two, 3))] * 2
    scratch += [dma((3,))] * 2 + [dma((3, 2, side))] * 4 + [dma((2,))] * 2
    shapes = (
        jax.ShapeDtypeStruct((seeds, width), BF16),
        jax.ShapeDtypeStruct((height, width), F32),
        jax.ShapeDtypeStruct((height, width), F32),
        jax.ShapeDtypeStruct((height, width), F32),
    )
    results = pl.pallas_call(
        functools.partial(kernel, stores, groups, slots),
        out_shape=shapes,
        in_specs=[vmem] * 10 + [hbm] * 4,
        out_specs=(vmem,) * 4,
        scratch_shapes=scratch,
        compiler_params=pltpu.CompilerParams(
            collective_id=0, has_side_effects=True, vmem_limit_bytes=60 * 1024 * 1024
        ),
    )(
        jnp.transpose(sent_ids, (2, 0, 1)), block_sizes, self_ids,
        near_one.T, degree_one, near_two.T, degree_two, near_three.T, degree_three,
        cotangent, features, weight_one, weight_two, weight_three,
    )
    return pl.pallas_call(copies, out_shape=shapes, in_specs=[vmem] * 4, out_specs=(vmem,) * 4)(*results)


def solution(mesh):
    stores, groups = mesh.shape["store"], mesh.shape["trainer"]
    both = ("store", "trainer")
    placed = (
        P(both, None), P(both, None, None), P(both, None), P("trainer"), P("trainer", None), P("trainer"),
        P("trainer", None), P("trainer"), P("trainer", None), P("trainer"),
        P(None, "store"), P(None, "store"), P(None, "store"), P("trainer", "store"),
    )
    return jax.shard_map(
        functools.partial(run, stores, groups),
        mesh=mesh, in_specs=placed, out_specs=(P("trainer", "store"),) * 4, check_vma=False,
    )
```

```python
import functools
import math

import jax
import jax.numpy as jnp
from jax import lax
from jax.experimental import pallas as pl
from jax.experimental.pallas import tpu as pltpu
from jax.sharding import PartitionSpec as P

MESH = pl.DeviceIdType.MESH
F32 = jnp.float32
BF16 = jnp.bfloat16
SLOT = 16


def dot(a, b, left=1, right=0):
    return lax.dot_general(a, b, (((left,), (right,)), ((), ())), preferred_element_type=F32)


def slope(preact):
    sigma = jax.nn.sigmoid(preact)
    return sigma * (1.0 + preact * (1.0 - sigma))


def rows_at(index, size):
    return pl.ds(pl.multiple_of(index * size, size), size)


def step_of(rows, most):
    size = min(rows, most)
    while rows % size:
        size -= 1
    return size


def count_matches(ids, wanted, rows, width):
    high = step_of(rows, 128)
    wide = step_of(width, 256)

    def body(index, carry):
        here = rows_at(index, high)
        part = ids[here, :].astype(jnp.int16)
        for start in range(0, width, wide):
            place = (lax.broadcasted_iota(jnp.int32, (high, wide), 1) + start).astype(jnp.int16)
            for column_list, dst in wanted:
                total = None
                for column in column_list:
                    found = jnp.where(part[:, column : column + 1] == place, BF16(1), BF16(0))
                    total = found if total is None else total + found
                dst[here, start : start + wide] = total
        return carry

    lax.fori_loop(0, rows // high, body, 0)


def kernel(
    stores, groups, slots,
    sent, sizes, self_ids, near_one_t, degree_one, near_two_t, degree_two, near_three_t, degree_three,
    cot, feat_hbm, one_hbm, two_hbm, three_hbm,
    emb_out, one_out, two_out, three_out,
    near_one, near_two, near_three, asked, extra, feat, hot, picked, landed, dense, inputs, fills, filled, valid, sums,
    tile_one, tile_self, tile_two, tile_three, w_one, w_rows,
    j_one, j_two, j_three, pre_one, pre_two, hid_one, hid_two, cots, dpres, spread_two, below3, dpre_one,
    part_two, got_two, part_three, got_three,
    full, px_send, px_recv, blk, rr, line, thin, last, move_send, move_recv,
    load_sem, in_send, in_recv, cn_ssem, cn_rsem, ag1_send, ag1_recv, agd_send, agd_recv,
    cot_ssem, cot_rsem, wz_ssem, wz_rsem, wp_ssem, wp_rsem, ws_ssem, ws_rsem,
    rs_ssem, rs_rsem, px_ssem, px_rsem, rr_ssem, rr_rsem, ls_ssem, ls_rsem, mv_ssem, mv_rsem,
):
    devices = stores * groups
    z = lax.axis_index("store")
    t = lax.axis_index("trainer")
    me = z * groups + t
    chip, core = t // 2, lax.rem(t, 2)
    chips = groups // 2
    sibling = t + 1 - 2 * core
    right, left, across = (lax.rem(z + k, stores) for k in (1, 3, 2))
    others = ((across, 2), (right, 0), (left, 1))
    width = cot.shape[1]
    seeds, mid, outer = cot.shape[0], near_two.shape[0], near_one.shape[0]
    kept = groups * slots
    cells = stores * kept
    fan = near_two_t.shape[0]
    pending = []

    def remote(src, dst, send_sem, recv_sem, store, trainer):
        return pltpu.make_async_remote_copy(
            src_ref=src, dst_ref=dst, send_sem=send_sem, recv_sem=recv_sem,
            device_id=(store, trainer), device_id_type=MESH,
        )

    def await_bytes(ref, sem):
        pltpu.make_async_copy(ref, ref, sem).wait()

    barrier = pltpu.get_barrier_semaphore()

    def greet(index, carry):
        other = lax.rem(me + index, devices)
        pl.semaphore_signal(
            barrier, inc=1, device_id=(other // groups, lax.rem(other, groups)), device_id_type=MESH
        )
        return carry

    lax.fori_loop(1, devices, greet, 0)

    share = w_rows.shape[4]

    def piece_of(hbm, store):
        return hbm.at[pl.ds(pl.multiple_of(core * stores * width + store * width + chip * share, share), share), :]

    loads = [pltpu.make_async_copy(feat_hbm, feat, load_sem.at[0])]
    for place, hbm in enumerate((two_hbm, three_hbm)):
        loads.append(pltpu.make_async_copy(piece_of(hbm, z), w_rows.at[place, core, chip, z], load_sem.at[1 + place]))
    loads.append(pltpu.make_async_copy(cot, cots.at[z], load_sem.at[3]))
    for store in range(stores):
        for half in range(2):
            loads.append(
                pltpu.make_async_copy(
                    one_hbm.at[pl.ds((half * stores + store) * width, width), :],
                    w_one.at[store, pl.ds(half * width, width), :],
                    load_sem.at[4 + store * 2 + half],
                )
            )
    for load in loads:
        load.start()

    slot = lax.broadcasted_iota(jnp.int32, (SLOT, groups), 0)
    amounts = jnp.broadcast_to(sizes[...], (SLOT, groups))
    wanted = jnp.concatenate([sent[index] for index in range(slots)] + [jnp.full((SLOT - slots, groups), -1, jnp.int32)], axis=0)
    wanted = jnp.where(slot < amounts, wanted, -1)
    notes = jnp.where(slot == slots, amounts, 0).astype(F32)
    for group in range(groups):
        here = pl.ds(group * SLOT, SLOT)
        extra[here, :] = jnp.broadcast_to(notes[:, group : group + 1], (SLOT, extra.shape[1]))
        asked[here, :] = jnp.broadcast_to(wanted[:, group : group + 1], (SLOT, SLOT))
    count_matches(asked, [([0], hot)], groups * SLOT, feat.shape[0])
    loads[0].wait()
    pl.semaphore_wait(barrier, devices - 1)

    for store, place in others:
        remote(cot, cots.at[z], cot_ssem.at[place], cot_rsem.at[place], store, t).start()
        pending.append(lambda place=place: await_bytes(cot, cot_ssem.at[place]))
        for number, hbm in enumerate((two_hbm, three_hbm)):
            spot = w_rows.at[number, core, chip, z]
            remote(piece_of(hbm, store), spot, wz_ssem.at[number, place], wz_rsem.at[number, place], store, t).start()
            pending.append(lambda number=number, place=place, spot=spot: await_bytes(spot, wz_ssem.at[number, place]))

    def fetch(quarter, carry):
        columns = pl.ds(pl.multiple_of(quarter * width, width), width)
        rows = step_of(groups * SLOT, 256)
        for start in range(0, groups * SLOT, rows):
            part = dot(hot[start : start + rows, :], feat[:, columns])
            counts = jnp.concatenate([extra[start : start + rows, :]] * (width // extra.shape[1]), axis=1)
            picked[quarter, start : start + rows, :] = (part + counts).astype(BF16)

        def send(number, inner):
            trainer = lax.rem(t + number * 13, groups)
            remote(
                picked.at[quarter, rows_at(trainer, SLOT), :], landed.at[quarter, rows_at(t, SLOT), :],
                in_send.at[quarter], in_recv.at[quarter], z, trainer,
            ).start()
            return inner

        lax.fori_loop(1, groups, send, 0)
        pltpu.make_async_copy(
            picked.at[quarter, rows_at(t, SLOT), :], landed.at[quarter, rows_at(t, SLOT), :], in_recv.at[quarter]
        ).start()
        return carry

    lax.fori_loop(0, stores, fetch, 0)

    def leave_blocks():
        for quarter in range(stores):
            await_bytes(picked.at[quarter, pl.ds(0, (groups - 1) * SLOT), :], in_send.at[quarter])

    pending.append(leave_blocks)

    def moved(index):
        return index + (SLOT - slots) * ((index * ((1 << 19) // slots + 1)) >> 19)

    from_row = moved(lax.broadcasted_iota(jnp.int32, (kept, 1), 0))
    place = lax.broadcasted_iota(jnp.int32, (kept, groups * SLOT), 1)
    dense[...] = jnp.where(from_row == place, 1.0, 0.0).astype(BF16)
    ring_one = lambda source, index: inputs.at[index, pl.ds(pl.multiple_of(source * kept, kept), kept), :]

    def start_gather(piece_at, index, send_sem, recv_sem):
        piece = piece_at(z, index)
        remote(piece, piece, send_sem.at[0, index], recv_sem.at[0, index], right, t).start()
        remote(piece, piece, send_sem.at[1, index], recv_sem.at[1, index], left, t).start()

    def take_gather(piece_at, chunks, send_sem, recv_sem, near, far, between):
        for index in range(chunks):
            for side_at, (source, onward) in enumerate(((left, right), (right, left))):
                piece = piece_at(source, index)
                await_bytes(piece, recv_sem.at[side_at, index])
                if index % 2 == side_at:
                    remote(piece, piece, send_sem.at[2, index], recv_sem.at[2, index], onward, t).start()
            near(index)
        between()
        for index in range(chunks):
            await_bytes(piece_at(across, index), recv_sem.at[2, index])
            far(index)
        for way in range(3):
            for index in range(chunks):
                pending.append(
                    lambda way=way, index=index: await_bytes(piece_at(z, index), send_sem.at[way, index])
                )

    def pass_inputs(quarter):
        await_bytes(landed.at[quarter], in_recv.at[quarter])
        inputs[quarter, pl.ds(pl.multiple_of(z * kept, kept), kept), :] = dot(dense[...], landed[quarter]).astype(BF16)
        start_gather(ring_one, quarter, ag1_send, ag1_recv)

    pass_inputs(0)
    owner = lax.broadcasted_iota(jnp.int32, (groups, 1), 0)
    place = lax.broadcasted_iota(jnp.int32, (groups, groups * SLOT), 1)
    note = jnp.where(owner * SLOT + slots == place, 1.0, 0.0).astype(BF16)
    fills[z] = dot(note, landed[0, :, 0 : fills.shape[2]]).astype(BF16)
    for store, place in others:
        remote(fills.at[z], fills.at[z], cn_ssem.at[place], cn_rsem.at[place], store, t).start()
        pending.append(lambda place=place: await_bytes(fills.at[z], cn_ssem.at[place]))
    pass_inputs(1)
    for load in loads[1:]:
        load.wait()

    def upright(near, degree, own, dst):
        rows = near.shape[1]
        place = lax.broadcasted_iota(jnp.int32, (fan, rows), 0)
        parts = [jnp.where(place < degree[...][None, :], near, -1)] + own
        parts.append(jnp.full((SLOT - fan - len(own), rows), -1, jnp.int32))
        dst[...] = jnp.concatenate(parts, axis=0).T

    upright(near_one_t[...], degree_one, [self_ids[...][None, :]], near_one)
    upright(near_two_t[...], degree_two, [], near_two)
    upright(near_three_t[...], degree_three, [], near_three)
    slots_used = list(range(fan))
    count_matches(near_one, [(slots_used, tile_one), ([fan], tile_self)], outer, cells)
    count_matches(near_two, [(slots_used, tile_two)], mid, outer)
    count_matches(near_three, [(slots_used, tile_three)], seeds, mid)
    for quarter in range(2, stores):
        pass_inputs(quarter)

    def counted(near):
        return 1.0 + jnp.sum(jnp.where(near[...] >= 0, 1.0, 0.0), axis=1, keepdims=True)

    def spread_below(total, near, tile):
        rows = near.shape[0]
        scaled = (total[:, width:] / counted(near)).astype(BF16)
        below = dot(tile[...], scaled, 0, 0)
        upper = below[:rows] + (total[:, :width] + scaled.astype(F32))
        return jnp.concatenate([upper, below[rows:]], axis=0)

    for number in range(2):
        for store, place in others:
            await_bytes(w_rows.at[number, core, chip, store], wz_rsem.at[number, place])

        def pass_on(index, carry, number=number):
            target = lax.rem(chip + index, chips)
            spot = w_rows.at[number, core, chip]
            remote(spot, spot, wp_ssem.at[number], wp_rsem.at[number], z, target * 2 + core).start()
            return carry

        lax.fori_loop(1, chips, pass_on, 0)
        pending.append(lambda number=number: await_bytes(w_rows.at[number, core, pl.ds(0, chips - 1)], wp_ssem.at[number]))

    def note_filled():
        for store, place in others:
            await_bytes(fills.at[store], cn_rsem.at[place])
        row = lax.broadcasted_iota(jnp.int32, (kept, 1), 0)
        owner = (row * ((1 << 19) // slots + 1)) >> 19
        place = lax.broadcasted_iota(jnp.int32, (kept, groups), 1)
        pick = jnp.where(owner == place, 1.0, 0.0).astype(BF16)
        spot = (row - owner * slots).astype(F32)
        for store in range(stores):
            amount = dot(pick, fills[store])
            filled[store * kept : (store + 1) * kept, :] = jnp.where(spot < amount, 1.0, 0.0).astype(BF16)
        valid[...] = 1.0 + dot(tile_one[...], filled[...])

    rows_one = outer // 2

    def plane_part(tile, here, quarter, store):
        spot = pl.ds(pl.multiple_of(store * kept, kept), kept)
        return dot(tile[here, spot], inputs[quarter, spot, :])

    def start_sums(quarter):
        def body(index, carry):
            here = rows_at(index, rows_one)
            for place, tile in enumerate((tile_self, tile_one)):
                sums[quarter, place, here, :] = (
                    plane_part(tile, here, quarter, z)
                    + plane_part(tile, here, quarter, left)
                    + plane_part(tile, here, quarter, right)
                )
            return carry

        lax.fori_loop(0, 2, body, 0)

    def layer_one(quarter):
        def body(index, carry):
            here = rows_at(index, rows_one)
            own = sums[quarter, 0, here, :] + plane_part(tile_self, here, quarter, across)
            total = own + (sums[quarter, 1, here, :] + plane_part(tile_one, here, quarter, across))
            mean = total / jnp.concatenate([valid[here, :]] * (width // valid.shape[1]), axis=1)
            j_one[quarter, here, :] = jnp.concatenate([own, mean], axis=1).astype(BF16)
            part = dot(j_one[quarter, here, :], w_one[quarter])
            pre_one[here, :] = part if quarter == 0 else pre_one[here, :] + part
            return carry

        lax.fori_loop(0, 2, body, 0)

    def swap_weights():
        for number in range(2):
            spot = w_rows.at[number, core]
            await_bytes(w_rows.at[number, core, pl.ds(0, chips - 1)], wp_rsem.at[number])
            remote(spot, spot, ws_ssem.at[number], ws_rsem.at[number], z, sibling).start()
            pending.append(lambda spot=spot, number=number: await_bytes(spot, ws_ssem.at[number]))

    def before_sums():
        swap_weights()
        note_filled()

    take_gather(ring_one, stores, ag1_send, ag1_recv, start_sums, layer_one, before_sums)
    hid_one[...] = (pre_one[...] * jax.nn.sigmoid(pre_one[...])).astype(BF16)
    for number in range(2):
        await_bytes(w_rows.at[number, 1 - core], ws_rsem.at[number])

    def rows_of(number, store):
        return w_rows[number, :, :, store].reshape(2 * width, width)

    def join(hidden, near, tile, joined):
        rows = near.shape[0]
        own = hidden[0:rows, :]
        mean = (own.astype(F32) + dot(tile[...], hidden[...])) / counted(near)
        joined[...] = jnp.concatenate([own, mean.astype(BF16)], axis=1)

    def send_partials(joined, number, part, got, chunks):
        rows = part.shape[1] // chunks
        for index in range(chunks):
            here = pl.ds(index * rows, rows)
            for store, place in others:
                part[place, here, :] = dot(joined[here, :], rows_of(number, store)).astype(BF16)
                sems = rs_ssem.at[number, index, place], rs_rsem.at[number, index, place]
                remote(part.at[place, here, :], got.at[place, here, :], *sems, store, t).start()
                pending.append(lambda place=place, here=here, sem=sems[0]: await_bytes(part.at[place, here, :], sem))

    def take_partials(joined, number, got, index, rows, places):
        here = pl.ds(index * rows, rows)
        total = dot(joined[here, :], rows_of(number, z))
        for place in range(places):
            await_bytes(got.at[place, here, :], rs_rsem.at[number, index, place])
            total = total + got[place, here, :].astype(F32)
        return total

    def send_by(index, place, store):
        here = pl.ds(index * rows_two, rows_two)
        sems = rs_ssem.at[0, index, place], rs_rsem.at[0, index, place]
        remote(part_two.at[place, here, :], got_two.at[place, here, :], *sems, store, t).start()
        pending.append(lambda: await_bytes(part_two.at[place, here, :], sems[0]))

    def start_ring():
        for index in range(chunks_two):
            here = pl.ds(index * rows_two, rows_two)
            part_two[2, here, :] = dot(j_two[here, :], rows_of(0, across)).astype(BF16)
            send_by(index, 2, (right, left)[index % 2])
        for index in range(chunks_two):
            here = pl.ds(index * rows_two, rows_two)
            place = 1 - index % 2
            store = (right, left)[place]
            part_two[place, here, :] = dot(j_two[here, :], rows_of(0, store)).astype(BF16)
            send_by(index, place, store)

    def close_ring():
        for index in range(chunks_two):
            here = pl.ds(index * rows_two, rows_two)
            place = index % 2
            store = (right, left)[place]
            total = dot(j_two[here, :], rows_of(0, store))
            await_bytes(got_two.at[2, here, :], rs_rsem.at[0, index, 2])
            part_two[place, here, :] = (total + got_two[2, here, :].astype(F32)).astype(BF16)
            send_by(index, place, store)

    join(hid_one, near_two, tile_two, j_two)
    chunks_two = agd_send.shape[1]
    rows_two = mid // chunks_two
    ring_two = lambda source, index: dpres.at[source, rows_at(index, rows_two), :]
    start_ring()
    for store, place in others:
        await_bytes(cots.at[store], cot_rsem.at[place])
    spread = dot(cots[0], rows_of(1, 0), 1, 1)
    for store in range(1, stores):
        spread = spread + dot(cots[store], rows_of(1, store), 1, 1)
    below3[...] = spread_below(spread, near_three, tile_three)
    close_ring()
    for index in range(chunks_two):
        here = rows_at(index, rows_two)
        pre_two[here, :] = take_partials(j_two, 0, got_two, index, rows_two, 2)
        dpres[z, here, :] = (below3[here, :] * slope(pre_two[here, :])).astype(BF16)
        start_gather(ring_two, index, agd_send, agd_recv)
    hid_two[...] = (pre_two[...] * jax.nn.sigmoid(pre_two[...])).astype(BF16)
    join(hid_two, near_three, tile_three, j_three)

    height = full.shape[2]
    per_slice = width // height

    def pass_over(number, first, amount):
        spot = pl.ds(first, amount)
        remote(
            px_send.at[number, spot], px_recv.at[number, spot], px_ssem.at[number], px_rsem.at[number], z, sibling
        ).start()

    def left_over(number):
        pending.append(lambda: await_bytes(px_send.at[number], px_ssem.at[number]))

    pairs = per_slice // 2 if per_slice % 2 == 0 else 0

    def grad_of_columns(number, joined, dpre):
        def products(store, carry):
            part = dot(joined[store], dpre[...], 0, 0)
            for half in range(2):
                for index in range(per_slice):
                    start = half * width + index * height
                    full[number, half * (groups // 2) + store * per_slice + index] = part[start : start + height, :]
            for half in range(2):
                for index in range(pairs):
                    block = half * (groups // 2) + store * per_slice + 2 * index + 1 - core
                    px_send[number, store * per_slice + half * pairs + index] = full[number, block].astype(BF16)
            if pairs:
                pass_over(number, store * per_slice, per_slice)
            return carry

        lax.fori_loop(0, stores, products, 0)
        if not pairs:
            for index in range(chips):
                px_send[number, index] = full[number, index * 2 + 1 - core].astype(BF16)
            pass_over(number, 0, chips)
        left_over(number)

    def column_slot(index):
        if not pairs:
            return index
        half, rest = index // (chips // 2), lax.rem(index, chips // 2)
        return rest // pairs * per_slice + half * pairs + lax.rem(rest, pairs)

    def grad_of_rows(number, joined, columns, store):
        part = dot(joined[...], columns[store], 0, 0)
        passed = lax.rem(store, 2) != core
        first = store // 2 * 2 * per_slice

        @pl.when(passed)
        def _():
            for index in range(2 * per_slice):
                px_send[number, first + index] = part[index * height : (index + 1) * height, :].astype(BF16)
            pass_over(number, first, 2 * per_slice)

        @pl.when(jnp.logical_not(passed))
        def _():
            for index in range(2 * per_slice):
                full[number, index * stores + store] = part[index * height : (index + 1) * height, :]

    def row_slot(index):
        return lax.rem(index, stores // 2) * 2 * per_slice + index // (stores // 2)

    side = rr.shape[2]
    place_x, place_y = chip // side, lax.rem(chip, side)
    spots = (place_x, place_y)

    def partner(way, index):
        target = lax.rem(spots[way] + index, side)
        column = (target, place_y) if way == 0 else (place_x, target)
        return target, (column[0] * side + column[1]) * 2 + core

    def share_first(number, slot_of):
        await_bytes(px_recv.at[number], px_rsem.at[number])

        def body(index, carry):
            total = full[number, index * 2 + core] + px_recv[number, slot_of(index)].astype(F32)
            first, second = index // side, lax.rem(index, side)
            blk[number, 0, first, second] = total[: height // 2].astype(BF16)
            blk[number, 1, second, first] = total[height // 2 :].astype(BF16)
            return carry

        lax.fori_loop(0, chips, body, 0)
        for way in range(2):
            for index in range(1, side):
                target, trainer = partner(way, index)
                remote(
                    blk.at[number, way, target], rr.at[number, way, index],
                    rr_ssem.at[number, way, index], rr_rsem.at[number, way, index], z, trainer,
                ).start()
                pending.append(
                    lambda way=way, index=index, target=target: await_bytes(
                        blk.at[number, way, target], rr_ssem.at[number, way, index]
                    )
                )

    def share_second(number):
        for way in range(2):
            total = blk[number, way, spots[way]].astype(F32)
            for index in range(1, side):
                await_bytes(rr.at[number, way, index], rr_rsem.at[number, way, index])
                total = total + rr[number, way, index].astype(F32)
            line[number, way] = total
            thin[number, way] = total.astype(BF16)
            for index in range(1, side):
                target, trainer = partner(1 - way, index)
                remote(
                    thin.at[number, way, target], last.at[number, way, index],
                    ls_ssem.at[number, way, index], ls_rsem.at[number, way, index], z, trainer,
                ).start()
                pending.append(
                    lambda way=way, index=index, target=target: await_bytes(
                        thin.at[number, way, target], ls_ssem.at[number, way, index]
                    )
                )

    def summed(number):
        halves = []
        for way in range(2):
            total = line[number, way, spots[1 - way]]
            for index in range(1, side):
                await_bytes(last.at[number, way, index], ls_rsem.at[number, way, index])
                total = total + last[number, way, index].astype(F32)
            halves.append(total)
        return jnp.concatenate(halves, axis=0)

    block, to_store = t // stores, lax.rem(t, stores)
    to_trainer = jnp.where(
        block < per_slice, z * per_slice + block, groups // 2 + z * per_slice + block - per_slice
    )
    moves = jnp.logical_or(to_store != z, to_trainer != t)

    def move(number):
        move_send[number] = summed(number).astype(BF16)
        sems = mv_ssem.at[number], mv_rsem.at[number]

        @pl.when(moves)
        def _():
            remote(move_send.at[number], move_recv.at[number], *sems, to_store, to_trainer).start()

        @pl.when(jnp.logical_not(moves))
        def _():
            pltpu.make_async_copy(move_send.at[number], move_recv.at[number], mv_rsem.at[number]).start()

        def leave():
            @pl.when(moves)
            def _():
                await_bytes(move_send.at[number], mv_ssem.at[number])

        pending.append(leave)

    def take_move(number, out):
        await_bytes(move_recv.at[number], mv_rsem.at[number])
        out[...] = move_recv[number].astype(F32)

    for turn in range(stores):
        grad_of_rows(1, j_three, cots, lax.rem(core + 1 + turn * 2 + turn // 2, stores))
    left_over(1)

    def spread_part(here, source):
        return dot(dpres[source, here, :], rows_of(0, source), 1, 1)

    def near_two_spread(index):
        here = rows_at(index, rows_two)
        spread_two[here, :] = spread_part(here, z) + spread_part(here, left) + spread_part(here, right)

    def far_two_spread(index):
        here = rows_at(index, rows_two)
        spread_two[here, :] += spread_part(here, across)

    def meanwhile():
        share_first(1, row_slot)
        for store in (left, right, z):
            grad_of_rows(0, j_two, dpres, store)

    take_gather(ring_two, chunks_two, agd_send, agd_recv, near_two_spread, far_two_spread, meanwhile)
    grad_of_rows(0, j_two, dpres, across)
    left_over(0)
    below2 = spread_below(spread_two[...], near_two, tile_two)
    dpre_one[...] = (below2 * slope(pre_one[...])).astype(BF16)
    early = list(pending)
    pending.clear()
    share_first(0, row_slot)
    grad_of_columns(2, j_one, dpre_one)
    share_second(1)
    send_partials(j_three, 1, part_three, got_three, 1)
    share_first(2, column_slot)
    share_second(0)
    move(1)
    move(0)
    for leave in early:
        leave()
    share_second(2)
    emb_out[...] = take_partials(j_three, 1, got_three, 0, seeds, 3).astype(BF16)
    take_move(1, three_out)
    one_out[...] = summed(2)
    take_move(0, two_out)

    for leave in pending:
        leave()


def copies(*refs):
    half = len(refs) // 2
    for source, target in zip(refs[:half], refs[half:]):
        target[...] = source[...]


def run(
    stores, groups, features, sent_ids, block_sizes, self_ids, near_one, degree_one, near_two, degree_two,
    near_three, degree_three, weight_one, weight_two, weight_three, cotangent,
):
    slots = sent_ids.shape[2]
    outer, mid, seeds = near_one.shape[0], near_two.shape[0], near_three.shape[0]
    fan = near_one.shape[1]
    fwidth = features.shape[1]
    width = cotangent.shape[1]
    devices = stores * groups
    cells = devices * slots
    height = 2 * fwidth // groups

    vmem = pl.BlockSpec(memory_space=pltpu.VMEM)
    hbm = pl.BlockSpec(memory_space=pl.ANY)
    lanes = min(128, width)
    chunks_two = 4
    dma = pltpu.SemaphoreType.DMA
    chips = groups // 2
    side = math.isqrt(chips)
    scratch = [pltpu.VMEM((rows, SLOT), jnp.int32) for rows in (outer, mid, seeds, groups * SLOT)]
    scratch += [
        pltpu.VMEM((groups * SLOT, lanes), F32),
        pltpu.VMEM(features.shape, BF16),
        pltpu.VMEM((groups * SLOT, features.shape[0]), BF16),
        pltpu.VMEM((stores, groups * SLOT, width), BF16),
        pltpu.VMEM((stores, groups * SLOT, width), BF16),
        pltpu.VMEM((groups * slots, groups * SLOT), BF16),
        pltpu.VMEM((stores, cells, width), BF16),
        pltpu.VMEM((stores, groups, lanes), BF16),
        pltpu.VMEM((cells, lanes), BF16),
        pltpu.VMEM((outer, lanes), F32),
        pltpu.VMEM((stores, 2, outer, width), F32),
        pltpu.VMEM((outer, cells), BF16),
        pltpu.VMEM((outer, cells), BF16),
        pltpu.VMEM((mid, outer), BF16),
        pltpu.VMEM((seeds, mid), BF16),
        pltpu.VMEM((stores, 2 * width, width), BF16),
        pltpu.VMEM((2, 2, chips, stores, width // chips, width), BF16),
        pltpu.VMEM((stores, outer, 2 * width), BF16),
        pltpu.VMEM((mid, 2 * width), BF16),
        pltpu.VMEM((seeds, 2 * width), BF16),
        pltpu.VMEM((outer, width), F32),
        pltpu.VMEM((mid, width), F32),
        pltpu.VMEM((outer, width), BF16),
        pltpu.VMEM((mid, width), BF16),
        pltpu.VMEM((stores, seeds, width), BF16),
        pltpu.VMEM((stores, mid, width), BF16),
        pltpu.VMEM((mid, 2 * width), F32),
        pltpu.VMEM((mid, width), F32),
        pltpu.VMEM((outer, width), BF16),
    ]
    scratch += [pltpu.VMEM((3, mid, width), BF16)] * 2 + [pltpu.VMEM((3, seeds, width), BF16)] * 2
    scratch += [pltpu.VMEM((3, groups, height, width), F32)]
    scratch += [pltpu.VMEM((3, chips, height, width), BF16)] * 2
    scratch += [pltpu.VMEM((3, 2, side, side, height // 2, width), BF16)] * 2
    scratch += [pltpu.VMEM((3, 2, side, height // 2, width), kind) for kind in (F32, BF16, BF16)]
    scratch += [pltpu.VMEM((2, height, width), BF16)] * 2
    scratch += [dma((4 + 2 * stores,)), dma((stores,)), dma((stores,)), dma((3,)), dma((3,))]
    scratch += [dma((3, chunks)) for chunks in (stores, stores, chunks_two, chunks_two)]
    scratch += [dma((3,))] * 2 + [dma((2, 3))] * 2 + [dma((2,))] * 4 + [dma((2, chunks_two, 3))] * 2
    scratch += [dma((3,))] * 2 + [dma((3, 2, side))] * 4 + [dma((2,))] * 2
    shapes = (
        jax.ShapeDtypeStruct((seeds, width), BF16),
        jax.ShapeDtypeStruct((height, width), F32),
        jax.ShapeDtypeStruct((height, width), F32),
        jax.ShapeDtypeStruct((height, width), F32),
    )
    results = pl.pallas_call(
        functools.partial(kernel, stores, groups, slots),
        out_shape=shapes,
        in_specs=[vmem] * 10 + [hbm] * 4,
        out_specs=(vmem,) * 4,
        scratch_shapes=scratch,
        compiler_params=pltpu.CompilerParams(
            collective_id=0, has_side_effects=True, vmem_limit_bytes=60 * 1024 * 1024
        ),
    )(
        jnp.transpose(sent_ids, (2, 0, 1)), block_sizes, self_ids,
        near_one.T, degree_one, near_two.T, degree_two, near_three.T, degree_three,
        cotangent, features, weight_one, weight_two, weight_three,
    )
    return pl.pallas_call(copies, out_shape=shapes, in_specs=[vmem] * 4, out_specs=(vmem,) * 4)(*results)


def solution(mesh):
    stores, groups = mesh.shape["store"], mesh.shape["trainer"]
    both = ("store", "trainer")
    placed = (
        P(both, None), P(both, None, None), P(both, None), P("trainer"), P("trainer", None), P("trainer"),
        P("trainer", None), P("trainer"), P("trainer", None), P("trainer"),
        P(None, "store"), P(None, "store"), P(None, "store"), P("trainer", "store"),
    )
    return jax.shard_map(
        functools.partial(run, stores, groups),
        mesh=mesh, in_specs=placed, out_specs=(P("trainer", "store"),) * 4, check_vma=False,
    )
```
